128 devices in a mesh: pert: 4 (over x), band: 8 (over y_hi, z), slab: 4 (over y_lo, core).
Axes of the slice: x: 4, y: 4 (y_hi: 2, y_lo: 2; y = y_hi * 2 + y_lo), z: 4, core: 2. Of those that a mesh axis runs over, the one named last changes fastest.
Arguments:
- wave_coeffs: bfloat16 [64, 55296], P('band', 'slab'), may hold values from -0.02734375 to 0.02734375
- band_energies: float32 [64], P('band'), may hold values from -2 to -0.5
- trial_potentials: float32 [4, 96, 9216], P('pert', 'slab'), may hold values from -1 to 1
- wave_map: int32 [55296], P('slab'), may hold values from 0 to 221183, as said below
Outputs:
- residual_field: float32 [4, 96, 9216], P('pert', 'slab', 'band')
- projected: float32 [4, 4], P(None, 'pert')
The draws below stay inside these ranges and needn't reach their ends.
Inputs may be any that keep to these rules, and one draw needn't show every extreme that they name: `wave_map`: within each of the 4 blocks of 13824 entries the positions are distinct and increasing, and every block holds 0 and the block's largest position.
All inputs are finite; a program needn't handle non-finite values.
Results may differ from the reference program's by a relative error of at most 0.025.
Values may be sent and summed in bfloat16 or wider, within the bound.
A program may use at most 192 MiB of HBM per device.

```python
import jax
import jax.numpy as jnp
from jax import lax

N1 = 96
N2 = 96
N3 = 96
NB = 64
NPERT = 4
NPW = 55296
N_SLAB = 4


def draw_wave_map(key, part):
    key = jax.random.fold_in(key, 7)
    local = N1 * N2 * N3 // N_SLAB
    keep = local // 16

    def one_block(sub):
        order = jax.random.permutation(sub, local - 2) + 1
        chosen = jnp.concatenate([jnp.zeros((1,), jnp.int32), order[:keep - 2].astype(jnp.int32), jnp.full((1,), local - 1, jnp.int32)])
        return jnp.sort(chosen)
    return jax.vmap(one_block)(jax.random.split(key, N_SLAB)).reshape(-1)


def level_of(stream_key, extent, pieces, least, top_value):
    loudness, own = 1.0, jax.random.fold_in(stream_key, 6)
    for dim, parts in pieces:
        heights = jnp.exp(jax.random.uniform(jax.random.fold_in(own, dim), (parts,), jnp.float32, least / len(pieces), top_value / len(pieces)))
        loudness = loudness * jnp.repeat(heights, extent[dim] // parts).reshape([-1 if axis == dim else 1 for axis in range(len(extent))])
    return loudness


def centred(key, shape, width, limit, shards=(), kind=jnp.bfloat16):
    drawn = width * jax.random.normal(key, shape, jnp.float32)
    if shards:
        drawn = drawn * level_of(key, shape, shards, -0.22, 0.18)
    return jnp.clip(drawn, -limit, limit).astype(kind)


def setup_inputs(seed: int = 0) -> dict:
    key_list = jax.random.split(jax.random.key(seed), 5)
    return {
        "wave_coeffs": centred(key_list[0], (NB, NPW), NPW ** -0.5, 0.02734375, ((0, 8), (1, 4))),
        "band_energies": jnp.clip(-2.0 + 1.5 * jax.random.uniform(key_list[1], (NB,), jnp.float32) ** level_of(key_list[1], (NB,), ((0, 8),), -0.2, 0.2), -2.0, -0.5),
        "trial_potentials": jnp.clip(jax.random.uniform(key_list[2], (NPERT, N1, N2 * N3), jnp.float32, -1.0, 1.0) * level_of(key_list[2], (NPERT, N1, N2 * N3), ((0, 4), (1, 4)), -0.4, 0.0), -1.0, 1.0),
        "wave_map": draw_wave_map(jax.random.fold_in(key_list[4], 71), 0),
    }


def cosines(n):
    rows = jnp.arange(n, dtype=jnp.int32).astype(jnp.float32)[:, None]
    cols = jnp.arange(n, dtype=jnp.int32).astype(jnp.float32)[None, :]
    table = jnp.sqrt(2.0 / n) * jnp.cos(jnp.pi * rows * (cols + 0.5) / n)
    table = table * jnp.where(rows == 0, jnp.sqrt(0.5), 1.0)
    return table.astype(jnp.bfloat16).astype(jnp.float32)

def along(table, field, axis):
    moved = jnp.moveaxis(field.astype(jnp.float32), axis, -1)
    out = jnp.einsum('...k,jk->...j', moved, table, precision=lax.Precision.HIGHEST)
    return jnp.moveaxis(out, -1, axis).astype(jnp.bfloat16)

def reference(wave_coeffs, band_energies, trial_potentials, wave_map):
    nbands = wave_coeffs.shape[0]
    npert = trial_potentials.shape[0]
    stick = N2 * N3 // N_SLAB
    per_block = wave_map.shape[0] // N_SLAB
    block = (jnp.arange(wave_map.shape[0], dtype=jnp.int32) // per_block).astype(jnp.int32)
    wmap = wave_map.astype(jnp.int32)
    xpos = (wmap // stick).astype(jnp.int32)
    jpos = (block * stick + wmap % stick).astype(jnp.int32)
    flat = (xpos * (N2 * N3) + jpos).astype(jnp.int32)
    ypos = (jpos // N3).astype(jnp.int32)
    zpos = (jpos % N3).astype(jnp.int32)
    kin = 2.0 * (xpos.astype(jnp.float32) ** 2 / (N1 * N1) + ypos.astype(jnp.float32) ** 2 / (N2 * N2) + zpos.astype(jnp.float32) ** 2 / (N3 * N3))
    tab_x, tab_y, tab_z = (cosines(N1), cosines(N2), cosines(N3))
    cells = N1 * N2 * N3

    def to_real(coeffs):
        count = coeffs.shape[0]
        cube = jnp.zeros((count, cells), jnp.bfloat16).at[:, flat].set(coeffs).reshape(count, N1, N2, N3)
        cube = along(tab_x.T, cube, 1)
        cube = along(tab_y.T, cube, 2)
        return along(tab_z.T, cube, 3)

    def to_waves(real):
        count = real.shape[0]
        cube = along(tab_z, real, 3)
        cube = along(tab_y, cube, 2)
        cube = along(tab_x, cube, 1)
        return cube.reshape(count, cells)[:, flat]
    psi_real = to_real(wave_coeffs)
    scale = 4.0 * cells / nbands

    def one_potential(potential):
        product = (potential.reshape(1, N1, N2, N3) * psi_real.astype(jnp.float32)).astype(jnp.bfloat16)
        waves = to_waves(product)
        correlation = jnp.dot(wave_coeffs.astype(jnp.float32), waves.T.astype(jnp.float32), preferred_element_type=jnp.float32).astype(jnp.bfloat16)
        rhs = (waves.astype(jnp.float32) - jnp.dot(correlation.T.astype(jnp.float32), wave_coeffs.astype(jnp.float32), preferred_element_type=jnp.float32)).astype(jnp.bfloat16)
        squares = rhs.astype(jnp.float32) ** 2
        numer = lax.optimization_barrier(jnp.sum(squares, axis=1))
        denom = lax.optimization_barrier(jnp.sum((kin[None, :] - band_energies[:, None]) * squares, axis=1))
        step = -numer / denom
        field = to_real(rhs)
        terms = step[:, None, None, None] * psi_real.astype(jnp.float32) * field.astype(jnp.float32)
        return scale * lax.optimization_barrier(jnp.sum(terms, axis=0))
    density = lax.map(one_potential, trial_potentials).reshape(npert, cells)
    basis = trial_potentials.reshape(npert, cells)
    gram = jnp.dot(basis, basis.T, precision=lax.Precision.HIGHEST) / cells
    projected = jnp.dot(basis, density.T, precision=lax.Precision.HIGHEST) / cells
    factor = jnp.linalg.cholesky(gram)
    coeffs = jax.scipy.linalg.cho_solve((factor, True), projected)
    residual_field = density - jnp.dot(coeffs.T, basis, precision=lax.Precision.HIGHEST)
    return (residual_field.reshape(npert, N1, N2 * N3), projected)
```

```python
import jax
import jax.numpy as jnp
from jax import lax
from jax.experimental import pallas as pl
from jax.experimental.pallas import tpu as pltpu
from jax.sharding import PartitionSpec as P

N1 = 96
N2 = 96
N3 = 96
LANES = 128
WIN = 384
F32 = jnp.float32
BF16 = jnp.bfloat16


def cosines(n):
    rows = jnp.arange(n, dtype=jnp.int32).astype(jnp.float32)[:, None]
    cols = jnp.arange(n, dtype=jnp.int32).astype(jnp.float32)[None, :]
    table = jnp.sqrt(2.0 / n) * jnp.cos(jnp.pi * rows * (cols + 0.5) / n)
    table = table * jnp.where(rows == 0, jnp.sqrt(0.5), 1.0)
    return table.astype(jnp.bfloat16)


def dot(a, b):
    return jnp.dot(a, b, preferred_element_type=F32)


def row_range(starts_ref, s, kx):
    first = starts_ref[s, kx]
    end = starts_ref[s, kx + 1]
    base = pl.multiple_of((first // LANES) * LANES, LANES)
    return first, end, base


def scatter_window(data_ref, s, base, first, end, ny):
    rows = data_ref[s, :, pl.ds(base, WIN)]
    place = base + lax.broadcasted_iota(jnp.int32, (1, WIN), 1)
    inside = (place >= first) & (place < end)
    ypos = jnp.where(inside, rows[2:3], -1.0)
    hot_y = (lax.broadcasted_iota(jnp.int32, (ny, WIN), 0).astype(F32) == ypos).astype(F32)
    hot_z = lax.broadcasted_iota(jnp.int32, (N3, WIN), 0).astype(F32) == rows[3:4]
    spread = jnp.concatenate(
        [jnp.where(hot_z, rows[0:1], 0.0), jnp.where(hot_z, rows[1:2], 0.0)], axis=0
    )
    return lax.dot_general(
        hot_y.astype(BF16),
        spread.astype(BF16),
        (((1,), (1,)), ((), ())),
        preferred_element_type=F32,
    )


def scatter_planes(starts_ref, data_ref, plane_ref):
    slabs = data_ref.shape[0]
    ny = N2 // slabs

    @pl.loop(0, N1)
    def _(kx):
        parts = []
        for s in range(slabs):
            first, end, base = row_range(starts_ref, s, kx)
            parts.append(scatter_window(data_ref, s, base, first, end, ny))
        plane_ref[kx] = jnp.concatenate(parts, axis=0).astype(BF16)

    @pl.when(starts_ref[0, N1 + 1] > 0)
    def _():
        @pl.loop(0, N1)
        def _(kx):
            parts = []
            for s in range(slabs):
                first, end, base = row_range(starts_ref, s, kx)

                def more(i, acc):
                    at = pl.multiple_of(base + i * WIN, LANES)
                    return acc + scatter_window(data_ref, s, at, first, end, ny)

                windows = (end - base + WIN - 1) // WIN
                parts.append(lax.fori_loop(1, windows, more, jnp.zeros((ny, 2 * N3), F32)))
            total = plane_ref[kx].astype(F32) + jnp.concatenate(parts, axis=0)
            plane_ref[kx] = total.astype(BF16)


def inverse_zy(plane_ref, turned_ref, inv_y, inv_z):
    @pl.loop(0, N1)
    def _(kx):
        z_done = dot(plane_ref[kx], inv_z).astype(BF16)
        done = dot(inv_y, z_done)
        turned_ref[0, pl.ds(kx, N2, stride=N1), :] = done[:, :LANES]
        turned_ref[1, pl.ds(kx, N2, stride=N1), :] = done[:, LANES:]


def turned_rows(turned_ref, i):
    at = pl.ds(pl.multiple_of(i * N1, 8), N1)
    return jnp.concatenate([turned_ref[0, at, :], turned_ref[1, at, :]], axis=1).astype(BF16)


def psi_kernel(starts_ref, data_ref, inv_x_ref, inv_y_ref, inv_z_ref, psi_ref, plane_ref, turned_ref):
    scatter_planes(starts_ref, data_ref, plane_ref)
    inverse_zy(plane_ref, turned_ref, inv_y_ref[...], inv_z_ref[...])

    @pl.loop(0, N2)
    def _(y):
        psi_ref[y] = dot(inv_x_ref[...], turned_rows(turned_ref, y)).astype(BF16)


def field_kernel(
    starts_ref, step_ref, data_ref, psi_ref, inv_x_ref, inv_y_ref, inv_z_ref, out_ref, plane_ref, turned_ref
):
    scatter_planes(starts_ref, data_ref, plane_ref)
    inverse_zy(plane_ref, turned_ref, inv_y_ref[...], inv_z_ref[...])

    @pl.loop(0, N2)
    def _(y):
        field = dot(inv_x_ref[...], turned_rows(turned_ref, y)).astype(BF16).astype(F32)
        terms = psi_ref[y].astype(F32) * field
        density = step_ref[0] * terms[:, :LANES] + step_ref[1] * terms[:, LANES:]
        out_ref[y] = density.astype(out_ref.dtype)


def gather_window(data_ref, wave_ref, out_ref, s, kx, base, first, end, ny):
    at = pl.ds(base, WIN)
    rows = data_ref[s, :, at]
    place = base + lax.broadcasted_iota(jnp.int32, (1, WIN), 1)
    inside = (place >= first) & (place < end)
    hot_z = (lax.broadcasted_iota(jnp.int32, (LANES, WIN), 0).astype(F32) == rows[3:4]).astype(F32)
    hot_y = lax.broadcasted_iota(jnp.int32, (ny, WIN), 0).astype(F32) == rows[2:3]
    mine = wave_ref[kx, s * ny : (s + 1) * ny, :]
    both = jnp.concatenate([mine[:, :LANES], mine[:, LANES:]], axis=0).astype(BF16)
    picked = dot(both, hot_z.astype(BF16))
    one = jnp.sum(jnp.where(hot_y, picked[:ny], 0.0), axis=0, keepdims=True)
    two = jnp.sum(jnp.where(hot_y, picked[ny:], 0.0), axis=0, keepdims=True)
    found = jnp.concatenate([one, two], axis=0)
    out_ref[s, 0:2, at] = jnp.where(inside, found, out_ref[s, 0:2, at])


def waves_kernel(
    starts_ref, data_ref, psi_ref, pot_ref, fwd_x_ref, fwd_y_ref, fwd_z_ref, out_ref, turned_ref, wave_ref
):
    slabs = data_ref.shape[0]
    ny = N2 // slabs
    out_ref[...] = jnp.zeros_like(out_ref)

    @pl.loop(0, N2)
    def _(y):
        pot = jnp.concatenate([pot_ref[s, y].astype(F32) for s in range(slabs)], axis=0)
        pot = jnp.concatenate([pot, pot], axis=1)
        product = (pot * psi_ref[y].astype(F32)).astype(BF16)
        done = dot(fwd_x_ref[...], product)
        turned_ref[0, pl.ds(y, N1, stride=N2), :] = done[:, :LANES]
        turned_ref[1, pl.ds(y, N1, stride=N2), :] = done[:, LANES:]

    @pl.loop(0, N1)
    def _(kx):
        y_done = dot(fwd_y_ref[...], turned_rows(turned_ref, kx)).astype(BF16)
        wave_ref[kx] = dot(y_done, fwd_z_ref[...])

    @pl.loop(0, N1)
    def _(kx):
        for s in range(slabs):
            first, end, base = row_range(starts_ref, s, kx)
            gather_window(data_ref, wave_ref, out_ref, s, kx, base, first, end, ny)

    @pl.when(starts_ref[0, N1 + 1] > 0)
    def _():
        @pl.loop(0, N1)
        def _(kx):
            for s in range(slabs):
                first, end, base = row_range(starts_ref, s, kx)

                @pl.loop(1, (end - base + WIN - 1) // WIN)
                def _(i):
                    at = pl.multiple_of(base + i * WIN, LANES)
                    gather_window(data_ref, wave_ref, out_ref, s, kx, at, first, end, ny)


SMEM = pl.BlockSpec(memory_space=pltpu.SMEM)
VMEM = pl.BlockSpec(memory_space=pltpu.VMEM)
PARAMS = dict(vmem_limit_bytes=56 * 1024 * 1024)


def cost(flops, moved):
    return pl.CostEstimate(flops=int(flops), bytes_accessed=int(moved), transcendentals=0)


def plane_scratch():
    return [pltpu.VMEM((N1, N2, 2 * N3), BF16), pltpu.VMEM((2, N1 * N2, LANES), F32)]


def psi_of(starts, data, inv_x, inv_y, inv_z):
    return pl.pallas_call(
        psi_kernel,
        out_shape=jax.ShapeDtypeStruct((N2, N1, 2 * LANES), BF16),
        in_specs=[SMEM] + [VMEM] * 4,
        out_specs=VMEM,
        scratch_shapes=plane_scratch(),
        compiler_params=pltpu.CompilerParams(**PARAMS),
        cost_estimate=cost(2e10, 8e6),
        name="psi",
    )(starts, data, inv_x, inv_y, inv_z)


def waves_of(starts, data, psi, pot, fwd_x, fwd_y, fwd_z):
    return pl.pallas_call(
        waves_kernel,
        out_shape=jax.ShapeDtypeStruct(data.shape[:1] + (2,) + data.shape[2:], F32),
        in_specs=[SMEM] + [VMEM] * 6,
        out_specs=VMEM,
        scratch_shapes=[pltpu.VMEM((2, N1 * N2, LANES), F32), pltpu.VMEM((N1, N2, 2 * LANES), F32)],
        compiler_params=pltpu.CompilerParams(**PARAMS),
        cost_estimate=cost(2e10, 8e6),
        name="waves",
    )(starts, data, psi, pot, fwd_x, fwd_y, fwd_z)


def density_of(starts, step, data, psi, inv_x, inv_y, inv_z):
    return pl.pallas_call(
        field_kernel,
        out_shape=jax.ShapeDtypeStruct((N2, N1, LANES), BF16),
        in_specs=[SMEM, SMEM] + [VMEM] * 5,
        out_specs=VMEM,
        scratch_shapes=plane_scratch(),
        compiler_params=pltpu.CompilerParams(**PARAMS),
        cost_estimate=cost(2e10, 8e6),
        name="field",
    )(starts, step, data, psi, inv_x, inv_y, inv_z)


def tables():
    tab_x, tab_y, tab_z = (cosines(N1), cosines(N2), cosines(N3))
    pad = LANES - N3
    wide = jnp.pad(tab_z, ((0, 0), (0, pad)))
    none = jnp.zeros_like(wide)
    inv_z = jnp.block([[wide, none], [none, wide]])
    square = jnp.pad(tab_z.T, ((0, pad), (0, pad)))
    empty = jnp.zeros_like(square)
    fwd_z = jnp.block([[square, empty], [empty, square]])
    return tab_x, tab_y, inv_z, fwd_z


def row_starts(wave_map, stick):
    edges = jnp.arange(N1 + 1, dtype=jnp.int32) * stick
    return jnp.sum((wave_map[None, :] < edges[:, None]).astype(jnp.int32), axis=1)


def with_flag(starts):
    base = starts[:, :-1] // LANES * LANES
    over = jnp.any(starts[:, 1:] > base + WIN).astype(jnp.int32)
    return jnp.concatenate([starts, jnp.full((starts.shape[0], 1), over)], axis=1)


def packed(two, ypos, zpos):
    count = two.shape[2]
    rows = jnp.concatenate(
        [two.astype(F32), ypos[:, None].astype(F32), zpos[:, None].astype(F32)], axis=1
    )
    return jnp.pad(rows, ((0, 0), (0, 4), (0, WIN)))


def per_device(wave_coeffs, band_energies, trial_potentials, wave_map):
    slabs = lax.axis_size("slab")
    me = lax.axis_index("slab")
    bands, npw = wave_coeffs.shape
    planes, cross = trial_potentials.shape[1:]
    stick = N2 * N3 // slabs
    ny = N2 // slabs
    tab_x, tab_y, inv_z, fwd_z = tables()

    starts = row_starts(wave_map, stick)
    both = lax.all_gather(jnp.concatenate([wave_map, starts]), "slab", axis=0)
    maps = both[:, :npw]
    starts = with_flag(both[:, npw:])
    xpos = maps // stick
    ypos = maps % stick // N3
    zpos = maps % N3
    mine = lax.all_to_all(
        wave_coeffs.reshape(slabs, bands // slabs, npw), "slab", split_axis=0, concat_axis=0
    )
    all_bands = lax.all_gather(wave_coeffs, "band", axis=0, tiled=True)
    local_pot = trial_potentials.reshape(planes, N2, N3)
    pot = jnp.pad(local_pot.astype(BF16).swapaxes(0, 1), ((0, 0), (0, 0), (0, LANES - N3)))
    pot = lax.all_gather(pot, "slab", axis=0)

    psi = psi_of(starts, packed(mine, ypos, zpos), tab_x.T, tab_y.T, inv_z)
    waves = waves_of(starts, packed(mine, ypos, zpos), psi, pot, tab_x, tab_y, fwd_z)
    waves = waves[:, :, :npw].astype(BF16)
    waves = lax.all_to_all(waves, "slab", split_axis=0, concat_axis=0).reshape(bands, npw)
    correlation = lax.dot_general(
        all_bands, waves, (((1,), (1,)), ((), ())), preferred_element_type=F32
    )
    correlation = lax.psum(correlation, "slab").astype(BF16)
    removed = lax.dot_general(
        correlation, all_bands, (((0,), (0,)), ((), ())), preferred_element_type=F32
    )
    rhs = (waves.astype(F32) - removed).astype(BF16)
    rhs = lax.all_to_all(
        rhs.reshape(slabs, bands // slabs, npw), "slab", split_axis=0, concat_axis=0
    )
    yall = ypos + ny * jnp.arange(slabs, dtype=jnp.int32)[:, None]
    kin = 2.0 * (
        xpos.astype(F32) ** 2 / (N1 * N1)
        + yall.astype(F32) ** 2 / (N2 * N2)
        + zpos.astype(F32) ** 2 / (N3 * N3)
    )
    energies = lax.dynamic_slice_in_dim(band_energies, me * (bands // slabs), bands // slabs, 0)
    squares = rhs.astype(F32) ** 2
    numer = jnp.sum(squares, axis=(0, 2))
    denom = jnp.sum((kin[:, None, :] - energies[None, :, None]) * squares, axis=(0, 2))
    step = -numer / denom
    scale = 4.0 * N1 * N2 * N3 / all_bands.shape[0]
    density = density_of(
        starts, scale * step, packed(rhs, ypos, zpos), psi, tab_x.T, tab_y.T, inv_z
    )
    width = cross // lax.axis_size("band")
    density = density[:, :, :N3]
    density = lax.psum_scatter(density, "band", scatter_dimension=0, tiled=True)
    density = lax.psum_scatter(density, "slab", scatter_dimension=1, tiled=True)
    density = density.astype(F32).swapaxes(0, 1).reshape(1, planes, width)
    offset = lax.axis_index("band") * width
    share = lax.dynamic_slice_in_dim(trial_potentials, offset, width, 2)
    potentials = lax.all_gather(share, "pert", axis=0, tiled=True)
    cells = N1 * N2 * N3
    flat_pot = potentials.reshape(potentials.shape[0], -1)
    flat_den = density.reshape(density.shape[0], -1)
    gram = jnp.dot(flat_pot, flat_pot.T, precision=lax.Precision.HIGHEST)
    projected = jnp.dot(flat_pot, flat_den.T, precision=lax.Precision.HIGHEST)
    gram, projected = lax.psum((gram, projected), ("band", "slab"))
    gram = gram / cells
    projected = projected / cells
    factor = jnp.linalg.cholesky(gram)
    coeffs = jax.scipy.linalg.cho_solve((factor, True), projected)
    residual_field = density - jnp.einsum(
        "pq,pxc->qxc", coeffs, potentials, precision=lax.Precision.HIGHEST
    )
    return (residual_field, projected)


def solution(mesh):
    return jax.shard_map(
        per_device,
        mesh=mesh,
        in_specs=(P("band", "slab"), P("band"), P("pert", "slab", None), P("slab")),
        out_specs=(P("pert", "slab", "band"), P(None, "pert")),
        check_vma=False,
    )
```

```python
import jax
import jax.numpy as jnp
from jax import lax
from jax.experimental import pallas as pl
from jax.experimental.pallas import tpu as pltpu
from jax.sharding import PartitionSpec as P

N1 = 96
N2 = 96
N3 = 96
LANES = 128
WIN = 512
TILE = 2
F32 = jnp.float32
BF16 = jnp.bfloat16
NT = (((1,), (1,)), ((), ()))
MESH = pl.DeviceIdType.MESH


def cosines(n):
    rows = jnp.arange(n, dtype=jnp.int32).astype(jnp.float32)[:, None]
    cols = jnp.arange(n, dtype=jnp.int32).astype(jnp.float32)[None, :]
    table = jnp.sqrt(2.0 / n) * jnp.cos(jnp.pi * rows * (cols + 0.5) / n)
    table = table * jnp.where(rows == 0, jnp.sqrt(0.5), 1.0)
    return table.astype(jnp.bfloat16)


def dot(a, b):
    return jnp.dot(a, b, preferred_element_type=F32)


def window_base(starts_ref, s, tile):
    return pl.multiple_of((starts_ref[s, tile] // LANES) * LANES, LANES)


def hot_rows(rows, tile, cells):
    at = rows[2:3] - (tile * cells).astype(F32)
    return lax.broadcasted_iota(jnp.int32, (cells, WIN), 0).astype(F32) == at


def hot_z(rows):
    here = lax.broadcasted_iota(jnp.int32, (N3, WIN), 0).astype(F32) == rows[3:4]
    return here.astype(F32).astype(BF16)


def scatter_window(data_ref, s, base, tile, cells):
    rows = data_ref[s, :, pl.ds(base, WIN)]
    hot = hot_rows(rows, tile, cells)
    both = [jnp.where(hot, rows[0:1], 0.0), jnp.where(hot, rows[1:2], 0.0)]
    left = jnp.concatenate(both, axis=0).astype(BF16)
    return lax.dot_general(left, hot_z(rows), NT, preferred_element_type=F32)


def plane_of(parts, t, ny):
    cells = TILE * ny
    rows = [p[b * cells + t * ny : b * cells + (t + 1) * ny] for b in range(2) for p in parts]
    return jnp.concatenate(rows, axis=0)


def scatter_planes(starts_ref, data_ref, plane_ref):
    slabs = data_ref.shape[0]
    ny = N2 // slabs
    cells = TILE * ny
    tiles = N1 // TILE
    unroll = 4

    @pl.loop(0, tiles // unroll)
    def _(group):
        for u in range(unroll):
            tile = group * unroll + u
            parts = [
                scatter_window(data_ref, s, window_base(starts_ref, s, tile), tile, cells)
                for s in range(slabs)
            ]
            for t in range(TILE):
                plane_ref[tile * TILE + t] = plane_of(parts, t, ny).astype(BF16)

    @pl.when(starts_ref[0, tiles + 1] > 0)
    def _():
        @pl.loop(0, tiles)
        def _(tile):
            parts = []
            for s in range(slabs):
                base = window_base(starts_ref, s, tile)

                def more(i, acc):
                    at = pl.multiple_of(base + i * WIN, LANES)
                    return acc + scatter_window(data_ref, s, at, tile, cells)

                windows = (starts_ref[s, tile + 1] - base + WIN - 1) // WIN
                zero = jnp.zeros((2 * cells, N3), F32)
                parts.append(lax.fori_loop(1, windows, more, zero))
            for t in range(TILE):
                old = plane_ref[tile * TILE + t].astype(F32)
                plane_ref[tile * TILE + t] = (old + plane_of(parts, t, ny)).astype(BF16)


def inverse_zy(plane_ref, turned_ref, inv_y, inv_z):
    width = 16

    @pl.loop(0, N1 // width)
    def _(group):
        first = pl.multiple_of(group * width, width)
        flat = plane_ref[pl.ds(first, width)].reshape(width * 2 * N2, N3)
        z_done = dot(flat, inv_z).astype(BF16)
        done = []
        for u in range(width):
            one = z_done[2 * N2 * u : 2 * N2 * u + N2]
            two = z_done[2 * N2 * u + N2 : 2 * N2 * (u + 1)]
            done.append(dot(inv_y, jnp.concatenate([one, two], axis=1)).astype(BF16))
        turned_ref[:, pl.ds(first, width), :] = jnp.swapaxes(jnp.stack(done, axis=0), 0, 1)


def psi_kernel(starts_ref, data_ref, inv_x_ref, inv_y_ref, inv_z_ref, psi_ref, plane_ref, turned_ref):
    scatter_planes(starts_ref, data_ref, plane_ref)
    inverse_zy(plane_ref, turned_ref, inv_y_ref[...], inv_z_ref[...])
    unroll = 8

    @pl.loop(0, N2 // unroll)
    def _(group):
        for u in range(unroll):
            y = group * unroll + u
            psi_ref[y] = dot(inv_x_ref[...], turned_ref[y]).astype(BF16)


def field_kernel(
    starts_ref, data_ref, step_ref, psi_ref, inv_x_ref, inv_y_ref, inv_z_ref, out_ref, plane_ref, turned_ref
):
    scatter_planes(starts_ref, data_ref, plane_ref)
    inverse_zy(plane_ref, turned_ref, inv_y_ref[...], inv_z_ref[...])
    slabs, _, planes, _ = out_ref.shape
    unroll = 8

    @pl.loop(0, N2 // unroll)
    def _(group):
        for u in range(unroll):
            y = group * unroll + u
            field = dot(inv_x_ref[...], turned_ref[y]).astype(BF16).astype(F32)
            terms = psi_ref[y].astype(F32) * field
            density = step_ref[0:1] * terms[:, :LANES] + step_ref[1:2] * terms[:, LANES:]
            for s in range(slabs):
                out_ref[s, y] = density[s * planes : (s + 1) * planes].astype(out_ref.dtype)


def gather_window(data_ref, wave_ref, sum_ref, s, base, tile, ny):
    cells = TILE * ny
    at = pl.ds(base, WIN)
    rows = data_ref[s, :, at]
    hot = hot_rows(rows, tile, cells)
    both = [
        wave_ref[tile * TILE + t, b * N2 + s * ny : b * N2 + (s + 1) * ny, :]
        for b in range(2)
        for t in range(TILE)
    ]
    picked = dot(jnp.concatenate(both, axis=0).astype(BF16), hot_z(rows))
    one = jnp.sum(jnp.where(hot, picked[:cells], 0.0), axis=0, keepdims=True)
    two = jnp.sum(jnp.where(hot, picked[cells:], 0.0), axis=0, keepdims=True)
    sum_ref[s, 0:2, at] += jnp.concatenate([one, two], axis=0)


def waves_kernel(
    starts_ref, data_ref, psi_ref, pot_ref, fwd_x_ref, fwd_y_ref, fwd_z_ref, out_ref, turned_ref, wave_ref, sum_ref
):
    slabs = data_ref.shape[0]
    ny = N2 // slabs
    tiles = N1 // TILE
    sum_ref[...] = jnp.zeros_like(sum_ref)
    width = 16

    @pl.loop(0, N2 // width)
    def _(group):
        first = pl.multiple_of(group * width, width)
        done = []
        for u in range(width):
            y = first + u
            pot = jnp.concatenate([pot_ref[s, y].astype(F32) for s in range(slabs)], axis=0)
            pot = jnp.concatenate([pot, pot], axis=1)
            product = (pot * psi_ref[y].astype(F32)).astype(BF16)
            done.append(dot(fwd_x_ref[...], product).astype(BF16))
        turned_ref[:, pl.ds(first, width), :] = jnp.swapaxes(jnp.stack(done, axis=0), 0, 1)

    unroll = 8

    @pl.loop(0, N1 // unroll)
    def _(group):
        done = []
        for u in range(unroll):
            y_done = dot(fwd_y_ref[...], turned_ref[group * unroll + u]).astype(BF16)
            done += [y_done[:, :LANES], y_done[:, LANES:]]
        waves = dot(jnp.concatenate(done, axis=0), fwd_z_ref[...])
        for u in range(unroll):
            wave_ref[group * unroll + u] = waves[u * 2 * N2 : (u + 1) * 2 * N2]

    several = 4

    @pl.loop(0, tiles // several)
    def _(group):
        for u in range(several):
            tile = group * several + u
            for s in range(slabs):
                base = window_base(starts_ref, s, tile)
                gather_window(data_ref, wave_ref, sum_ref, s, base, tile, ny)

    @pl.when(starts_ref[0, tiles + 1] > 0)
    def _():
        @pl.loop(0, tiles)
        def _(tile):
            for s in range(slabs):
                base = window_base(starts_ref, s, tile)

                @pl.loop(1, (starts_ref[s, tile + 1] - base + WIN - 1) // WIN)
                def _(i):
                    at = pl.multiple_of(base + i * WIN, LANES)
                    gather_window(data_ref, wave_ref, sum_ref, s, at, tile, ny)

    out_ref[...] = sum_ref[:, :, : out_ref.shape[2]].astype(out_ref.dtype)


SMEM = pl.BlockSpec(memory_space=pltpu.SMEM)
VMEM = pl.BlockSpec(memory_space=pltpu.VMEM)
LIMIT = 56 * 1024 * 1024


def greet(peers):
    barrier = pltpu.get_barrier_semaphore()
    for peer in peers:
        pl.semaphore_signal(barrier, inc=1, device_id=peer, device_id_type=MESH)
    pl.semaphore_wait(barrier, len(peers))


def send(src, dst, send_sem, recv_sem, peer):
    copy = pltpu.make_async_remote_copy(
        src_ref=src, dst_ref=dst, send_sem=send_sem, recv_sem=recv_sem, device_id=peer, device_id_type=MESH
    )
    copy.start()
    return copy


def slab_peers(slabs):
    me = lax.axis_index("slab")
    return [lax.rem(me + d, slabs) for d in range(1, slabs)]


def start_kernel(coef_ref, map_ref, coefs_ref, maps_ref, send_sem, recv_sem):
    slabs = coef_ref.shape[0]
    me = lax.axis_index("slab")
    peers = slab_peers(slabs)
    greet([{"slab": peer} for peer in peers])
    copies = []
    for i, peer in enumerate(peers):
        to = {"slab": peer}
        copies.append(send(coef_ref.at[peer], coefs_ref.at[me], send_sem.at[0, i], recv_sem.at[0, i], to))
        copies.append(send(map_ref, maps_ref.at[me], send_sem.at[1, i], recv_sem.at[1, i], to))
    coefs_ref[me] = coef_ref[me]
    maps_ref[me] = map_ref[...]
    for copy in copies:
        copy.wait()


def middle_kernel(
    waves_ref, bands_ref, index_ref, energy_ref, data_ref, step_ref,
    got_ref, corr_ref, rhs_ref, back_ref, total_ref, send_sem, recv_sem,
):
    slabs, two, npw = waves_ref.shape
    chunk = 1536
    me = lax.axis_index("slab")
    peers = slab_peers(slabs)
    greet([{"slab": peer} for peer in peers])
    copies = []
    for i, peer in enumerate(peers):
        to = {"slab": peer}
        copies.append(send(waves_ref.at[peer], got_ref.at[me], send_sem.at[0, i], recv_sem.at[0, i], to))
    got_ref[me] = waves_ref[me]
    for copy in copies:
        copy.wait()

    def waves_at(at):
        return jnp.concatenate([got_ref[t, :, at].astype(F32) for t in range(slabs)], axis=0)

    total_ref[...] = jnp.zeros_like(total_ref)

    @pl.loop(0, npw // chunk)
    def _(i):
        at = pl.ds(pl.multiple_of(i * chunk, chunk), chunk)
        total_ref[...] += lax.dot_general(
            waves_at(at).astype(BF16), bands_ref[:, at], NT, preferred_element_type=F32
        )

    copies = []
    for i, peer in enumerate(peers):
        to = {"slab": peer}
        copies.append(send(total_ref, corr_ref.at[i], send_sem.at[1, i], recv_sem.at[1, i], to))
    for copy in copies:
        copy.wait()
    correlation = total_ref[...]
    for i in range(slabs - 1):
        correlation = correlation + corr_ref[i]
    correlation = correlation.astype(BF16)

    @pl.loop(0, npw // chunk)
    def _(i):
        at = pl.ds(pl.multiple_of(i * chunk, chunk), chunk)
        rhs = (waves_at(at) - dot(correlation, bands_ref[:, at])).astype(BF16)
        for t in range(slabs):
            rhs_ref[t, :, at] = rhs[two * t : two * (t + 1)]

    copies = []
    for i, peer in enumerate(peers):
        to = {"slab": peer}
        copies.append(send(rhs_ref.at[peer], back_ref.at[me], send_sem.at[2, i], recv_sem.at[2, i], to))
    back_ref[me] = rhs_ref[me]
    for copy in copies:
        copy.wait()

    data_ref[...] = index_ref[...]
    numer = jnp.zeros((two, chunk), F32)
    denom = jnp.zeros((two, chunk), F32)
    energy = jnp.concatenate([jnp.full((1, chunk), energy_ref[b], F32) for b in range(two)], axis=0)
    for s in range(slabs):
        for i in range(npw // chunk):
            at = pl.ds(i * chunk, chunk)
            mine = back_ref[s, :, at].astype(F32)
            data_ref[s, 0:2, at] = mine
            squares = mine * mine
            numer = numer + squares
            denom = denom + (index_ref[s, 4:5, at] - energy) * squares
    step = -jnp.sum(numer, axis=1, keepdims=True) / jnp.sum(denom, axis=1, keepdims=True)
    step_ref[...] = jnp.broadcast_to(step, step_ref.shape)


def reduce_kernel(
    density_ref, share_ref, out_ref, projected_ref,
    from_core, half_ref, from_y, quarter_ref, from_z, pots_ref, sums_ref, from_sums, send_sem, recv_sem,
):
    slabs, _, planes, lanes = density_ref.shape
    perts, rows = pots_ref.shape[:2]
    pert, band, slab = (lax.axis_index(name) for name in ("pert", "band", "slab"))
    y_lo, core = slab // 2, lax.rem(slab, 2)
    y_hi, z = band // 4, lax.rem(band, 4)

    def id_of(y_hi, y_lo, z):
        return {"band": y_hi * 4 + z, "slab": y_lo * 2 + core}

    sibling = {"slab": y_lo * 2 + 1 - core}
    y_steps = [(0, 1), (1, 0), (1, 1)]
    y_coords = [(lax.rem(y_hi + a, 2), lax.rem(y_lo + b, 2)) for a, b in y_steps]
    y_peers = [id_of(a, b, z) for a, b in y_coords]
    z_coords = [lax.rem(z + d, 4) for d in range(1, 4)]
    z_peers = [id_of(y_hi, y_lo, c) for c in z_coords]
    p_coords = [lax.rem(pert + d, perts) for d in range(1, perts)]
    p_peers = [{"pert": c} for c in p_coords]
    greet([sibling] + y_peers + z_peers + p_peers)

    copies = []
    for a in range(2):
        src = density_ref.at[a * 2 + 1 - core]
        copies.append(send(src, from_core.at[a], send_sem.at[0, a], recv_sem.at[0, a], sibling))
    pot_copies = []
    for i, peer in enumerate(p_peers):
        pot_copies.append(send(share_ref, pots_ref.at[pert], send_sem.at[1, i], recv_sem.at[1, i], peer))
    pots_ref[pert] = share_ref[...]
    for copy in copies:
        copy.wait()
    for a in range(2):
        @pl.loop(0, N2 // 8)
        def _(i):
            at = pl.ds(pl.multiple_of(i * 8, 8), 8)
            total = density_ref[a * 2 + core, at].astype(F32) + from_core[a, at].astype(F32)
            half_ref[a, at] = total.astype(BF16)

    quarter = N2 // 2
    copies = []
    for i, (a, b) in enumerate(y_coords):
        src = half_ref.at[b, pl.ds(a * quarter, quarter)]
        copies.append(send(src, from_y.at[i], send_sem.at[2, i], recv_sem.at[2, i], y_peers[i]))
    for copy in copies:
        copy.wait()
    mine = y_hi * quarter

    @pl.loop(0, 4)
    def _(i):
        total = half_ref[y_lo, pl.ds(mine + i * rows, rows)].astype(F32)
        for j in range(3):
            total = total + from_y[j, pl.ds(i * rows, rows)].astype(F32)
        quarter_ref[i] = total.astype(BF16)

    copies = []
    for i, c in enumerate(z_coords):
        copies.append(send(quarter_ref.at[c], from_z.at[i], send_sem.at[3, i], recv_sem.at[3, i], z_peers[i]))
    for copy in pot_copies:
        copy.wait()

    def total_of(a):
        a = jnp.sum(a, axis=0)
        a = a[0:8] + a[8:16] + a[16:24]
        return jnp.sum(a, axis=0, keepdims=True)

    pots = [pots_ref[p] for p in range(perts)]
    pairs = [(p, q) for p in range(perts) for q in range(p + 1)]
    sums = [total_of(pots[p] * pots[q]) for p, q in pairs]
    for copy in copies:
        copy.wait()
    density = quarter_ref[z].astype(F32)
    for j in range(3):
        density = density + from_z[j].astype(F32)
    sums += [total_of(pots[p] * density) for p in range(perts)]
    used = len(sums)
    sums += [jnp.zeros((1, lanes), F32)] * (16 - used)
    sums_ref[0] = jnp.concatenate(sums, axis=0)

    at = 0
    for level, group in enumerate([[sibling], y_peers, z_peers]):
        copies = []
        for i, peer in enumerate(group):
            copies.append(
                send(sums_ref.at[level], from_sums.at[at + i], send_sem.at[4 + level, i], recv_sem.at[4 + level, i], peer)
            )
        for copy in copies:
            copy.wait()
        total = sums_ref[level]
        for i in range(len(group)):
            total = total + from_sums[at + i]
        sums_ref[level + 1] = total
        at += len(group)

    cells = 1.0 / (N1 * N2 * N3)
    totals = jnp.broadcast_to(jnp.sum(sums_ref[3], axis=1, keepdims=True) * cells, (16, lanes))
    gram = {pair: totals[k : k + 1] for k, pair in enumerate(pairs)}
    rhs = [totals[len(pairs) + p : len(pairs) + p + 1] for p in range(perts)]
    factor = {}
    for p in range(perts):
        for q in range(p + 1):
            value = gram[p, q]
            for k in range(q):
                value = value - factor[p, k] * factor[q, k]
            factor[p, q] = jnp.sqrt(value) if p == q else value / factor[q, q]
    coeffs = []
    for p in range(perts):
        value = rhs[p]
        for k in range(p):
            value = value - factor[p, k] * coeffs[k]
        coeffs.append(value / factor[p, p])
    for p in reversed(range(perts)):
        value = coeffs[p]
        for k in range(p + 1, perts):
            value = value - factor[k, p] * coeffs[k]
        coeffs[p] = value / factor[p, p]
    for p in range(perts):
        density = density - coeffs[p][None] * pots[p]
    out_ref[...] = density
    projected_ref[...] = jnp.concatenate(rhs + rhs, axis=0)


def cost(flops, moved):
    return pl.CostEstimate(flops=int(flops), bytes_accessed=int(moved), transcendentals=0)


def params(remote=None):
    if remote is None:
        return pltpu.CompilerParams(vmem_limit_bytes=LIMIT)
    return pltpu.CompilerParams(vmem_limit_bytes=LIMIT, collective_id=remote, has_side_effects=True)


def shape(dims, kind):
    return jax.ShapeDtypeStruct(dims, kind)


def plane_scratch():
    return [pltpu.VMEM((N1, 2 * N2, N3), BF16), pltpu.VMEM((N2, N1, 2 * LANES), BF16)]


def start_of(coefs, wave_map):
    slabs, _, npw = coefs.shape
    return pl.pallas_call(
        start_kernel,
        out_shape=(shape(coefs.shape, BF16), shape((slabs, 1, npw), jnp.int32)),
        in_specs=[VMEM] * 2,
        out_specs=(VMEM, VMEM),
        scratch_shapes=[pltpu.SemaphoreType.DMA((2, slabs - 1))] * 2,
        compiler_params=params(1),
        name="start",
    )(coefs, wave_map.reshape(1, npw))


def psi_of(starts, data, inv_x, inv_y, inv_z):
    return pl.pallas_call(
        psi_kernel,
        out_shape=shape((N2, N1, 2 * LANES), BF16),
        in_specs=[SMEM] + [VMEM] * 4,
        out_specs=VMEM,
        scratch_shapes=plane_scratch(),
        compiler_params=params(),
        cost_estimate=cost(2e10, 8e6),
        name="psi",
    )(starts, data, inv_x, inv_y, inv_z)


def waves_of(starts, data, psi, pot, fwd_x, fwd_y, fwd_z, npw):
    slabs = data.shape[0]
    return pl.pallas_call(
        waves_kernel,
        out_shape=shape((slabs, 2, npw), BF16),
        in_specs=[SMEM] + [VMEM] * 6,
        out_specs=VMEM,
        scratch_shapes=[
            pltpu.VMEM((N1, N2, 2 * LANES), BF16),
            pltpu.VMEM((N1, 2 * N2, N3), F32),
            pltpu.VMEM((slabs, 2, data.shape[2]), F32),
        ],
        compiler_params=params(),
        cost_estimate=cost(2e10, 8e6),
        name="waves",
    )(starts, data, psi, pot, fwd_x, fwd_y, fwd_z)


def middle_of(waves, bands, index, energies):
    slabs, two, npw = waves.shape
    block = pltpu.VMEM(waves.shape, BF16)
    small = (slabs * two, bands.shape[0])
    return pl.pallas_call(
        middle_kernel,
        out_shape=(shape(index.shape, F32), shape((two, LANES), F32)),
        in_specs=[VMEM] * 3 + [SMEM],
        out_specs=(VMEM, VMEM),
        scratch_shapes=[
            block,
            pltpu.VMEM((slabs - 1,) + small, F32),
            block,
            block,
            pltpu.VMEM(small, F32),
            pltpu.SemaphoreType.DMA((3, slabs - 1)),
            pltpu.SemaphoreType.DMA((3, slabs - 1)),
        ],
        compiler_params=params(2),
        name="middle",
    )(waves, bands, index, energies)


def density_of(starts, data, step, psi, inv_x, inv_y, inv_z, slabs):
    return pl.pallas_call(
        field_kernel,
        out_shape=shape((slabs, N2, N1 // slabs, LANES), BF16),
        in_specs=[SMEM] + [VMEM] * 6,
        out_specs=VMEM,
        scratch_shapes=plane_scratch(),
        compiler_params=params(),
        cost_estimate=cost(2e10, 8e6),
        name="field",
    )(starts, data, step, psi, inv_x, inv_y, inv_z)


def reduced(density, share, perts):
    slabs, _, planes, lanes = density.shape
    rows = share.shape[0]
    block = (rows, planes, lanes)
    return pl.pallas_call(
        reduce_kernel,
        out_shape=(shape(block, F32), shape((8, lanes), F32)),
        in_specs=[VMEM] * 2,
        out_specs=(VMEM, VMEM),
        scratch_shapes=[
            pltpu.VMEM((2, N2, planes, lanes), BF16),
            pltpu.VMEM((2, N2, planes, lanes), BF16),
            pltpu.VMEM((3, N2 // 2, planes, lanes), BF16),
            pltpu.VMEM((4,) + block, BF16),
            pltpu.VMEM((3,) + block, BF16),
            pltpu.VMEM((perts,) + block, F32),
            pltpu.VMEM((4, 16, lanes), F32),
            pltpu.VMEM((7, 16, lanes), F32),
            pltpu.SemaphoreType.DMA((7, 3)),
            pltpu.SemaphoreType.DMA((7, 3)),
        ],
        compiler_params=params(3),
        name="reduce",
    )(density, share)


def tables():
    tab_x, tab_y, tab_z = (cosines(N1), cosines(N2), cosines(N3))
    inv_z = jnp.pad(tab_z, ((0, 0), (0, LANES - N3)))
    return tab_x, tab_y, inv_z


def tile_starts(maps, stick):
    edges = jnp.arange(N1 // TILE + 1, dtype=jnp.int32) * (TILE * stick)
    starts = jnp.sum((maps[:, None, :] < edges[None, :, None]).astype(jnp.int32), axis=2)
    over = jnp.any(starts[:, 1:] > starts[:, :-1] // LANES * LANES + WIN).astype(jnp.int32)
    return jnp.concatenate([starts, jnp.full((starts.shape[0], 1), over)], axis=1)


def index_rows(maps, ny):
    slabs, npw = maps.shape
    xpos = maps // (ny * N3)
    ypos = maps // N3 % ny + ny * jnp.arange(slabs, dtype=jnp.int32)[:, None]
    zpos = maps % N3
    kin = 2.0 * (
        xpos.astype(F32) ** 2 / (N1 * N1)
        + ypos.astype(F32) ** 2 / (N2 * N2)
        + zpos.astype(F32) ** 2 / (N3 * N3)
    )
    rows = jnp.stack([(maps // N3).astype(F32), zpos.astype(F32), kin], axis=1)
    return jnp.pad(rows, ((0, 0), (2, 3), (0, 2 * WIN)), constant_values=-1.0)


def per_device(wave_coeffs, band_energies, trial_potentials, wave_map):
    slabs = lax.axis_size("slab")
    me = lax.axis_index("slab")
    bands, npw = wave_coeffs.shape
    planes, cross = trial_potentials.shape[1:]
    ny = N2 // slabs
    tab_x, tab_y, inv_z = tables()

    coefs, maps = start_of(wave_coeffs.reshape(slabs, bands // slabs, npw), wave_map)
    maps = maps.reshape(slabs, npw)
    all_bands = lax.all_gather(wave_coeffs, "band", axis=0, tiled=True)
    turned = trial_potentials.reshape(planes, N2, N3).swapaxes(0, 1)
    turned = jnp.pad(turned, ((0, 0), (0, 0), (0, LANES - N3)))
    pot = lax.all_gather(turned.astype(BF16), "slab", axis=0)
    rows = N2 // lax.axis_size("band")
    share = lax.dynamic_slice_in_dim(turned, lax.axis_index("band") * rows, rows, 0)

    starts = tile_starts(maps, ny * N3)
    index = index_rows(maps, ny)
    data = lax.dynamic_update_slice(index, coefs.astype(F32), (0, 0, 0))
    psi = psi_of(starts, data, tab_x.T, tab_y.T, inv_z)
    waves = waves_of(starts, data, psi, pot, tab_x, tab_y, inv_z.T, npw)
    energies = lax.dynamic_slice_in_dim(band_energies, me * (bands // slabs), bands // slabs, 0)
    data, step = middle_of(waves, all_bands, index, energies)
    step = step * (4.0 * N1 * N2 * N3 / all_bands.shape[0])
    density = density_of(starts, data, step, psi, tab_x.T, tab_y.T, inv_z, slabs)
    residual, projected = reduced(density, share, lax.axis_size("pert"))
    residual = residual[:, :, :N3].swapaxes(0, 1).reshape(1, planes, rows * N3)
    return (residual, projected[: lax.axis_size("pert"), :1])


def solution(mesh):
    return jax.shard_map(
        per_device,
        mesh=mesh,
        in_specs=(P("band", "slab"), P("band"), P("pert", "slab", None), P("slab")),
        out_specs=(P("pert", "slab", "band"), P(None, "pert")),
        check_vma=False,
    )
```

```python
import jax
import jax.numpy as jnp
from jax import lax
from jax.experimental import pallas as pl
from jax.experimental.pallas import tpu as pltpu
from jax.sharding import PartitionSpec as P

N1 = 96
N2 = 96
N3 = 96
LANES = 128
WIN = 512
TILE = 2
TILES = N1 // TILE
F32 = jnp.float32
BF16 = jnp.bfloat16
NT = (((1,), (1,)), ((), ()))
MESH = pl.DeviceIdType.MESH


def cosines(n):
    rows = jnp.arange(n, dtype=jnp.int32).astype(jnp.float32)[:, None]
    cols = jnp.arange(n, dtype=jnp.int32).astype(jnp.float32)[None, :]
    table = jnp.sqrt(2.0 / n) * jnp.cos(jnp.pi * rows * (cols + 0.5) / n)
    table = table * jnp.where(rows == 0, jnp.sqrt(0.5), 1.0)
    return table.astype(jnp.bfloat16)


def dot(a, b):
    return jnp.dot(a, b, preferred_element_type=F32)


def dot_nt(a, b):
    return lax.dot_general(a, b, NT, preferred_element_type=F32)


def iota(dims, axis):
    return lax.broadcasted_iota(jnp.int32, dims, axis)


def ones_at(rows, cols):
    return (iota((rows, cols), 0) == iota((rows, cols), 1)).astype(F32).astype(BF16)


def transposed(table):
    return dot_nt(ones_at(table.shape[1], table.shape[1]), table).astype(BF16)


def window_base(starts_ref, s, tile):
    return pl.multiple_of((starts_ref[s, 0, tile] // LANES) * LANES, LANES)


def overflow(starts_ref, slabs):
    total = starts_ref[0, 0, TILES + 1]
    for s in range(1, slabs):
        total = total + starts_ref[s, 0, TILES + 1]
    return total > 0


def hot_rows(rows, tile, cells):
    at = rows[2:3] - (tile * cells).astype(F32)
    return iota((cells, WIN), 0).astype(F32) == at


def hot_z(rows):
    here = iota((N3, WIN), 0).astype(F32) == rows[3:4]
    return here.astype(F32).astype(BF16)


def scatter_window(data_ref, s, base, tile, cells):
    rows = data_ref[s, :, pl.ds(base, WIN)]
    hot = hot_rows(rows, tile, cells)
    both = [jnp.where(hot, rows[0:1], 0.0), jnp.where(hot, rows[1:2], 0.0)]
    return dot_nt(jnp.concatenate(both, axis=0).astype(BF16), hot_z(rows))


def plane_of(parts, t, ny):
    cells = TILE * ny
    rows = [p[b * cells + t * ny : b * cells + (t + 1) * ny] for b in range(2) for p in parts]
    return jnp.concatenate(rows, axis=0)


def scatter_planes(starts_ref, data_ref, plane_ref):
    slabs = data_ref.shape[0]
    ny = N2 // slabs
    cells = TILE * ny
    unroll = 4

    @pl.loop(0, TILES // unroll)
    def _(group):
        for u in range(unroll):
            tile = group * unroll + u
            parts = [
                scatter_window(data_ref, s, window_base(starts_ref, s, tile), tile, cells)
                for s in range(slabs)
            ]
            for t in range(TILE):
                plane_ref[tile * TILE + t] = plane_of(parts, t, ny).astype(BF16)

    @pl.when(overflow(starts_ref, slabs))
    def _():
        @pl.loop(0, TILES)
        def _(tile):
            parts = []
            for s in range(slabs):
                base = window_base(starts_ref, s, tile)

                def more(i, acc):
                    at = pl.multiple_of(base + i * WIN, LANES)
                    return acc + scatter_window(data_ref, s, at, tile, cells)

                windows = (starts_ref[s, 0, tile + 1] - base + WIN - 1) // WIN
                zero = jnp.zeros((2 * cells, N3), F32)
                parts.append(lax.fori_loop(1, windows, more, zero))
            for t in range(TILE):
                old = plane_ref[tile * TILE + t].astype(F32)
                plane_ref[tile * TILE + t] = (old + plane_of(parts, t, ny)).astype(BF16)


def zy_kernel(starts_ref, data_ref, tab_ref, turned_ref, plane_ref):
    scatter_planes(starts_ref, data_ref, plane_ref)
    inv_y = transposed(tab_ref[...])
    inv_z = dot(tab_ref[...], ones_at(N3, LANES)).astype(BF16)
    width = 16

    @pl.loop(0, N1 // width)
    def _(group):
        first = pl.multiple_of(group * width, width)
        flat = plane_ref[pl.ds(first, width)].reshape(width * 2 * N2, N3)
        z_done = dot(flat, inv_z).astype(BF16)
        done = []
        for u in range(width):
            one = z_done[2 * N2 * u : 2 * N2 * u + N2]
            two = z_done[2 * N2 * u + N2 : 2 * N2 * (u + 1)]
            done.append(dot(inv_y, jnp.concatenate([one, two], axis=1)).astype(BF16))
        turned_ref[:, pl.ds(first, width), :] = jnp.swapaxes(jnp.stack(done, axis=0), 0, 1)


def gather_window(data_ref, wave_ref, sum_ref, s, base, tile, ny):
    cells = TILE * ny
    at = pl.ds(base, WIN)
    rows = data_ref[s, :, at]
    hot = hot_rows(rows, tile, cells)
    mine = wave_ref[s, pl.ds(tile * TILE, TILE)].reshape(TILE * 2 * ny, N3)
    picked = dot(mine, hot_z(rows))
    found = []
    for b in range(2):
        part = jnp.concatenate(
            [picked[(2 * t + b) * ny : (2 * t + b + 1) * ny] for t in range(TILE)], axis=0
        )
        found.append(jnp.sum(jnp.where(hot, part, 0.0), axis=0, keepdims=True))
    sum_ref[s, :, at] += jnp.concatenate(found, axis=0)


def gather_kernel(starts_ref, data_ref, wave_ref, out_ref, sum_ref):
    slabs = data_ref.shape[0]
    ny = N2 // slabs
    sum_ref[...] = jnp.zeros_like(sum_ref)
    several = 4

    @pl.loop(0, TILES // several)
    def _(group):
        for u in range(several):
            tile = group * several + u
            for s in range(slabs):
                gather_window(data_ref, wave_ref, sum_ref, s, window_base(starts_ref, s, tile), tile, ny)

    @pl.when(overflow(starts_ref, slabs))
    def _():
        @pl.loop(0, TILES)
        def _(tile):
            for s in range(slabs):
                base = window_base(starts_ref, s, tile)

                @pl.loop(1, (starts_ref[s, 0, tile + 1] - base + WIN - 1) // WIN)
                def _(i):
                    at = pl.multiple_of(base + i * WIN, LANES)
                    gather_window(data_ref, wave_ref, sum_ref, s, at, tile, ny)

    out_ref[...] = sum_ref[:, :, : out_ref.shape[2]].astype(out_ref.dtype)


SMEM = pl.BlockSpec(memory_space=pltpu.SMEM)
VMEM = pl.BlockSpec(memory_space=pltpu.VMEM)
LIMIT = 32 * 1024 * 1024


def greet(peers):
    barrier = pltpu.get_barrier_semaphore()
    for peer in peers:
        pl.semaphore_signal(barrier, inc=1, device_id=peer, device_id_type=MESH)
    pl.semaphore_wait(barrier, len(peers))


def remote(src, dst, send_sem, recv_sem, peer):
    return pltpu.make_async_remote_copy(
        src_ref=src, dst_ref=dst, send_sem=send_sem, recv_sem=recv_sem, device_id=peer, device_id_type=MESH
    )


def send(src, dst, send_sem, recv_sem, peer):
    copy = remote(src, dst, send_sem, recv_sem, peer)
    copy.start()
    return copy


def wait_all(copies):
    for copy in copies:
        copy.wait()


def slab_peers(slabs):
    me = lax.axis_index("slab")
    return [lax.rem(me + d, slabs) for d in range(1, slabs)]


def place():
    band, slab = lax.axis_index("band"), lax.axis_index("slab")
    return band // 4, slab // 2, lax.rem(band, 4), lax.rem(slab, 2)


def device(y_hi, y_lo, z, core):
    return {"band": y_hi * 4 + z, "slab": y_lo * 2 + core}


def start_kernel(
    coef_ref, map_ref, data_ref, starts_ref, own_coef, own_map, coefs_ref, maps_ref, send_sem, recv_sem
):
    slabs, two, npw = coefs_ref.shape
    ny = N2 // slabs
    me = lax.axis_index("slab")
    peers = slab_peers(slabs)
    chunk = 1536
    for r in range(npw // LANES):
        own_map[0:1, r * LANES : (r + 1) * LANES] = map_ref[r : r + 1, :]
    for i in range(npw // chunk):
        at = pl.ds(i * chunk, chunk)
        block = coef_ref[:, at].astype(F32)
        for t in range(slabs):
            own_coef[t, :, at] = block[two * t : two * (t + 1)].astype(BF16)
    greet([{"slab": peer} for peer in peers])
    coef_copies = []
    for i, peer in enumerate(peers):
        to = {"slab": peer}
        coef_copies.append(send(own_coef.at[peer], coefs_ref.at[me], send_sem.at[0, i], recv_sem.at[0, i], to))
    coefs_ref[me] = own_coef[me]
    edges = iota((56, LANES), 0) * (TILE * ny * N3)
    below = jnp.zeros((56, LANES), jnp.int32)
    for r in range(npw // LANES):
        below = below + (own_map[0:1, r * LANES : (r + 1) * LANES] < edges).astype(jnp.int32)
    count = jnp.sum(below.astype(F32), axis=1, keepdims=True)
    spread = jnp.where(iota((56, LANES), 0) == iota((56, LANES), 1), count, 0.0)
    starts = jnp.sum(spread, axis=0, keepdims=True).astype(jnp.int32)
    after = pltpu.roll(starts, LANES - 1, 1)
    lane = iota((1, LANES), 1)
    over = (after > jnp.bitwise_and(starts, -LANES) + WIN) & (lane < TILES)
    flag = jnp.max(over.astype(F32), axis=1, keepdims=True).astype(jnp.int32)
    own_map[0:1, npw : npw + LANES] = jnp.where(lane == TILES + 1, flag, starts)
    copies = []
    for i, peer in enumerate(peers):
        to = {"slab": peer}
        copies.append(send(own_map, maps_ref.at[me], send_sem.at[1, i], recv_sem.at[1, i], to))
    maps_ref[me] = own_map[...]
    data_ref[...] = jnp.full(data_ref.shape, -1.0, F32)
    wait_all(copies)
    for s in range(slabs):
        starts_ref[s] = maps_ref[s, :, npw : npw + LANES]
    y_first = (iota((slabs, 1), 0) * ny).astype(F32)
    for i in range(npw // chunk):
        at = pl.ds(i * chunk, chunk)
        cell = jnp.concatenate([maps_ref[s, :, at] for s in range(slabs)], axis=0).astype(F32)
        row = jnp.floor((cell + 0.5) * (1.0 / N3))
        zpos = cell - row * N3
        xpos = jnp.floor((row + 0.5) * (1.0 / ny))
        ypos = row - xpos * ny + y_first
        kin = 2.0 * (xpos * xpos / (N1 * N1) + ypos * ypos / (N2 * N2) + zpos * zpos / (N3 * N3))
        for s in range(slabs):
            lines = [part[s : s + 1] for part in (row, zpos, kin)]
            data_ref[s, 2:5, at] = jnp.concatenate(lines, axis=0)
    wait_all(coef_copies)
    for s in range(slabs):
        for i in range(npw // chunk):
            at = pl.ds(i * chunk, chunk)
            data_ref[s, 0:2, at] = coefs_ref[s, :, at].astype(F32)


def dense_kernel(
    turned_ref, pot_ref, tab_ref, psi_ref, wave_ref, pots_ref, back_ref, send_sem, recv_sem
):
    slabs = wave_ref.shape[0]
    ny = N2 // slabs
    y_hi, y_lo, z, core = place()
    me = lax.axis_index("slab")
    y = y_hi * 2 + y_lo
    sibling = device(y_hi, y_lo, z, 1 - core)

    def around(step, other):
        to = lax.rem(y + step + 4, 4)
        return device(to // 2, lax.rem(to, 2), z, other)

    for i in range(3):
        at = pl.ds(i * 3072, 3072)
        pots_ref[me, :, at] = pot_ref[:, at].astype(BF16)
    greet([sibling] + [around(step, other) for step in (-1, 1) for other in (0, 1)])
    mine = pots_ref.at[me]
    copies = [send(mine, mine, send_sem.at[2], recv_sem.at[2], sibling)]
    for other in (0, 1):
        to = around(2 * core - 1, other)
        copies.append(send(mine, mine, send_sem.at[other], recv_sem.at[core], to))

    inv_x = transposed(tab_ref[...])
    unroll = 8

    @pl.loop(0, N2 // unroll)
    def _(group):
        for u in range(unroll):
            row = group * unroll + u
            psi_ref[row] = dot(inv_x, turned_ref[row]).astype(BF16)

    copies[0].wait()
    for copy in copies[1:]:
        copy.wait_send()
    for other in (0, 1):
        slot = pots_ref.at[(1 - y_lo) * 2 + other]
        remote(slot, slot, send_sem.at[other], recv_sem.at[other], sibling).wait_recv()

    width = 16
    lane = iota((N1 // slabs, LANES), 1)

    @pl.loop(0, N2 // width)
    def _(group):
        first = pl.multiple_of(group * width, width)
        done = []
        for v in range(width // 4):
            quads = [[], [], [], []]
            for s in range(slabs):
                parts = []
                for j in range(3):
                    off = pl.multiple_of(group * (width * N3) + (3 * v + j) * LANES, LANES)
                    parts.append(pots_ref[s, :, pl.ds(off, LANES)].astype(F32))
                a, b, c = parts
                quads[0].append(a)
                quads[1].append(jnp.where(lane < 32, pltpu.roll(a, 32, 1), pltpu.roll(b, 32, 1)))
                quads[2].append(jnp.where(lane < 64, pltpu.roll(b, 64, 1), pltpu.roll(c, 64, 1)))
                quads[3].append(pltpu.roll(c, 96, 1))
            for u in range(4):
                pot = jnp.concatenate(quads[u], axis=0)
                psi = psi_ref[first + 4 * v + u].astype(F32)
                product = jnp.concatenate([pot * psi[:, :LANES], pot * psi[:, LANES:]], axis=1)
                done.append(dot(tab_ref[...], product.astype(BF16)).astype(BF16))
        back_ref[:, pl.ds(first, width), :] = jnp.swapaxes(jnp.stack(done, axis=0), 0, 1)

    fwd_z = dot_nt(ones_at(LANES, N3), tab_ref[...]).astype(BF16)

    @pl.loop(0, N1 // unroll)
    def _(group):
        done = []
        for u in range(unroll):
            y_done = dot(tab_ref[...], back_ref[group * unroll + u]).astype(BF16)
            done += [y_done[:, :LANES], y_done[:, LANES:]]
        waves = dot(jnp.concatenate(done, axis=0), fwd_z)
        for u in range(unroll):
            for s in range(slabs):
                one = waves[2 * u * N2 + s * ny : 2 * u * N2 + (s + 1) * ny]
                two = waves[(2 * u + 1) * N2 + s * ny : (2 * u + 1) * N2 + (s + 1) * ny]
                wave_ref[s, group * unroll + u] = jnp.concatenate([one, two], axis=0).astype(BF16)


def middle_kernel(
    waves_ref, bands_ref, index_ref, energy_ref, data_ref, step_ref,
    got_ref, corr_ref, rhs_ref, back_ref, total_ref, send_sem, recv_sem,
):
    slabs, two, npw = waves_ref.shape
    chunk = 1536
    me = lax.axis_index("slab")
    peers = slab_peers(slabs)
    greet([{"slab": peer} for peer in peers])
    copies = []
    for i, peer in enumerate(peers):
        to = {"slab": peer}
        copies.append(send(waves_ref.at[peer], got_ref.at[me], send_sem.at[0, i], recv_sem.at[0, i], to))
    got_ref[me] = waves_ref[me]
    data_ref[...] = index_ref[...]
    wait_all(copies)

    def waves_at(at):
        return jnp.concatenate([got_ref[t, :, at].astype(F32) for t in range(slabs)], axis=0)

    total = jnp.zeros(total_ref.shape, F32)
    for i in range(npw // chunk):
        at = pl.ds(i * chunk, chunk)
        total = total + dot_nt(waves_at(at).astype(BF16), bands_ref[:, at])
    total_ref[...] = total

    copies = []
    for i, peer in enumerate(peers):
        to = {"slab": peer}
        copies.append(send(total_ref, corr_ref.at[i], send_sem.at[1, i], recv_sem.at[1, i], to))
    wait_all(copies)
    correlation = total_ref[...]
    for i in range(slabs - 1):
        correlation = correlation + corr_ref[i]
    correlation = correlation.astype(BF16)

    for i in range(npw // chunk):
        at = pl.ds(i * chunk, chunk)
        rhs = (waves_at(at) - dot(correlation, bands_ref[:, at])).astype(BF16)
        for t in range(slabs):
            rhs_ref[t, :, at] = rhs[two * t : two * (t + 1)]

    copies = []
    for i, peer in enumerate(peers):
        to = {"slab": peer}
        copies.append(send(rhs_ref.at[peer], back_ref.at[me], send_sem.at[2, i], recv_sem.at[2, i], to))
    back_ref[me] = rhs_ref[me]
    wait_all(copies)

    numer = jnp.zeros((two, chunk), F32)
    denom = jnp.zeros((two, chunk), F32)
    energy = jnp.concatenate([jnp.full((1, chunk), energy_ref[b], F32) for b in range(two)], axis=0)
    for s in range(slabs):
        for i in range(npw // chunk):
            at = pl.ds(i * chunk, chunk)
            mine = back_ref[s, :, at].astype(F32)
            data_ref[s, 0:2, at] = mine
            squares = mine * mine
            numer = numer + squares
            denom = denom + (index_ref[s, 4:5, at] - energy) * squares
    step = -jnp.sum(numer, axis=1, keepdims=True) / jnp.sum(denom, axis=1, keepdims=True)
    scale = 4.0 * N1 * N2 * N3 / bands_ref.shape[0]
    step_ref[...] = jnp.broadcast_to(scale * step, step_ref.shape)


PART_A = 5
PART_B = 4
PARTS = PART_A + PART_B


def end_kernel(
    turned_ref, psi_ref, step_ref, pot_ref, tab_ref, out_ref, projected_ref,
    dens_ref, from_core, a_ref, b_ref, a_from_y, b_from_z, a_sum, b_sum, a_from_z, b_from_y,
    pots_ref, sums_ref, from_sums, core_send, core_recv, pot_send, pot_recv, a_send, a_recv, b_send, b_recv,
    a2_send, a2_recv, b2_send, b2_recv, sum_send, sum_recv,
):
    perts, planes, width = pots_ref.shape
    slabs = dens_ref.shape[0]
    y_hi, y_lo, z, core = place()
    pert, band = lax.axis_index("pert"), lax.axis_index("band")
    sibling = device(y_hi, y_lo, z, 1 - core)
    y_coords = [(1 - y_hi, y_lo), (1 - y_hi, 1 - y_lo), (y_hi, 1 - y_lo)]
    y_peers = [device(a, b, z, core) for a, b in y_coords]
    y_others = [device(a, b, z, 1 - core) for a, b in y_coords]
    z_coords = [lax.rem(z + d, 4) for d in range(1, 4)]
    z_peers = [device(y_hi, y_lo, c, core) for c in z_coords]
    p_peers = [{"pert": lax.rem(pert + d, perts)} for d in range(1, perts)]
    greet([sibling] + y_peers + y_others + z_peers + p_peers)

    pots_ref[pert] = pot_ref[:, pl.ds(pl.multiple_of(band * width, LANES), width)]
    pot_copies = []
    for i, peer in enumerate(p_peers):
        mine = pots_ref.at[pert]
        pot_copies.append(send(mine, mine, pot_send.at[i], pot_recv.at[i], peer))

    inv_x = transposed(tab_ref[...])
    lane = iota((N1, LANES), 1)
    half = 4 * PARTS

    def density_half(h):
        @pl.loop(0, 6)
        def _(group):
            for v in range(2):
                quad = h * 12 + group * 2 + v
                parts = []
                for u in range(4):
                    row = quad * 4 + u
                    field = dot(inv_x, turned_ref[row]).astype(BF16).astype(F32)
                    terms = psi_ref[row].astype(F32) * field
                    parts.append(step_ref[0:1] * terms[:, :LANES] + step_ref[1:2] * terms[:, LANES:])
                one, two, three = [pltpu.roll(parts[u], LANES - 32 * u, 1) for u in (1, 2, 3)]
                tiles = [
                    jnp.where(lane < 96, parts[0], one),
                    jnp.where(lane < 64, one, two),
                    jnp.where(lane < 32, two, three),
                ]
                for j, tile in enumerate(tiles):
                    for s in range(slabs):
                        dens_ref[s, quad * 3 + j] = tile[s * planes : (s + 1) * planes].astype(BF16)

    halves = [1 - y_hi, y_hi]
    core_copies = []
    for k, h in enumerate(halves):
        density_half(h)
        for l in range(2):
            src = dens_ref.at[l * 2 + 1 - core, pl.ds(h * half, half)]
            core_copies.append(
                send(src, from_core.at[k, l], core_send.at[k, l], core_recv.at[k, l], sibling)
            )

    a_copies, b_copies = [], []
    for k, h in enumerate(halves):
        wait_all(core_copies[2 * k : 2 * k + 2])
        for l in range(2):
            @pl.loop(0, 4)
            def _(c):
                for j in range(PARTS):
                    at = c * PARTS + j
                    total = dens_ref[l * 2 + core, h * half + at].astype(F32) + from_core[k, l, at].astype(F32)
                    if j < PART_A:
                        a_ref[k, l, c, j] = total.astype(BF16)
                    else:
                        b_ref[k, c, l, j - PART_A] = total.astype(BF16)
        targets = [(0, y_lo), (1, 1 - y_lo)] if k == 0 else [(2, 1 - y_lo)]
        for i, l in targets:
            a_copies.append(send(a_ref.at[k, l], a_from_y.at[i], a_send.at[i], a_recv.at[i], y_peers[i]))
        for i, c in enumerate(z_coords):
            b_copies.append(
                send(b_ref.at[k, c], b_from_z.at[k, i], b_send.at[k, i], b_recv.at[k, i], z_peers[i])
            )

    def total_of(pair):
        total = sum(pair(j) for j in range(PARTS))
        total = total[0:8] + total[8:16] + total[16:24]
        return jnp.sum(total, axis=0, keepdims=True)

    wait_all(pot_copies)

    def pot(p, j):
        return pots_ref[p, :, j * LANES : (j + 1) * LANES]

    pairs = [(p, q) for p in range(perts) for q in range(p + 1)]
    sums = [total_of(lambda j: pot(p, j) * pot(q, j)) for p, q in pairs]

    wait_all(a_copies)

    @pl.loop(0, 4)
    def _(c):
        for j in range(PART_A):
            total = a_ref[1, y_lo, c, j].astype(F32)
            for i in range(3):
                total = total + a_from_y[i, c, j].astype(F32)
            a_sum[c, j] = total.astype(BF16)

    copies = []
    for i, c in enumerate(z_coords):
        copies.append(send(a_sum.at[c], a_from_z.at[i], a2_send.at[i], a2_recv.at[i], z_peers[i]))
    wait_all(b_copies)
    for k in range(2):
        for l in range(2):
            for j in range(PART_B):
                total = b_ref[k, z, l, j].astype(F32)
                for i in range(3):
                    total = total + b_from_z[k, i, l, j].astype(F32)
                b_sum[k, l, j] = total.astype(BF16)
    for i, (k, l) in enumerate([(0, y_lo), (0, 1 - y_lo), (1, 1 - y_lo)]):
        copies.append(send(b_sum.at[k, l], b_from_y.at[i], b2_send.at[i], b2_recv.at[i], y_peers[i]))
    wait_all(copies)
    density = []
    for j in range(PARTS):
        if j < PART_A:
            total = a_sum[z, j].astype(F32)
            for i in range(3):
                total = total + a_from_z[i, j].astype(F32)
        else:
            total = b_sum[1, y_lo, j - PART_A].astype(F32)
            for i in range(3):
                total = total + b_from_y[i, j - PART_A].astype(F32)
        density.append(total)
    sums += [total_of(lambda j: pot(p, j) * density[j]) for p in range(perts)]
    sums += [jnp.zeros((1, LANES), F32)] * (16 - len(sums))
    sums_ref[0] = jnp.concatenate(sums, axis=0)

    at = 0
    for level, group in enumerate([[sibling] + y_peers + y_others, z_peers]):
        copies = []
        for i, peer in enumerate(group):
            k = at + i
            copies.append(send(sums_ref.at[level], from_sums.at[k], sum_send.at[k], sum_recv.at[k], peer))
        wait_all(copies)
        total = sums_ref[level]
        for i in range(len(group)):
            total = total + from_sums[at + i]
        sums_ref[level + 1] = total
        at += len(group)

    cells = 1.0 / (N1 * N2 * N3)
    totals = jnp.broadcast_to(jnp.sum(sums_ref[2], axis=1, keepdims=True) * cells, (16, LANES))
    gram = {pair: totals[k : k + 1] for k, pair in enumerate(pairs)}
    rhs = [totals[len(pairs) + p : len(pairs) + p + 1] for p in range(perts)]
    factor = {}
    for p in range(perts):
        for q in range(p + 1):
            value = gram[p, q]
            for k in range(q):
                value = value - factor[p, k] * factor[q, k]
            factor[p, q] = jnp.sqrt(value) if p == q else value / factor[q, q]
    coeffs = []
    for p in range(perts):
        value = rhs[p]
        for k in range(p):
            value = value - factor[p, k] * coeffs[k]
        coeffs.append(value / factor[p, p])
    for p in reversed(range(perts)):
        value = coeffs[p]
        for k in range(p + 1, perts):
            value = value - factor[k, p] * coeffs[k]
        coeffs[p] = value / factor[p, p]
    for j in range(PARTS):
        value = density[j]
        for p in range(perts):
            value = value - coeffs[p] * pot(p, j)
        out_ref[:, j * LANES : (j + 1) * LANES] = value
    projected_ref[...] = jnp.concatenate(rhs + rhs, axis=0)


def cost(flops, moved):
    return pl.CostEstimate(flops=int(flops), bytes_accessed=int(moved), transcendentals=0)


def params(collective=None):
    if collective is None:
        return pltpu.CompilerParams(vmem_limit_bytes=LIMIT)
    return pltpu.CompilerParams(vmem_limit_bytes=LIMIT, collective_id=collective, has_side_effects=True)


def shape(dims, kind):
    return jax.ShapeDtypeStruct(dims, kind)


def sems(*dims):
    return [pltpu.SemaphoreType.DMA(dims)] * 2


def start_of(coefs, wave_map, slabs):
    bands, npw = coefs.shape
    block = (slabs, bands // slabs, npw)
    return pl.pallas_call(
        start_kernel,
        out_shape=(shape((slabs, 8, npw + 2 * WIN), F32), shape((slabs, 1, LANES), jnp.int32)),
        in_specs=[VMEM] * 2,
        out_specs=(VMEM, VMEM),
        scratch_shapes=[
            pltpu.VMEM(block, BF16),
            pltpu.VMEM((1, npw + LANES), jnp.int32),
            pltpu.VMEM(block, BF16),
            pltpu.VMEM((slabs, 1, npw + LANES), jnp.int32),
        ]
        + sems(2, slabs - 1),
        compiler_params=params(1),
        name="start",
    )(coefs, wave_map.reshape(npw // LANES, LANES))


def zy_of(starts, data, tab):
    return pl.pallas_call(
        zy_kernel,
        out_shape=shape((N2, N1, 2 * LANES), BF16),
        in_specs=[SMEM] + [VMEM] * 2,
        out_specs=VMEM,
        scratch_shapes=[pltpu.VMEM((N1, 2 * N2, N3), BF16)],
        compiler_params=params(),
        cost_estimate=cost(2e10, 8e6),
        name="scatter_zy",
    )(starts, data, tab)


def dense_of(turned, pot, tab, slabs):
    return pl.pallas_call(
        dense_kernel,
        out_shape=(shape((N2, N1, 2 * LANES), BF16), shape((slabs, N1, 2 * N2 // slabs, N3), BF16)),
        in_specs=[VMEM] * 3,
        out_specs=(VMEM, VMEM),
        scratch_shapes=[
            pltpu.VMEM((slabs,) + pot.shape, BF16),
            pltpu.VMEM((N1, N2, 2 * LANES), BF16),
        ]
        + sems(3),
        compiler_params=params(4),
        cost_estimate=cost(2e10, 8e6),
        name="dense",
    )(turned, pot, tab)


def gather_of(starts, data, wave, npw):
    slabs = data.shape[0]
    return pl.pallas_call(
        gather_kernel,
        out_shape=shape((slabs, 2, npw), BF16),
        in_specs=[SMEM] + [VMEM] * 2,
        out_specs=VMEM,
        scratch_shapes=[pltpu.VMEM((slabs, 2, data.shape[2]), F32)],
        compiler_params=params(),
        cost_estimate=cost(2e10, 8e6),
        name="gather",
    )(starts, data, wave)


def middle_of(waves, bands, index, energies):
    slabs, two, npw = waves.shape
    block = pltpu.VMEM(waves.shape, BF16)
    small = (slabs * two, bands.shape[0])
    return pl.pallas_call(
        middle_kernel,
        out_shape=(shape(index.shape, F32), shape((two, LANES), F32)),
        in_specs=[VMEM] * 3 + [SMEM],
        out_specs=(VMEM, VMEM),
        scratch_shapes=[
            block,
            pltpu.VMEM((slabs - 1,) + small, F32),
            block,
            block,
            pltpu.VMEM(small, F32),
        ]
        + sems(3, slabs - 1),
        compiler_params=params(2),
        name="middle",
    )(waves, bands, index, energies)


def end_of(turned, psi, step, pot, tab, slabs, perts):
    planes, cross = pot.shape
    width = cross // 8
    tile = (planes, LANES)
    return pl.pallas_call(
        end_kernel,
        out_shape=(shape((planes, width), F32), shape((8, LANES), F32)),
        in_specs=[VMEM] * 5,
        out_specs=(VMEM, VMEM),
        scratch_shapes=[
            pltpu.VMEM((slabs, 8 * PARTS) + tile, BF16),
            pltpu.VMEM((2, 2, 4 * PARTS) + tile, BF16),
            pltpu.VMEM((2, 2, 4, PART_A) + tile, BF16),
            pltpu.VMEM((2, 4, 2, PART_B) + tile, BF16),
            pltpu.VMEM((3, 4, PART_A) + tile, BF16),
            pltpu.VMEM((2, 3, 2, PART_B) + tile, BF16),
            pltpu.VMEM((4, PART_A) + tile, BF16),
            pltpu.VMEM((2, 2, PART_B) + tile, BF16),
            pltpu.VMEM((3, PART_A) + tile, BF16),
            pltpu.VMEM((3, PART_B) + tile, BF16),
            pltpu.VMEM((perts, planes, width), F32),
            pltpu.VMEM((3, 16, LANES), F32),
            pltpu.VMEM((10, 16, LANES), F32),
        ]
        + sems(2, 2)
        + sems(3)
        + sems(3)
        + sems(2, 3)
        + sems(3)
        + sems(3)
        + sems(10),
        compiler_params=params(3),
        name="density",
    )(turned, psi, step, pot, tab)


def per_device(wave_coeffs, band_energies, trial_potentials, wave_map):
    slabs = lax.axis_size("slab")
    me = lax.axis_index("slab")
    bands, npw = wave_coeffs.shape
    planes, cross = trial_potentials.shape[1:]
    all_bands = lax.all_gather(wave_coeffs, "band", axis=0, tiled=True)
    tab = cosines(N1)
    pot = trial_potentials.reshape(planes, cross)
    energies = lax.dynamic_slice_in_dim(band_energies, me * (bands // slabs), bands // slabs, 0)
    data, starts = start_of(wave_coeffs, wave_map, slabs)
    turned = zy_of(starts, data, tab)
    psi, wave = dense_of(turned, pot, tab, slabs)
    waves = gather_of(starts, data, wave, npw)
    data, step = middle_of(waves, all_bands, data, energies)
    turned = zy_of(starts, data, tab)
    residual, projected = end_of(turned, psi, step, pot, tab, slabs, lax.axis_size("pert"))
    return (residual.reshape(1, planes, -1), projected[: lax.axis_size("pert"), :1])


def solution(mesh):
    return jax.shard_map(
        per_device,
        mesh=mesh,
        in_specs=(P("band", "slab"), P("band"), P("pert", "slab", None), P("slab")),
        out_specs=(P("pert", "slab", "band"), P(None, "pert")),
        check_vma=False,
    )
```

```python
import jax
import jax.numpy as jnp
from jax import lax
from jax.experimental import pallas as pl
from jax.experimental.pallas import tpu as pltpu
from jax.sharding import PartitionSpec as P

N1 = 96
N2 = 96
N3 = 96
LANES = 128
WIN = 512
TILE = 2
TILES = N1 // TILE
QUARTERS = 4
F32 = jnp.float32
BF16 = jnp.bfloat16
NT = (((1,), (1,)), ((), ()))
MESH = pl.DeviceIdType.MESH


def cosines(n):
    rows = jnp.arange(n, dtype=jnp.int32).astype(jnp.float32)[:, None]
    cols = jnp.arange(n, dtype=jnp.int32).astype(jnp.float32)[None, :]
    table = jnp.sqrt(2.0 / n) * jnp.cos(jnp.pi * rows * (cols + 0.5) / n)
    table = table * jnp.where(rows == 0, jnp.sqrt(0.5), 1.0)
    return table.astype(jnp.bfloat16)


def dot(a, b):
    return jnp.dot(a, b, preferred_element_type=F32)


def dot_nt(a, b):
    return lax.dot_general(a, b, NT, preferred_element_type=F32)


def iota(dims, axis):
    return lax.broadcasted_iota(jnp.int32, dims, axis)


def ones_at(rows, cols):
    return (iota((rows, cols), 0) == iota((rows, cols), 1)).astype(F32).astype(BF16)


def transposed(table):
    return dot_nt(ones_at(table.shape[1], table.shape[1]), table).astype(BF16)


def window_base(starts_ref, s, tile):
    return pl.multiple_of((starts_ref[s, 0, tile] // LANES) * LANES, LANES)


def overflow(starts_ref, slabs):
    total = starts_ref[0, 0, TILES + 1]
    for s in range(1, slabs):
        total = total + starts_ref[s, 0, TILES + 1]
    return total > 0


def hot_rows(rows, tile, cells):
    at = rows[2:3] - (tile * cells).astype(F32)
    return iota((cells, WIN), 0).astype(F32) == at


def hot_z(rows):
    here = iota((N3, WIN), 0).astype(F32) == rows[3:4]
    return here.astype(F32).astype(BF16)


def scatter_window(data_ref, s, base, tile, cells):
    rows = data_ref[s, :, pl.ds(base, WIN)]
    hot = hot_rows(rows, tile, cells)
    both = [jnp.where(hot, rows[0:1], 0.0), jnp.where(hot, rows[1:2], 0.0)]
    return dot_nt(jnp.concatenate(both, axis=0).astype(BF16), hot_z(rows))


def plane_of(parts, t, ny):
    cells = TILE * ny
    rows = [p[b * cells + t * ny : b * cells + (t + 1) * ny] for b in range(2) for p in parts]
    return jnp.concatenate(rows, axis=0)


def scatter_planes(starts_ref, data_ref, plane_ref):
    slabs = data_ref.shape[0]
    ny = N2 // slabs
    cells = TILE * ny
    unroll = 4

    @pl.loop(0, TILES // unroll)
    def _(group):
        for u in range(unroll):
            tile = group * unroll + u
            parts = [
                scatter_window(data_ref, s, window_base(starts_ref, s, tile), tile, cells)
                for s in range(slabs)
            ]
            for t in range(TILE):
                plane_ref[tile * TILE + t] = plane_of(parts, t, ny).astype(BF16)

    @pl.when(overflow(starts_ref, slabs))
    def _():
        @pl.loop(0, TILES)
        def _(tile):
            parts = []
            for s in range(slabs):
                base = window_base(starts_ref, s, tile)

                def more(i, acc):
                    at = pl.multiple_of(base + i * WIN, LANES)
                    return acc + scatter_window(data_ref, s, at, tile, cells)

                windows = (starts_ref[s, 0, tile + 1] - base + WIN - 1) // WIN
                zero = jnp.zeros((2 * cells, N3), F32)
                parts.append(lax.fori_loop(1, windows, more, zero))
            for t in range(TILE):
                old = plane_ref[tile * TILE + t].astype(F32)
                plane_ref[tile * TILE + t] = (old + plane_of(parts, t, ny)).astype(BF16)


def zy_kernel(starts_ref, data_ref, tab_ref, turned_ref, plane_ref):
    scatter_planes(starts_ref, data_ref, plane_ref)
    inv_y = transposed(tab_ref[...])
    inv_z = dot(tab_ref[...], ones_at(N3, LANES)).astype(BF16)
    width = 16

    @pl.loop(0, N1 // width)
    def _(group):
        first = pl.multiple_of(group * width, width)
        flat = plane_ref[pl.ds(first, width)].reshape(width * 2 * N2, N3)
        z_done = dot(flat, inv_z).astype(BF16)
        done = []
        for u in range(width):
            one = z_done[2 * N2 * u : 2 * N2 * u + N2]
            two = z_done[2 * N2 * u + N2 : 2 * N2 * (u + 1)]
            done.append(dot(inv_y, jnp.concatenate([one, two], axis=1)).astype(BF16))
        turned_ref[:, pl.ds(first, width), :] = jnp.swapaxes(jnp.stack(done, axis=0), 0, 1)


def gather_window(data_ref, wave_ref, sum_ref, s, base, tile, ny):
    cells = TILE * ny
    at = pl.ds(base, WIN)
    rows = data_ref[s, :, at]
    hot = hot_rows(rows, tile, cells)
    mine = wave_ref[s, pl.ds(tile * TILE, TILE)].reshape(TILE * 2 * ny, N3)
    picked = dot(mine, hot_z(rows))
    found = []
    for b in range(2):
        part = jnp.concatenate(
            [picked[(2 * t + b) * ny : (2 * t + b + 1) * ny] for t in range(TILE)], axis=0
        )
        found.append(jnp.sum(jnp.where(hot, part, 0.0), axis=0, keepdims=True))
    sum_ref[s, :, at] += jnp.concatenate(found, axis=0)


def gather_kernel(starts_ref, data_ref, wave_ref, out_ref, sum_ref):
    slabs = data_ref.shape[0]
    ny = N2 // slabs
    sum_ref[...] = jnp.zeros_like(sum_ref)
    several = 4

    @pl.loop(0, TILES // several)
    def _(group):
        for u in range(several):
            tile = group * several + u
            for s in range(slabs):
                gather_window(data_ref, wave_ref, sum_ref, s, window_base(starts_ref, s, tile), tile, ny)

    @pl.when(overflow(starts_ref, slabs))
    def _():
        @pl.loop(0, TILES)
        def _(tile):
            for s in range(slabs):
                base = window_base(starts_ref, s, tile)

                @pl.loop(1, (starts_ref[s, 0, tile + 1] - base + WIN - 1) // WIN)
                def _(i):
                    at = pl.multiple_of(base + i * WIN, LANES)
                    gather_window(data_ref, wave_ref, sum_ref, s, at, tile, ny)

    part = out_ref.shape[3]
    for q in range(out_ref.shape[1]):
        out_ref[:, q] = sum_ref[:, :, q * part : (q + 1) * part].astype(out_ref.dtype)


SMEM = pl.BlockSpec(memory_space=pltpu.SMEM)
VMEM = pl.BlockSpec(memory_space=pltpu.VMEM)
LIMIT = 32 * 1024 * 1024


def greet(peers):
    barrier = pltpu.get_barrier_semaphore()
    for peer in peers:
        pl.semaphore_signal(barrier, inc=1, device_id=peer, device_id_type=MESH)
    pl.semaphore_wait(barrier, len(peers))


def remote(src, dst, send_sem, recv_sem, peer):
    return pltpu.make_async_remote_copy(
        src_ref=src, dst_ref=dst, send_sem=send_sem, recv_sem=recv_sem, device_id=peer, device_id_type=MESH
    )


def send(src, dst, send_sem, recv_sem, peer):
    copy = remote(src, dst, send_sem, recv_sem, peer)
    copy.start()
    return copy


def wait_all(copies):
    for copy in copies:
        copy.wait()


def slab_peers(slabs):
    me = lax.axis_index("slab")
    return [lax.rem(me + d, slabs) for d in range(1, slabs)]


def place():
    band, slab = lax.axis_index("band"), lax.axis_index("slab")
    return band // 4, slab // 2, lax.rem(band, 4), lax.rem(slab, 2)


def device(y_hi, y_lo, z, core):
    return {"band": y_hi * 4 + z, "slab": y_lo * 2 + core}


def start_kernel(
    coef_ref, map_ref, data_ref, starts_ref, own_coef, own_map, coefs_ref, maps_ref, send_sem, recv_sem
):
    slabs, two, npw = coefs_ref.shape
    ny = N2 // slabs
    me = lax.axis_index("slab")
    peers = slab_peers(slabs)
    chunk = 1536
    for r in range(npw // LANES):
        own_map[0:1, r * LANES : (r + 1) * LANES] = map_ref[r : r + 1, :]
    for i in range(npw // chunk):
        at = pl.ds(i * chunk, chunk)
        block = coef_ref[:, at].astype(F32)
        for t in range(slabs):
            own_coef[t, :, at] = block[two * t : two * (t + 1)].astype(BF16)
    greet([{"slab": peer} for peer in peers])
    coef_copies = []
    for i, peer in enumerate(peers):
        to = {"slab": peer}
        coef_copies.append(send(own_coef.at[peer], coefs_ref.at[me], send_sem.at[0, i], recv_sem.at[0, i], to))
    coefs_ref[me] = own_coef[me]
    edges = iota((56, LANES), 0) * (TILE * ny * N3)
    below = jnp.zeros((56, LANES), jnp.int32)
    for r in range(npw // LANES):
        below = below + (own_map[0:1, r * LANES : (r + 1) * LANES] < edges).astype(jnp.int32)
    count = jnp.sum(below.astype(F32), axis=1, keepdims=True)
    spread = jnp.where(iota((56, LANES), 0) == iota((56, LANES), 1), count, 0.0)
    starts = jnp.sum(spread, axis=0, keepdims=True).astype(jnp.int32)
    after = pltpu.roll(starts, LANES - 1, 1)
    lane = iota((1, LANES), 1)
    over = (after > jnp.bitwise_and(starts, -LANES) + WIN) & (lane < TILES)
    flag = jnp.max(over.astype(F32), axis=1, keepdims=True).astype(jnp.int32)
    own_map[0:1, npw : npw + LANES] = jnp.where(lane == TILES + 1, flag, starts)
    copies = []
    for i, peer in enumerate(peers):
        to = {"slab": peer}
        copies.append(send(own_map, maps_ref.at[me], send_sem.at[1, i], recv_sem.at[1, i], to))
    maps_ref[me] = own_map[...]
    data_ref[...] = jnp.full(data_ref.shape, -1.0, F32)
    wait_all(copies)
    for s in range(slabs):
        starts_ref[s] = maps_ref[s, :, npw : npw + LANES]
    y_first = (iota((slabs, 1), 0) * ny).astype(F32)
    for i in range(npw // chunk):
        at = pl.ds(i * chunk, chunk)
        cell = jnp.concatenate([maps_ref[s, :, at] for s in range(slabs)], axis=0).astype(F32)
        row = jnp.floor((cell + 0.5) * (1.0 / N3))
        zpos = cell - row * N3
        xpos = jnp.floor((row + 0.5) * (1.0 / ny))
        ypos = row - xpos * ny + y_first
        kin = 2.0 * (xpos * xpos / (N1 * N1) + ypos * ypos / (N2 * N2) + zpos * zpos / (N3 * N3))
        for s in range(slabs):
            lines = [part[s : s + 1] for part in (row, zpos, kin)]
            data_ref[s, 2:5, at] = jnp.concatenate(lines, axis=0)
    wait_all(coef_copies)
    for s in range(slabs):
        for i in range(npw // chunk):
            at = pl.ds(i * chunk, chunk)
            data_ref[s, 0:2, at] = coefs_ref[s, :, at].astype(F32)


def dense_kernel(
    turned_ref, pot_ref, coef_ref, tab_ref, psi_ref, wave_ref, bands_ref,
    pots_ref, back_ref, send_sem, recv_sem, coef_send, coef_recv,
):
    slabs = wave_ref.shape[0]
    ny = N2 // slabs
    y_hi, y_lo, z, core = place()
    me = lax.axis_index("slab")
    y = y_hi * 2 + y_lo
    sibling = device(y_hi, y_lo, z, 1 - core)

    def around(step, other):
        to = lax.rem(y + step + 4, 4)
        return device(to // 2, lax.rem(to, 2), z, other)

    for i in range(3):
        at = pl.ds(i * 3072, 3072)
        pots_ref[me, :, at] = pot_ref[:, at].astype(BF16)
    steps = [(a, b) for a in range(2) for b in range(4) if a + b > 0]
    others = [(lax.rem(y_hi + a, 2), lax.rem(z + b, 4)) for a, b in steps]
    members = [device(a, y_lo, b, core) for a, b in others]
    greet([sibling] + [around(step, other) for step in (-1, 1) for other in (0, 1)] + members)
    mine = pots_ref.at[me]
    copies = [send(mine, mine, send_sem.at[2], recv_sem.at[2], sibling)]
    for other in (0, 1):
        to = around(2 * core - 1, other)
        copies.append(send(mine, mine, send_sem.at[other], recv_sem.at[core], to))

    inv_x = transposed(tab_ref[...])
    unroll = 8

    @pl.loop(0, N2 // unroll)
    def _(group):
        for u in range(unroll):
            row = group * unroll + u
            psi_ref[row] = dot(inv_x, turned_ref[row]).astype(BF16)

    copies[0].wait()
    for copy in copies[1:]:
        copy.wait_send()
    for other in (0, 1):
        slot = pots_ref.at[(1 - y_lo) * 2 + other]
        remote(slot, slot, send_sem.at[other], recv_sem.at[other], sibling).wait_recv()

    part = bands_ref.shape[3]
    at = pl.ds(pl.multiple_of(z * part, LANES), part)
    bands_ref[y_hi, z] = coef_ref[:, at]
    copies = []
    for i, (_, b) in enumerate(others):
        at = pl.ds(pl.multiple_of(b * part, LANES), part)
        copies.append(
            send(coef_ref.at[:, at], bands_ref.at[y_hi, z], coef_send.at[i], coef_recv.at[i], members[i])
        )

    width = 16
    lane = iota((N1 // slabs, LANES), 1)

    @pl.loop(0, N2 // width)
    def _(group):
        first = pl.multiple_of(group * width, width)
        done = []
        for v in range(width // 4):
            quads = [[], [], [], []]
            for s in range(slabs):
                parts = []
                for j in range(3):
                    off = pl.multiple_of(group * (width * N3) + (3 * v + j) * LANES, LANES)
                    parts.append(pots_ref[s, :, pl.ds(off, LANES)].astype(F32))
                a, b, c = parts
                quads[0].append(a)
                quads[1].append(jnp.where(lane < 32, pltpu.roll(a, 32, 1), pltpu.roll(b, 32, 1)))
                quads[2].append(jnp.where(lane < 64, pltpu.roll(b, 64, 1), pltpu.roll(c, 64, 1)))
                quads[3].append(pltpu.roll(c, 96, 1))
            for u in range(4):
                pot = jnp.concatenate(quads[u], axis=0)
                psi = psi_ref[first + 4 * v + u].astype(F32)
                product = jnp.concatenate([pot * psi[:, :LANES], pot * psi[:, LANES:]], axis=1)
                done.append(dot(tab_ref[...], product.astype(BF16)).astype(BF16))
        back_ref[:, pl.ds(first, width), :] = jnp.swapaxes(jnp.stack(done, axis=0), 0, 1)

    fwd_z = dot_nt(ones_at(LANES, N3), tab_ref[...]).astype(BF16)

    @pl.loop(0, N1 // unroll)
    def _(group):
        done = []
        for u in range(unroll):
            y_done = dot(tab_ref[...], back_ref[group * unroll + u]).astype(BF16)
            done += [y_done[:, :LANES], y_done[:, LANES:]]
        waves = dot(jnp.concatenate(done, axis=0), fwd_z)
        for u in range(unroll):
            for s in range(slabs):
                one = waves[2 * u * N2 + s * ny : 2 * u * N2 + (s + 1) * ny]
                two = waves[(2 * u + 1) * N2 + s * ny : (2 * u + 1) * N2 + (s + 1) * ny]
                wave_ref[s, group * unroll + u] = jnp.concatenate([one, two], axis=0).astype(BF16)

    wait_all(copies)


def middle_kernel(
    waves_ref, bands_ref, index_ref, energy_ref, data_ref, step_ref,
    got_ref, corr_ref, rhs_ref, back_ref, total_ref, send_sem, recv_sem,
):
    slabs, quarters, two, part = waves_ref.shape
    half, zs, bands, _ = bands_ref.shape
    chunk = 1152
    y_hi, y_lo, z, core = place()
    slab = lax.axis_index("slab")
    steps = [(a, b) for a in range(quarters) for b in range(slabs) if a + b > 0]
    others = [(lax.rem(z + a, quarters), lax.rem(slab + b, slabs)) for a, b in steps]
    peers = [{"band": y_hi * 4 + c, "slab": t} for c, t in others]
    greet(peers)
    copies = []
    for i, (c, t) in enumerate(others):
        src, dst = waves_ref.at[t, c], got_ref.at[z, slab]
        copies.append(send(src, dst, send_sem.at[0, i], recv_sem.at[0, i], peers[i]))
    got_ref[z, slab] = waves_ref[slab, z]
    data_ref[...] = index_ref[...]
    wait_all(copies)

    def waves_at(at):
        parts = [got_ref[c, t, :, at].astype(F32) for c in range(quarters) for t in range(slabs)]
        return jnp.concatenate(parts, axis=0)

    def bands_at(at):
        parts = [bands_ref[a, c, :, at].astype(F32) for a in range(half) for c in range(zs)]
        return jnp.concatenate(parts, axis=0).astype(BF16)

    total = jnp.zeros(total_ref.shape, F32)
    for i in range(part // chunk):
        at = pl.ds(i * chunk, chunk)
        total = total + dot_nt(waves_at(at).astype(BF16), bands_at(at))
    total_ref[...] = total

    copies = []
    for i, peer in enumerate(peers):
        copies.append(send(total_ref, corr_ref.at[i], send_sem.at[1, i], recv_sem.at[1, i], peer))
    wait_all(copies)
    correlation = total_ref[...]
    for i in range(len(peers)):
        correlation = correlation + corr_ref[i]
    correlation = correlation.astype(BF16)

    for i in range(part // chunk):
        at = pl.ds(i * chunk, chunk)
        rhs = (waves_at(at) - dot(correlation, bands_at(at))).astype(BF16).astype(F32)
        for c in range(quarters):
            for t in range(slabs):
                first = two * (c * slabs + t)
                rhs_ref[c, t, :, at] = rhs[first : first + two].astype(BF16)

    copies = []
    for i, (c, t) in enumerate(others):
        src, dst = rhs_ref.at[c, t], back_ref.at[slab, z]
        copies.append(send(src, dst, send_sem.at[2, i], recv_sem.at[2, i], peers[i]))
    back_ref[slab, z] = rhs_ref[z, slab]
    wait_all(copies)

    numer = jnp.zeros((two, chunk), F32)
    denom = jnp.zeros((two, chunk), F32)
    energy = jnp.concatenate([jnp.full((1, chunk), energy_ref[b], F32) for b in range(two)], axis=0)
    for s in range(slabs):
        for q in range(quarters):
            for i in range(part // chunk):
                at = pl.ds(q * part + i * chunk, chunk)
                mine = back_ref[s, q, :, i * chunk : (i + 1) * chunk].astype(F32)
                data_ref[s, 0:2, at] = mine
                squares = mine * mine
                numer = numer + squares
                denom = denom + (index_ref[s, 4:5, at] - energy) * squares
    step = -jnp.sum(numer, axis=1, keepdims=True) / jnp.sum(denom, axis=1, keepdims=True)
    scale = 4.0 * N1 * N2 * N3 / (half * zs * bands)
    step_ref[...] = jnp.broadcast_to(scale * step, step_ref.shape)


PART_A = 5
PART_B = 4
PARTS = PART_A + PART_B


def end_kernel(
    turned_ref, psi_ref, step_ref, pot_ref, tab_ref, out_ref, projected_ref,
    dens_ref, from_core, a_ref, b_ref, a_from_y, b_from_z, a_sum, b_sum, a_from_z, b_from_y,
    pots_ref, sums_ref, from_sums, core_send, core_recv, pot_send, pot_recv, a_send, a_recv, b_send, b_recv,
    a2_send, a2_recv, b2_send, b2_recv, sum_send, sum_recv,
):
    perts, planes, width = pots_ref.shape
    slabs = dens_ref.shape[0]
    y_hi, y_lo, z, core = place()
    pert, band = lax.axis_index("pert"), lax.axis_index("band")
    sibling = device(y_hi, y_lo, z, 1 - core)
    y_coords = [(1 - y_hi, y_lo), (1 - y_hi, 1 - y_lo), (y_hi, 1 - y_lo)]
    y_peers = [device(a, b, z, core) for a, b in y_coords]
    y_others = [device(a, b, z, 1 - core) for a, b in y_coords]
    z_coords = [lax.rem(z + d, 4) for d in range(1, 4)]
    z_peers = [device(y_hi, y_lo, c, core) for c in z_coords]
    p_peers = [{"pert": lax.rem(pert + d, perts)} for d in range(1, perts)]
    greet([sibling] + y_peers + y_others + z_peers + p_peers)

    pots_ref[pert] = pot_ref[:, pl.ds(pl.multiple_of(band * width, LANES), width)]
    pot_copies = []
    for i, peer in enumerate(p_peers):
        mine = pots_ref.at[pert]
        pot_copies.append(send(mine, mine, pot_send.at[i], pot_recv.at[i], peer))

    inv_x = transposed(tab_ref[...])
    lane = iota((N1, LANES), 1)
    half = 4 * PARTS

    def density_half(h):
        @pl.loop(0, 6)
        def _(group):
            for v in range(2):
                quad = h * 12 + group * 2 + v
                parts = []
                for u in range(4):
                    row = quad * 4 + u
                    field = dot(inv_x, turned_ref[row]).astype(BF16).astype(F32)
                    terms = psi_ref[row].astype(F32) * field
                    parts.append(step_ref[0:1] * terms[:, :LANES] + step_ref[1:2] * terms[:, LANES:])
                one, two, three = [pltpu.roll(parts[u], LANES - 32 * u, 1) for u in (1, 2, 3)]
                tiles = [
                    jnp.where(lane < 96, parts[0], one),
                    jnp.where(lane < 64, one, two),
                    jnp.where(lane < 32, two, three),
                ]
                for j, tile in enumerate(tiles):
                    for s in range(slabs):
                        dens_ref[s, quad * 3 + j] = tile[s * planes : (s + 1) * planes].astype(BF16)

    halves = [1 - y_hi, y_hi]
    core_copies = []
    for k, h in enumerate(halves):
        density_half(h)
        for l in range(2):
            src = dens_ref.at[l * 2 + 1 - core, pl.ds(h * half, half)]
            core_copies.append(
                send(src, from_core.at[k, l], core_send.at[k, l], core_recv.at[k, l], sibling)
            )

    a_copies, b_copies = [], []
    for k, h in enumerate(halves):
        wait_all(core_copies[2 * k : 2 * k + 2])
        for l in range(2):
            @pl.loop(0, 4)
            def _(c):
                for j in range(PARTS):
                    at = c * PARTS + j
                    total = dens_ref[l * 2 + core, h * half + at].astype(F32) + from_core[k, l, at].astype(F32)
                    if j < PART_A:
                        a_ref[k, l, c, j] = total.astype(BF16)
                    else:
                        b_ref[k, c, l, j - PART_A] = total.astype(BF16)
        targets = [(0, y_lo), (1, 1 - y_lo)] if k == 0 else [(2, 1 - y_lo)]
        for i, l in targets:
            a_copies.append(send(a_ref.at[k, l], a_from_y.at[i], a_send.at[i], a_recv.at[i], y_peers[i]))
        for i, c in enumerate(z_coords):
            b_copies.append(
                send(b_ref.at[k, c], b_from_z.at[k, i], b_send.at[k, i], b_recv.at[k, i], z_peers[i])
            )

    def total_of(pair):
        total = sum(pair(j) for j in range(PARTS))
        total = total[0:8] + total[8:16] + total[16:24]
        return jnp.sum(total, axis=0, keepdims=True)

    wait_all(pot_copies)

    def pot(p, j):
        return pots_ref[p, :, j * LANES : (j + 1) * LANES]

    pairs = [(p, q) for p in range(perts) for q in range(p + 1)]
    sums = [total_of(lambda j: pot(p, j) * pot(q, j)) for p, q in pairs]

    wait_all(a_copies)

    @pl.loop(0, 4)
    def _(c):
        for j in range(PART_A):
            total = a_ref[1, y_lo, c, j].astype(F32)
            for i in range(3):
                total = total + a_from_y[i, c, j].astype(F32)
            a_sum[c, j] = total.astype(BF16)

    copies = []
    for i, c in enumerate(z_coords):
        copies.append(send(a_sum.at[c], a_from_z.at[i], a2_send.at[i], a2_recv.at[i], z_peers[i]))
    wait_all(b_copies)
    for k in range(2):
        for l in range(2):
            for j in range(PART_B):
                total = b_ref[k, z, l, j].astype(F32)
                for i in range(3):
                    total = total + b_from_z[k, i, l, j].astype(F32)
                b_sum[k, l, j] = total.astype(BF16)
    for i, (k, l) in enumerate([(0, y_lo), (0, 1 - y_lo), (1, 1 - y_lo)]):
        copies.append(send(b_sum.at[k, l], b_from_y.at[i], b2_send.at[i], b2_recv.at[i], y_peers[i]))
    wait_all(copies)
    density = []
    for j in range(PARTS):
        if j < PART_A:
            total = a_sum[z, j].astype(F32)
            for i in range(3):
                total = total + a_from_z[i, j].astype(F32)
        else:
            total = b_sum[1, y_lo, j - PART_A].astype(F32)
            for i in range(3):
                total = total + b_from_y[i, j - PART_A].astype(F32)
        density.append(total)
    sums += [total_of(lambda j: pot(p, j) * density[j]) for p in range(perts)]
    sums += [jnp.zeros((1, LANES), F32)] * (16 - len(sums))
    sums_ref[0] = jnp.concatenate(sums, axis=0)

    at = 0
    for level, group in enumerate([[sibling] + y_peers + y_others, z_peers]):
        copies = []
        for i, peer in enumerate(group):
            k = at + i
            copies.append(send(sums_ref.at[level], from_sums.at[k], sum_send.at[k], sum_recv.at[k], peer))
        wait_all(copies)
        total = sums_ref[level]
        for i in range(len(group)):
            total = total + from_sums[at + i]
        sums_ref[level + 1] = total
        at += len(group)

    cells = 1.0 / (N1 * N2 * N3)
    totals = jnp.broadcast_to(jnp.sum(sums_ref[2], axis=1, keepdims=True) * cells, (16, LANES))
    gram = {pair: totals[k : k + 1] for k, pair in enumerate(pairs)}
    rhs = [totals[len(pairs) + p : len(pairs) + p + 1] for p in range(perts)]
    factor = {}
    for p in range(perts):
        for q in range(p + 1):
            value = gram[p, q]
            for k in range(q):
                value = value - factor[p, k] * factor[q, k]
            factor[p, q] = jnp.sqrt(value) if p == q else value / factor[q, q]
    coeffs = []
    for p in range(perts):
        value = rhs[p]
        for k in range(p):
            value = value - factor[p, k] * coeffs[k]
        coeffs.append(value / factor[p, p])
    for p in reversed(range(perts)):
        value = coeffs[p]
        for k in range(p + 1, perts):
            value = value - factor[k, p] * coeffs[k]
        coeffs[p] = value / factor[p, p]
    for j in range(PARTS):
        value = density[j]
        for p in range(perts):
            value = value - coeffs[p] * pot(p, j)
        out_ref[:, j * LANES : (j + 1) * LANES] = value
    projected_ref[...] = jnp.concatenate(rhs + rhs, axis=0)


def cost(flops, moved):
    return pl.CostEstimate(flops=int(flops), bytes_accessed=int(moved), transcendentals=0)


def params(collective=None):
    if collective is None:
        return pltpu.CompilerParams(vmem_limit_bytes=LIMIT)
    return pltpu.CompilerParams(vmem_limit_bytes=LIMIT, collective_id=collective, has_side_effects=True)


def shape(dims, kind):
    return jax.ShapeDtypeStruct(dims, kind)


def sems(*dims):
    return [pltpu.SemaphoreType.DMA(dims)] * 2


def start_of(coefs, wave_map, slabs):
    bands, npw = coefs.shape
    block = (slabs, bands // slabs, npw)
    return pl.pallas_call(
        start_kernel,
        out_shape=(shape((slabs, 8, npw + 2 * WIN), F32), shape((slabs, 1, LANES), jnp.int32)),
        in_specs=[VMEM] * 2,
        out_specs=(VMEM, VMEM),
        scratch_shapes=[
            pltpu.VMEM(block, BF16),
            pltpu.VMEM((1, npw + LANES), jnp.int32),
            pltpu.VMEM(block, BF16),
            pltpu.VMEM((slabs, 1, npw + LANES), jnp.int32),
        ]
        + sems(2, slabs - 1),
        compiler_params=params(1),
        name="start",
    )(coefs, wave_map.reshape(npw // LANES, LANES))


def zy_of(starts, data, tab):
    return pl.pallas_call(
        zy_kernel,
        out_shape=shape((N2, N1, 2 * LANES), BF16),
        in_specs=[SMEM] + [VMEM] * 2,
        out_specs=VMEM,
        scratch_shapes=[pltpu.VMEM((N1, 2 * N2, N3), BF16)],
        compiler_params=params(),
        cost_estimate=cost(2e10, 8e6),
        name="scatter_zy",
    )(starts, data, tab)


def dense_of(turned, pot, coefs, tab, slabs):
    bands, npw = coefs.shape
    return pl.pallas_call(
        dense_kernel,
        out_shape=(
            shape((N2, N1, 2 * LANES), BF16),
            shape((slabs, N1, 2 * N2 // slabs, N3), BF16),
            shape((2, 4, bands, npw // QUARTERS), BF16),
        ),
        in_specs=[VMEM] * 4,
        out_specs=(VMEM, VMEM, VMEM),
        scratch_shapes=[
            pltpu.VMEM((slabs,) + pot.shape, BF16),
            pltpu.VMEM((N1, N2, 2 * LANES), BF16),
        ]
        + sems(3)
        + sems(7),
        compiler_params=params(4),
        cost_estimate=cost(2e10, 8e6),
        name="dense",
    )(turned, pot, coefs, tab)


def gather_of(starts, data, wave, npw):
    slabs = data.shape[0]
    return pl.pallas_call(
        gather_kernel,
        out_shape=shape((slabs, QUARTERS, 2, npw // QUARTERS), BF16),
        in_specs=[SMEM] + [VMEM] * 2,
        out_specs=VMEM,
        scratch_shapes=[pltpu.VMEM((slabs, 2, data.shape[2]), F32)],
        compiler_params=params(),
        cost_estimate=cost(2e10, 8e6),
        name="gather",
    )(starts, data, wave)


def middle_of(waves, bands, index, energies):
    slabs, quarters, two, part = waves.shape
    block = pltpu.VMEM(waves.shape, BF16)
    peers = slabs * quarters - 1
    small = (slabs * quarters * two, bands.shape[0] * bands.shape[1] * bands.shape[2])
    return pl.pallas_call(
        middle_kernel,
        out_shape=(shape(index.shape, F32), shape((two, LANES), F32)),
        in_specs=[VMEM] * 3 + [SMEM],
        out_specs=(VMEM, VMEM),
        scratch_shapes=[
            block,
            pltpu.VMEM((peers,) + small, F32),
            block,
            block,
            pltpu.VMEM(small, F32),
        ]
        + sems(3, peers),
        compiler_params=params(2),
        name="middle",
    )(waves, bands, index, energies)


def end_of(turned, psi, step, pot, tab, slabs, perts):
    planes, cross = pot.shape
    width = cross // 8
    tile = (planes, LANES)
    return pl.pallas_call(
        end_kernel,
        out_shape=(shape((planes, width), F32), shape((8, LANES), F32)),
        in_specs=[VMEM] * 5,
        out_specs=(VMEM, VMEM),
        scratch_shapes=[
            pltpu.VMEM((slabs, 8 * PARTS) + tile, BF16),
            pltpu.VMEM((2, 2, 4 * PARTS) + tile, BF16),
            pltpu.VMEM((2, 2, 4, PART_A) + tile, BF16),
            pltpu.VMEM((2, 4, 2, PART_B) + tile, BF16),
            pltpu.VMEM((3, 4, PART_A) + tile, BF16),
            pltpu.VMEM((2, 3, 2, PART_B) + tile, BF16),
            pltpu.VMEM((4, PART_A) + tile, BF16),
            pltpu.VMEM((2, 2, PART_B) + tile, BF16),
            pltpu.VMEM((3, PART_A) + tile, BF16),
            pltpu.VMEM((3, PART_B) + tile, BF16),
            pltpu.VMEM((perts, planes, width), F32),
            pltpu.VMEM((3, 16, LANES), F32),
            pltpu.VMEM((10, 16, LANES), F32),
        ]
        + sems(2, 2)
        + sems(3)
        + sems(3)
        + sems(2, 3)
        + sems(3)
        + sems(3)
        + sems(10),
        compiler_params=params(3),
        name="density",
    )(turned, psi, step, pot, tab)


def per_device(wave_coeffs, band_energies, trial_potentials, wave_map):
    slabs = lax.axis_size("slab")
    me = lax.axis_index("slab")
    bands, npw = wave_coeffs.shape
    planes, cross = trial_potentials.shape[1:]
    tab = cosines(N1)
    pot = trial_potentials.reshape(planes, cross)
    energies = lax.dynamic_slice_in_dim(band_energies, me * (bands // slabs), bands // slabs, 0)
    data, starts = start_of(wave_coeffs, wave_map, slabs)
    turned = zy_of(starts, data, tab)
    psi, wave, all_bands = dense_of(turned, pot, wave_coeffs, tab, slabs)
    waves = gather_of(starts, data, wave, npw)
    data, step = middle_of(waves, all_bands, data, energies)
    turned = zy_of(starts, data, tab)
    residual, projected = end_of(turned, psi, step, pot, tab, slabs, lax.axis_size("pert"))
    return (residual.reshape(1, planes, -1), projected[: lax.axis_size("pert"), :1])


def solution(mesh):
    return jax.shard_map(
        per_device,
        mesh=mesh,
        in_specs=(P("band", "slab"), P("band"), P("pert", "slab", None), P("slab")),
        out_specs=(P("pert", "slab", "band"), P(None, "pert")),
        check_vma=False,
    )
```

```python
import jax
import jax.numpy as jnp
from jax import lax
from jax.experimental import pallas as pl
from jax.experimental.pallas import tpu as pltpu
from jax.sharding import PartitionSpec as P

N1 = 96
N2 = 96
N3 = 96
LANES = 128
WIN = 512
TILE = 2
TILES = N1 // TILE
QUARTERS = 4
F32 = jnp.float32
BF16 = jnp.bfloat16
NT = (((1,), (1,)), ((), ()))
MESH = pl.DeviceIdType.MESH


def cosines(n):
    rows = jnp.arange(n, dtype=jnp.int32).astype(jnp.float32)[:, None]
    cols = jnp.arange(n, dtype=jnp.int32).astype(jnp.float32)[None, :]
    table = jnp.sqrt(2.0 / n) * jnp.cos(jnp.pi * rows * (cols + 0.5) / n)
    table = table * jnp.where(rows == 0, jnp.sqrt(0.5), 1.0)
    return table.astype(jnp.bfloat16)


def dot(a, b):
    return jnp.dot(a, b, preferred_element_type=F32)


def dot_nt(a, b):
    return lax.dot_general(a, b, NT, preferred_element_type=F32)


def iota(dims, axis):
    return lax.broadcasted_iota(jnp.int32, dims, axis)


def ones_at(rows, cols):
    return (iota((rows, cols), 0) == iota((rows, cols), 1)).astype(F32).astype(BF16)


def transposed(table):
    return dot_nt(ones_at(table.shape[1], table.shape[1]), table).astype(BF16)


def window_base(starts_ref, s, tile):
    return pl.multiple_of((starts_ref[s, 0, tile] // LANES) * LANES, LANES)


def overflow(starts_ref, slabs):
    total = starts_ref[0, 0, TILES + 1]
    for s in range(1, slabs):
        total = total + starts_ref[s, 0, TILES + 1]
    return total > 0


def hot_rows(rows, tile, cells):
    at = rows[2:3] - (tile * cells).astype(F32)
    return iota((cells, WIN), 0).astype(F32) == at


def hot_z(rows):
    here = iota((N3, WIN), 0).astype(F32) == rows[3:4]
    return here.astype(F32).astype(BF16)


def scatter_window(data_ref, s, base, tile, cells):
    rows = data_ref[s, :, pl.ds(base, WIN)]
    hot = hot_rows(rows, tile, cells)
    both = [jnp.where(hot, rows[0:1], 0.0), jnp.where(hot, rows[1:2], 0.0)]
    return dot_nt(jnp.concatenate(both, axis=0).astype(BF16), hot_z(rows))


def plane_of(parts, t, ny):
    cells = TILE * ny
    rows = [p[b * cells + t * ny : b * cells + (t + 1) * ny] for b in range(2) for p in parts]
    return jnp.concatenate(rows, axis=0)


def scatter_planes(starts_ref, data_ref, plane_ref):
    slabs = data_ref.shape[0]
    ny = N2 // slabs
    cells = TILE * ny
    unroll = 4

    @pl.loop(0, TILES // unroll)
    def _(group):
        for u in range(unroll):
            tile = group * unroll + u
            parts = [
                scatter_window(data_ref, s, window_base(starts_ref, s, tile), tile, cells)
                for s in range(slabs)
            ]
            for t in range(TILE):
                plane_ref[tile * TILE + t] = plane_of(parts, t, ny).astype(BF16)

    @pl.when(overflow(starts_ref, slabs))
    def _():
        @pl.loop(0, TILES)
        def _(tile):
            parts = []
            for s in range(slabs):
                base = window_base(starts_ref, s, tile)

                def more(i, acc):
                    at = pl.multiple_of(base + i * WIN, LANES)
                    return acc + scatter_window(data_ref, s, at, tile, cells)

                windows = (starts_ref[s, 0, tile + 1] - base + WIN - 1) // WIN
                zero = jnp.zeros((2 * cells, N3), F32)
                parts.append(lax.fori_loop(1, windows, more, zero))
            for t in range(TILE):
                old = plane_ref[tile * TILE + t].astype(F32)
                plane_ref[tile * TILE + t] = (old + plane_of(parts, t, ny)).astype(BF16)


def zy_kernel(starts_ref, data_ref, tab_ref, turned_ref, plane_ref):
    scatter_planes(starts_ref, data_ref, plane_ref)
    inv_y = transposed(tab_ref[...])
    inv_z = dot(tab_ref[...], ones_at(N3, LANES)).astype(BF16)
    width = 16

    @pl.loop(0, N1 // width)
    def _(group):
        first = pl.multiple_of(group * width, width)
        flat = plane_ref[pl.ds(first, width)].reshape(width * 2 * N2, N3)
        z_done = dot(flat, inv_z).astype(BF16)
        done = []
        for u in range(width):
            one = z_done[2 * N2 * u : 2 * N2 * u + N2]
            two = z_done[2 * N2 * u + N2 : 2 * N2 * (u + 1)]
            done.append(dot(inv_y, jnp.concatenate([one, two], axis=1)).astype(BF16))
        turned_ref[:, pl.ds(first, width), :] = jnp.swapaxes(jnp.stack(done, axis=0), 0, 1)


def gather_window(data_ref, wave_ref, sum_ref, s, base, tile, ny):
    cells = TILE * ny
    at = pl.ds(base, WIN)
    rows = data_ref[s, :, at]
    hot = hot_rows(rows, tile, cells)
    mine = wave_ref[s, pl.ds(tile * TILE, TILE)].reshape(TILE * 2 * ny, N3)
    picked = dot(mine, hot_z(rows))
    found = []
    for b in range(2):
        part = jnp.concatenate(
            [picked[(2 * t + b) * ny : (2 * t + b + 1) * ny] for t in range(TILE)], axis=0
        )
        found.append(jnp.sum(jnp.where(hot, part, 0.0), axis=0, keepdims=True))
    sum_ref[s, :, at] += jnp.concatenate(found, axis=0)


def gather_kernel(starts_ref, data_ref, wave_ref, out_ref, sum_ref):
    slabs = data_ref.shape[0]
    ny = N2 // slabs
    sum_ref[...] = jnp.zeros_like(sum_ref)
    several = 4

    @pl.loop(0, TILES // several)
    def _(group):
        for u in range(several):
            tile = group * several + u
            for s in range(slabs):
                gather_window(data_ref, wave_ref, sum_ref, s, window_base(starts_ref, s, tile), tile, ny)

    @pl.when(overflow(starts_ref, slabs))
    def _():
        @pl.loop(0, TILES)
        def _(tile):
            for s in range(slabs):
                base = window_base(starts_ref, s, tile)

                @pl.loop(1, (starts_ref[s, 0, tile + 1] - base + WIN - 1) // WIN)
                def _(i):
                    at = pl.multiple_of(base + i * WIN, LANES)
                    gather_window(data_ref, wave_ref, sum_ref, s, at, tile, ny)

    part = out_ref.shape[3]
    for q in range(out_ref.shape[1]):
        out_ref[:, q] = sum_ref[:, :, q * part : (q + 1) * part].astype(out_ref.dtype)


SMEM = pl.BlockSpec(memory_space=pltpu.SMEM)
VMEM = pl.BlockSpec(memory_space=pltpu.VMEM)
HBM = pl.BlockSpec(memory_space=pltpu.HBM)
LIMIT = 32 * 1024 * 1024


def greet(peers):
    barrier = pltpu.get_barrier_semaphore()
    for peer in peers:
        pl.semaphore_signal(barrier, inc=1, device_id=peer, device_id_type=MESH)
    pl.semaphore_wait(barrier, len(peers))


def remote(src, dst, send_sem, recv_sem, peer):
    return pltpu.make_async_remote_copy(
        src_ref=src, dst_ref=dst, send_sem=send_sem, recv_sem=recv_sem, device_id=peer, device_id_type=MESH
    )


def send(src, dst, send_sem, recv_sem, peer):
    copy = remote(src, dst, send_sem, recv_sem, peer)
    copy.start()
    return copy


def wait_all(copies):
    for copy in copies:
        copy.wait()


def slab_peers(slabs):
    me = lax.axis_index("slab")
    return [lax.rem(me + d, slabs) for d in range(1, slabs)]


def place():
    band, slab = lax.axis_index("band"), lax.axis_index("slab")
    return band // 4, slab // 2, lax.rem(band, 4), lax.rem(slab, 2)


def device(y_hi, y_lo, z, core):
    return {"band": y_hi * 4 + z, "slab": y_lo * 2 + core}


def start_kernel(
    coef_ref, map_ref, data_ref, starts_ref, own_coef, own_map, coefs_ref, maps_ref, send_sem, recv_sem
):
    slabs, two, npw = coefs_ref.shape
    ny = N2 // slabs
    me = lax.axis_index("slab")
    peers = slab_peers(slabs)
    chunk = 1536
    for r in range(npw // LANES):
        own_map[0:1, r * LANES : (r + 1) * LANES] = map_ref[r : r + 1, :]
    for i in range(npw // chunk):
        at = pl.ds(i * chunk, chunk)
        block = coef_ref[:, at].astype(F32)
        for t in range(slabs):
            own_coef[t, :, at] = block[two * t : two * (t + 1)].astype(BF16)
    greet([{"slab": peer} for peer in peers])
    coef_copies = []
    for i, peer in enumerate(peers):
        to = {"slab": peer}
        coef_copies.append(send(own_coef.at[peer], coefs_ref.at[me], send_sem.at[0, i], recv_sem.at[0, i], to))
    coefs_ref[me] = own_coef[me]
    edges = iota((56, LANES), 0) * (TILE * ny * N3)
    below = jnp.zeros((56, LANES), jnp.int32)
    for r in range(npw // LANES):
        below = below + (own_map[0:1, r * LANES : (r + 1) * LANES] < edges).astype(jnp.int32)
    count = jnp.sum(below.astype(F32), axis=1, keepdims=True)
    spread = jnp.where(iota((56, LANES), 0) == iota((56, LANES), 1), count, 0.0)
    starts = jnp.sum(spread, axis=0, keepdims=True).astype(jnp.int32)
    after = pltpu.roll(starts, LANES - 1, 1)
    lane = iota((1, LANES), 1)
    over = (after > jnp.bitwise_and(starts, -LANES) + WIN) & (lane < TILES)
    flag = jnp.max(over.astype(F32), axis=1, keepdims=True).astype(jnp.int32)
    own_map[0:1, npw : npw + LANES] = jnp.where(lane == TILES + 1, flag, starts)
    copies = []
    for i, peer in enumerate(peers):
        to = {"slab": peer}
        copies.append(send(own_map, maps_ref.at[me], send_sem.at[1, i], recv_sem.at[1, i], to))
    maps_ref[me] = own_map[...]
    data_ref[...] = jnp.full(data_ref.shape, -1.0, F32)
    wait_all(copies)
    for s in range(slabs):
        starts_ref[s] = maps_ref[s, :, npw : npw + LANES]
    y_first = (iota((slabs, 1), 0) * ny).astype(F32)
    for i in range(npw // chunk):
        at = pl.ds(i * chunk, chunk)
        cell = jnp.concatenate([maps_ref[s, :, at] for s in range(slabs)], axis=0).astype(F32)
        row = jnp.floor((cell + 0.5) * (1.0 / N3))
        zpos = cell - row * N3
        xpos = jnp.floor((row + 0.5) * (1.0 / ny))
        ypos = row - xpos * ny + y_first
        kin = 2.0 * (xpos * xpos / (N1 * N1) + ypos * ypos / (N2 * N2) + zpos * zpos / (N3 * N3))
        for s in range(slabs):
            lines = [part[s : s + 1] for part in (row, zpos, kin)]
            data_ref[s, 2:5, at] = jnp.concatenate(lines, axis=0)
    wait_all(coef_copies)
    for s in range(slabs):
        for i in range(npw // chunk):
            at = pl.ds(i * chunk, chunk)
            data_ref[s, 0:2, at] = coefs_ref[s, :, at].astype(F32)


def dense_kernel(
    turned_ref, pot_ref, coef_ref, tab_ref, psi_out, wave_ref, bands_ref,
    psi_ref, pots_ref, back_ref, send_sem, recv_sem, coef_send, coef_recv, psi_sem,
):
    slabs = wave_ref.shape[0]
    ny = N2 // slabs
    y_hi, y_lo, z, core = place()
    me = lax.axis_index("slab")
    y = y_hi * 2 + y_lo
    sibling = device(y_hi, y_lo, z, 1 - core)

    def around(step):
        to = lax.rem(y + step + 4, 4)
        return device(to // 2, lax.rem(to, 2), z, core)

    for i in range(3):
        at = pl.ds(i * 3072, 3072)
        pots_ref[me, :, at] = pot_ref[:, at].astype(BF16)
    steps = [(a, b) for a in range(2) for b in range(4) if a + b > 0]
    others = [(lax.rem(y_hi + a, 2), lax.rem(z + b, 4)) for a, b in steps]
    members = [device(a, y_lo, b, core) for a, b in others]
    greet([sibling, around(-1), around(1)] + members)
    mine = pots_ref.at[me]
    to_far = send(mine, mine, send_sem.at[0], recv_sem.at[0], around(2 * core - 1))
    to_near = send(mine, mine, send_sem.at[1], recv_sem.at[1], sibling)

    inv_x = transposed(tab_ref[...])
    unroll = 8

    def psi_rows(first, last):
        @pl.loop(first, last)
        def _(group):
            for u in range(unroll):
                row = group * unroll + u
                psi_ref[row] = dot(inv_x, turned_ref[row]).astype(BF16)

    groups = N2 // unroll
    psi_rows(0, groups - 3)
    to_far.wait_send()
    slot = pots_ref.at[(1 - y_lo) * 2 + core]
    remote(slot, slot, send_sem.at[0], recv_sem.at[0], sibling).wait_recv()
    passed = send(slot, slot, send_sem.at[2], recv_sem.at[2], sibling)
    part = bands_ref.shape[3]
    quarter = pl.ds(pl.multiple_of(lax.axis_index("pert") * part, LANES), part)
    bands_ref[y_hi, z] = coef_ref[:, quarter]
    copies = []
    for i, member in enumerate(members):
        src = coef_ref.at[:, quarter]
        copies.append(send(src, bands_ref.at[y_hi, z], coef_send.at[i], coef_recv.at[i], member))
    psi_rows(groups - 3, groups)
    store = pltpu.make_async_copy(psi_ref, psi_out, psi_sem)
    store.start()
    to_near.wait()
    passed.wait_send()
    slot = pots_ref.at[(1 - y_lo) * 2 + 1 - core]
    remote(slot, slot, send_sem.at[2], recv_sem.at[2], sibling).wait_recv()

    width = 16
    lane = iota((N1 // slabs, LANES), 1)

    @pl.loop(0, N2 // width)
    def _(group):
        first = pl.multiple_of(group * width, width)
        done = []
        for v in range(width // 4):
            quads = [[], [], [], []]
            for s in range(slabs):
                parts = []
                for j in range(3):
                    off = pl.multiple_of(group * (width * N3) + (3 * v + j) * LANES, LANES)
                    parts.append(pots_ref[s, :, pl.ds(off, LANES)].astype(F32))
                a, b, c = parts
                quads[0].append(a)
                quads[1].append(jnp.where(lane < 32, pltpu.roll(a, 32, 1), pltpu.roll(b, 32, 1)))
                quads[2].append(jnp.where(lane < 64, pltpu.roll(b, 64, 1), pltpu.roll(c, 64, 1)))
                quads[3].append(pltpu.roll(c, 96, 1))
            for u in range(4):
                pot = jnp.concatenate(quads[u], axis=0)
                psi = psi_ref[first + 4 * v + u].astype(F32)
                product = jnp.concatenate([pot * psi[:, :LANES], pot * psi[:, LANES:]], axis=1)
                done.append(dot(tab_ref[...], product.astype(BF16)).astype(BF16))
        back_ref[:, pl.ds(first, width), :] = jnp.swapaxes(jnp.stack(done, axis=0), 0, 1)

    fwd_z = dot_nt(ones_at(LANES, N3), tab_ref[...]).astype(BF16)

    @pl.loop(0, N1 // unroll)
    def _(group):
        done = []
        for u in range(unroll):
            y_done = dot(tab_ref[...], back_ref[group * unroll + u]).astype(BF16)
            done += [y_done[:, :LANES], y_done[:, LANES:]]
        waves = dot(jnp.concatenate(done, axis=0), fwd_z)
        for u in range(unroll):
            for s in range(slabs):
                one = waves[2 * u * N2 + s * ny : 2 * u * N2 + (s + 1) * ny]
                two = waves[(2 * u + 1) * N2 + s * ny : (2 * u + 1) * N2 + (s + 1) * ny]
                wave_ref[s, group * unroll + u] = jnp.concatenate([one, two], axis=0).astype(BF16)

    store.wait()
    wait_all(copies)


def middle_kernel(
    waves_ref, bands_ref, index_ref, energy_ref, data_ref, step_ref,
    got_ref, corr_ref, rhs_ref, back_ref, total_ref, send_sem, recv_sem,
):
    slabs, quarters, two, part = waves_ref.shape
    half, zs, bands, _ = bands_ref.shape
    chunk = 1152
    pert, slab = lax.axis_index("pert"), lax.axis_index("slab")
    steps = [(a, b) for a in range(quarters) for b in range(slabs) if a + b > 0]
    others = [(lax.rem(pert + a, quarters), lax.rem(slab + b, slabs)) for a, b in steps]
    peers = [{"pert": c, "slab": t} for c, t in others]
    greet(peers)
    copies = []
    for i, (c, t) in enumerate(others):
        src, dst = waves_ref.at[t, c], got_ref.at[pert, slab]
        copies.append(send(src, dst, send_sem.at[0, i], recv_sem.at[0, i], peers[i]))
    got_ref[pert, slab] = waves_ref[slab, pert]
    data_ref[...] = index_ref[...]
    wait_all(copies)

    def waves_at(at):
        parts = [got_ref[c, t, :, at].astype(F32) for c in range(quarters) for t in range(slabs)]
        return jnp.concatenate(parts, axis=0)

    def bands_at(at):
        parts = [bands_ref[a, c, :, at].astype(F32) for a in range(half) for c in range(zs)]
        return jnp.concatenate(parts, axis=0).astype(BF16)

    rows, count = quarters * slabs * two, half * zs * bands
    total = jnp.zeros((rows, count), F32)
    for i in range(part // chunk):
        at = pl.ds(i * chunk, chunk)
        total = total + dot_nt(waves_at(at).astype(BF16), bands_at(at))
    total_ref[...] = jnp.concatenate([total[: rows // 2], total[rows // 2 :]], axis=1)

    copies = []
    for i, peer in enumerate(peers):
        copies.append(send(total_ref, corr_ref.at[i], send_sem.at[1, i], recv_sem.at[1, i], peer))
    wait_all(copies)
    total = total_ref[...]
    for i in range(len(peers)):
        total = total + corr_ref[i]
    correlation = jnp.concatenate([total[:, :count], total[:, count:]], axis=0).astype(BF16)

    overlap = jnp.zeros((rows, rows), F32)
    for i in range(part // chunk):
        at = pl.ds(i * chunk, chunk)
        waves = waves_at(at)
        rhs = (waves - dot(correlation, bands_at(at))).astype(BF16)
        overlap = overlap + dot_nt(rhs, waves.astype(BF16))
        rhs = rhs.astype(F32)
        for c in range(quarters):
            for t in range(slabs):
                first = two * (c * slabs + t)
                rhs_ref[c, t, :, at] = rhs[first : first + two].astype(BF16)
    own = rows // quarters
    same = lax.rem(iota((rows, rows), 0), own) == lax.rem(iota((rows, rows), 1), own)
    kept = jnp.where(same, overlap, 0.0)
    lane = iota((rows, LANES), 1)
    tail = jnp.zeros((rows, LANES), F32)
    for p in range(quarters):
        mine = jnp.sum(kept[:, p * own : (p + 1) * own], axis=1, keepdims=True)
        high = mine.astype(BF16).astype(F32)
        tail = jnp.where(lane == p, high, tail)
        tail = jnp.where(lane == quarters + p, mine - high, tail)
    for c in range(quarters):
        for t in range(slabs):
            first = two * (c * slabs + t)
            rhs_ref[c, t, :, part:] = tail[first : first + two].astype(BF16)

    copies = []
    for i, (c, t) in enumerate(others):
        src, dst = rhs_ref.at[c, t], back_ref.at[slab, pert]
        copies.append(send(src, dst, send_sem.at[2, i], recv_sem.at[2, i], peers[i]))
    back_ref[slab, pert] = rhs_ref[pert, slab]
    wait_all(copies)

    numer = jnp.zeros((two, chunk), F32)
    denom = jnp.zeros((two, chunk), F32)
    tail = jnp.zeros((two, LANES), F32)
    energy = jnp.concatenate([jnp.full((1, chunk), energy_ref[b], F32) for b in range(two)], axis=0)
    for s in range(slabs):
        for q in range(quarters):
            tail = tail + back_ref[s, q, :, part:].astype(F32)
            for i in range(part // chunk):
                at = pl.ds(q * part + i * chunk, chunk)
                mine = back_ref[s, q, :, i * chunk : (i + 1) * chunk].astype(F32)
                data_ref[s, 0:2, at] = mine
                squares = mine * mine
                numer = numer + squares
                denom = denom + (index_ref[s, 4:5, at] - energy) * squares
    step = -jnp.sum(numer, axis=1, keepdims=True) / jnp.sum(denom, axis=1, keepdims=True)
    step = step * (4.0 * N1 * N2 * N3 / count)
    tail = step * (tail + pltpu.roll(tail, LANES - quarters, 1))
    tail = jnp.sum(tail, axis=0, keepdims=True)
    wide = jnp.broadcast_to(step, (two, LANES))
    step_ref[...] = jnp.concatenate([wide, tail, jnp.zeros((8 - two - 1, LANES), F32)], axis=0)


PART_A = 5
PART_B = 4
PARTS = PART_A + PART_B


def end_kernel(
    turned_ref, psi_ref, step_ref, pot_ref, tab_ref, out_ref, projected_ref,
    dens_ref, from_core, a_ref, b_ref, a_from_y, b_from_z, a_sum, b_sum, a_from_z, b_from_y,
    pots_ref, sums_ref, from_sums, core_send, core_recv, pot_send, pot_recv, a_send, a_recv, b_send, b_recv,
    a2_send, a2_recv, b2_send, b2_recv, sum_send, sum_recv,
):
    perts, planes, width = pots_ref.shape
    slabs = dens_ref.shape[0]
    y_hi, y_lo, z, core = place()
    pert, band = lax.axis_index("pert"), lax.axis_index("band")
    sibling = device(y_hi, y_lo, z, 1 - core)
    y_coords = [(1 - y_hi, y_lo), (1 - y_hi, 1 - y_lo), (y_hi, 1 - y_lo)]
    y_peers = [device(a, b, z, core) for a, b in y_coords]
    y_others = [device(a, b, z, 1 - core) for a, b in y_coords]
    z_coords = [lax.rem(z + d, 4) for d in range(1, 4)]
    z_peers = [device(y_hi, y_lo, c, core) for c in z_coords]
    p_peers = [{"pert": lax.rem(pert + d, perts)} for d in range(1, perts)]
    greet([sibling] + y_peers + y_others + z_peers + p_peers)

    pots_ref[pert] = pot_ref[:, pl.ds(pl.multiple_of(band * width, LANES), width)]
    pot_copies = []
    for i, peer in enumerate(p_peers):
        mine = pots_ref.at[pert]
        pot_copies.append(send(mine, mine, pot_send.at[i], pot_recv.at[i], peer))

    inv_x = transposed(tab_ref[...])
    lane = iota((N1, LANES), 1)
    half = 4 * PARTS

    def density_part(h, first, last):
        @pl.loop(first, last)
        def _(group):
            for v in range(2):
                quad = h * 12 + group * 2 + v
                parts = []
                for u in range(4):
                    row = quad * 4 + u
                    field = dot(inv_x, turned_ref[row]).astype(BF16).astype(F32)
                    terms = psi_ref[row].astype(F32) * field
                    parts.append(step_ref[0:1] * terms[:, :LANES] + step_ref[1:2] * terms[:, LANES:])
                one, two, three = [pltpu.roll(parts[u], LANES - 32 * u, 1) for u in (1, 2, 3)]
                tiles = [
                    jnp.where(lane < 96, parts[0], one),
                    jnp.where(lane < 64, one, two),
                    jnp.where(lane < 32, two, three),
                ]
                for j, tile in enumerate(tiles):
                    for s in range(slabs):
                        dens_ref[s, quad * 3 + j] = tile[s * planes : (s + 1) * planes].astype(BF16)

    halves = [1 - y_hi, y_hi]
    core_copies, a_copies, b_copies = [], [], []

    def to_sibling(k):
        h = halves[k]
        for l in range(2):
            src = dens_ref.at[l * 2 + 1 - core, pl.ds(h * half, half)]
            core_copies.append(
                send(src, from_core.at[k, l], core_send.at[k, l], core_recv.at[k, l], sibling)
            )

    def to_others(k):
        h = halves[k]
        wait_all(core_copies[2 * k : 2 * k + 2])
        for l in range(2):
            @pl.loop(0, 4)
            def _(c):
                for j in range(PARTS):
                    at = c * PARTS + j
                    total = dens_ref[l * 2 + core, h * half + at].astype(F32) + from_core[k, l, at].astype(F32)
                    if j < PART_A:
                        a_ref[k, l, c, j] = total.astype(BF16)
                    else:
                        b_ref[k, c, l, j - PART_A] = total.astype(BF16)
        targets = [(0, y_lo), (1, 1 - y_lo)] if k == 0 else [(2, 1 - y_lo)]
        for i, l in targets:
            a_copies.append(send(a_ref.at[k, l], a_from_y.at[i], a_send.at[i], a_recv.at[i], y_peers[i]))
        for i, c in enumerate(z_coords):
            b_copies.append(
                send(b_ref.at[k, c], b_from_z.at[k, i], b_send.at[k, i], b_recv.at[k, i], z_peers[i])
            )

    density_part(halves[0], 0, 6)
    to_sibling(0)
    density_part(halves[1], 0, 3)
    to_others(0)
    density_part(halves[1], 3, 6)
    to_sibling(1)

    def total_of(pair):
        total = sum(pair(j) for j in range(PARTS))
        total = total[0:8] + total[8:16] + total[16:24]
        return jnp.sum(total, axis=0, keepdims=True)

    def pot(p, j):
        return pots_ref[p, :, j * LANES : (j + 1) * LANES]

    wait_all(pot_copies)
    pairs = [(p, q) for p in range(perts) for q in range(p + 1)]
    sums = [total_of(lambda j: pot(p, j) * pot(q, j)) for p, q in pairs]
    line = iota((1, LANES), 1)
    sums += [jnp.where(line == p, step_ref[2:3], 0.0) for p in range(perts)]
    sums += [jnp.zeros((1, LANES), F32)] * (16 - len(sums))
    sums_ref[0] = jnp.concatenate(sums, axis=0)
    to_others(1)

    def sum_sends(level, first, group):
        copies = []
        for i, peer in enumerate(group):
            k = first + i
            copies.append(send(sums_ref.at[level], from_sums.at[k], sum_send.at[k], sum_recv.at[k], peer))
        return copies

    def sum_up(level, first, copies):
        wait_all(copies)
        total = sums_ref[level]
        for i in range(len(copies)):
            total = total + from_sums[first + i]
        sums_ref[level + 1] = total

    near = [sibling] + y_peers + y_others
    near_copies = sum_sends(0, 0, near)

    wait_all(a_copies)

    @pl.loop(0, 4)
    def _(c):
        for j in range(PART_A):
            total = a_ref[1, y_lo, c, j].astype(F32)
            for i in range(3):
                total = total + a_from_y[i, c, j].astype(F32)
            a_sum[c, j] = total.astype(BF16)

    copies = []
    for i, c in enumerate(z_coords):
        copies.append(send(a_sum.at[c], a_from_z.at[i], a2_send.at[i], a2_recv.at[i], z_peers[i]))
    wait_all(b_copies)
    for k in range(2):
        for l in range(2):
            for j in range(PART_B):
                total = b_ref[k, z, l, j].astype(F32)
                for i in range(3):
                    total = total + b_from_z[k, i, l, j].astype(F32)
                b_sum[k, l, j] = total.astype(BF16)
    for i, (k, l) in enumerate([(0, y_lo), (0, 1 - y_lo), (1, 1 - y_lo)]):
        copies.append(send(b_sum.at[k, l], b_from_y.at[i], b2_send.at[i], b2_recv.at[i], y_peers[i]))
    sum_up(0, 0, near_copies)
    far_copies = sum_sends(1, len(near), z_peers)
    wait_all(copies)
    density = []
    for j in range(PARTS):
        if j < PART_A:
            total = a_sum[z, j].astype(F32)
            for i in range(3):
                total = total + a_from_z[i, j].astype(F32)
        else:
            total = b_sum[1, y_lo, j - PART_A].astype(F32)
            for i in range(3):
                total = total + b_from_y[i, j - PART_A].astype(F32)
        density.append(total)
    sum_up(1, len(near), far_copies)

    cells = 1.0 / (N1 * N2 * N3)
    totals = jnp.broadcast_to(jnp.sum(sums_ref[2], axis=1, keepdims=True) * cells, (16, LANES))
    gram = {pair: totals[k : k + 1] for k, pair in enumerate(pairs)}
    rhs = [totals[len(pairs) + p : len(pairs) + p + 1] for p in range(perts)]
    factor = {}
    for p in range(perts):
        for q in range(p + 1):
            value = gram[p, q]
            for k in range(q):
                value = value - factor[p, k] * factor[q, k]
            factor[p, q] = jnp.sqrt(value) if p == q else value / factor[q, q]
    coeffs = []
    for p in range(perts):
        value = rhs[p]
        for k in range(p):
            value = value - factor[p, k] * coeffs[k]
        coeffs.append(value / factor[p, p])
    for p in reversed(range(perts)):
        value = coeffs[p]
        for k in range(p + 1, perts):
            value = value - factor[k, p] * coeffs[k]
        coeffs[p] = value / factor[p, p]
    for j in range(PARTS):
        value = density[j]
        for p in range(perts):
            value = value - coeffs[p] * pot(p, j)
        out_ref[:, j * LANES : (j + 1) * LANES] = value
    projected_ref[...] = jnp.concatenate(rhs + rhs, axis=0)


def cost(flops, moved):
    return pl.CostEstimate(flops=int(flops), bytes_accessed=int(moved), transcendentals=0)


def params(collective=None):
    if collective is None:
        return pltpu.CompilerParams(vmem_limit_bytes=LIMIT)
    return pltpu.CompilerParams(vmem_limit_bytes=LIMIT, collective_id=collective, has_side_effects=True)


def shape(dims, kind):
    return jax.ShapeDtypeStruct(dims, kind)


def sems(*dims):
    return [pltpu.SemaphoreType.DMA(dims)] * 2


def start_of(coefs, wave_map, slabs):
    bands, npw = coefs.shape
    block = (slabs, bands // slabs, npw)
    return pl.pallas_call(
        start_kernel,
        out_shape=(shape((slabs, 8, npw + 2 * WIN), F32), shape((slabs, 1, LANES), jnp.int32)),
        in_specs=[VMEM] * 2,
        out_specs=(VMEM, VMEM),
        scratch_shapes=[
            pltpu.VMEM(block, BF16),
            pltpu.VMEM((1, npw + LANES), jnp.int32),
            pltpu.VMEM(block, BF16),
            pltpu.VMEM((slabs, 1, npw + LANES), jnp.int32),
        ]
        + sems(2, slabs - 1),
        compiler_params=params(1),
        name="start",
    )(coefs, wave_map.reshape(npw // LANES, LANES))


def zy_of(starts, data, tab):
    return pl.pallas_call(
        zy_kernel,
        out_shape=shape((N2, N1, 2 * LANES), BF16),
        in_specs=[SMEM] + [VMEM] * 2,
        out_specs=VMEM,
        scratch_shapes=[pltpu.VMEM((N1, 2 * N2, N3), BF16)],
        compiler_params=params(),
        cost_estimate=cost(2e10, 8e6),
        name="scatter_zy",
    )(starts, data, tab)


def dense_of(turned, pot, coefs, tab, slabs):
    bands, npw = coefs.shape
    return pl.pallas_call(
        dense_kernel,
        out_shape=(
            shape((N2, N1, 2 * LANES), BF16),
            shape((slabs, N1, 2 * N2 // slabs, N3), BF16),
            shape((2, 4, bands, npw // QUARTERS), BF16),
        ),
        in_specs=[VMEM] * 4,
        out_specs=(HBM, VMEM, VMEM),
        scratch_shapes=[
            pltpu.VMEM((N2, N1, 2 * LANES), BF16),
            pltpu.VMEM((slabs,) + pot.shape, BF16),
            pltpu.VMEM((N1, N2, 2 * LANES), BF16),
        ]
        + sems(3)
        + sems(7)
        + [pltpu.SemaphoreType.DMA(())],
        compiler_params=params(4),
        cost_estimate=cost(2e10, 8e6),
        name="dense",
    )(turned, pot, coefs, tab)


def gather_of(starts, data, wave, npw):
    slabs = data.shape[0]
    return pl.pallas_call(
        gather_kernel,
        out_shape=shape((slabs, QUARTERS, 2, npw // QUARTERS), BF16),
        in_specs=[SMEM] + [VMEM] * 2,
        out_specs=VMEM,
        scratch_shapes=[pltpu.VMEM((slabs, 2, data.shape[2]), F32)],
        compiler_params=params(),
        cost_estimate=cost(2e10, 8e6),
        name="gather",
    )(starts, data, wave)


def middle_of(waves, bands, index, energies):
    slabs, quarters, two, part = waves.shape
    peers = slabs * quarters - 1
    small = (slabs * quarters * two // 2, LANES)
    longer = pltpu.VMEM((slabs, quarters, two, part + LANES), BF16)
    return pl.pallas_call(
        middle_kernel,
        out_shape=(shape(index.shape, F32), shape((8, LANES), F32)),
        in_specs=[VMEM] * 3 + [SMEM],
        out_specs=(VMEM, VMEM),
        scratch_shapes=[
            pltpu.VMEM(waves.shape, BF16),
            pltpu.VMEM((peers,) + small, F32),
            longer,
            longer,
            pltpu.VMEM(small, F32),
        ]
        + sems(3, peers),
        compiler_params=params(2),
        name="middle",
    )(waves, bands, index, energies)


def end_of(turned, psi, step, pot, tab, slabs, perts):
    planes, cross = pot.shape
    width = cross // 8
    tile = (planes, LANES)
    return pl.pallas_call(
        end_kernel,
        out_shape=(shape((planes, width), F32), shape((8, LANES), F32)),
        in_specs=[VMEM] * 5,
        out_specs=(VMEM, VMEM),
        scratch_shapes=[
            pltpu.VMEM((slabs, 8 * PARTS) + tile, BF16),
            pltpu.VMEM((2, 2, 4 * PARTS) + tile, BF16),
            pltpu.VMEM((2, 2, 4, PART_A) + tile, BF16),
            pltpu.VMEM((2, 4, 2, PART_B) + tile, BF16),
            pltpu.VMEM((3, 4, PART_A) + tile, BF16),
            pltpu.VMEM((2, 3, 2, PART_B) + tile, BF16),
            pltpu.VMEM((4, PART_A) + tile, BF16),
            pltpu.VMEM((2, 2, PART_B) + tile, BF16),
            pltpu.VMEM((3, PART_A) + tile, BF16),
            pltpu.VMEM((3, PART_B) + tile, BF16),
            pltpu.VMEM((perts, planes, width), F32),
            pltpu.VMEM((3, 16, LANES), F32),
            pltpu.VMEM((10, 16, LANES), F32),
        ]
        + sems(2, 2)
        + sems(3)
        + sems(3)
        + sems(2, 3)
        + sems(3)
        + sems(3)
        + sems(10),
        compiler_params=params(3),
        name="density",
    )(turned, psi, step, pot, tab)


def per_device(wave_coeffs, band_energies, trial_potentials, wave_map):
    slabs = lax.axis_size("slab")
    me = lax.axis_index("slab")
    bands, npw = wave_coeffs.shape
    planes, cross = trial_potentials.shape[1:]
    tab = cosines(N1)
    pot = trial_potentials.reshape(planes, cross)
    energies = lax.dynamic_slice_in_dim(band_energies, me * (bands // slabs), bands // slabs, 0)
    data, starts = start_of(wave_coeffs, wave_map, slabs)
    turned = zy_of(starts, data, tab)
    psi, wave, all_bands = dense_of(turned, pot, wave_coeffs, tab, slabs)
    waves = gather_of(starts, data, wave, npw)
    data, step = middle_of(waves, all_bands, data, energies)
    turned = zy_of(starts, data, tab)
    residual, projected = end_of(turned, psi, step, pot, tab, slabs, lax.axis_size("pert"))
    return (residual.reshape(1, planes, -1), projected[: lax.axis_size("pert"), :1])


def solution(mesh):
    return jax.shard_map(
        per_device,
        mesh=mesh,
        in_specs=(P("band", "slab"), P("band"), P("pert", "slab", None), P("slab")),
        out_specs=(P("pert", "slab", "band"), P(None, "pert")),
        check_vma=False,
    )
```

```python
import jax
import jax.numpy as jnp
from jax import lax
from jax.experimental import pallas as pl
from jax.experimental.pallas import tpu as pltpu
from jax.sharding import PartitionSpec as P

N1 = 96
N2 = 96
N3 = 96
LANES = 128
WIN = 512
TILE = 2
TILES = N1 // TILE
QUARTERS = 4
F32 = jnp.float32
BF16 = jnp.bfloat16
NT = (((1,), (1,)), ((), ()))
MESH = pl.DeviceIdType.MESH


def cosines(n):
    rows = jnp.arange(n, dtype=jnp.int32).astype(jnp.float32)[:, None]
    cols = jnp.arange(n, dtype=jnp.int32).astype(jnp.float32)[None, :]
    table = jnp.sqrt(2.0 / n) * jnp.cos(jnp.pi * rows * (cols + 0.5) / n)
    table = table * jnp.where(rows == 0, jnp.sqrt(0.5), 1.0)
    return table.astype(jnp.bfloat16)


def dot(a, b):
    return jnp.dot(a, b, preferred_element_type=F32)


def dot_nt(a, b):
    return lax.dot_general(a, b, NT, preferred_element_type=F32)


def iota(dims, axis):
    return lax.broadcasted_iota(jnp.int32, dims, axis)


def ones_at(rows, cols):
    return (iota((rows, cols), 0) == iota((rows, cols), 1)).astype(F32).astype(BF16)


def transposed(table):
    return dot_nt(ones_at(table.shape[1], table.shape[1]), table).astype(BF16)


def window_base(starts_ref, s, tile):
    return pl.multiple_of((starts_ref[s, 0, tile] // LANES) * LANES, LANES)


def overflow(starts_ref, slabs):
    total = starts_ref[0, 0, TILES + 1]
    for s in range(1, slabs):
        total = total + starts_ref[s, 0, TILES + 1]
    return total > 0


def hot_rows(rows, tile, cells):
    at = rows[2:3] - (tile * cells).astype(F32)
    return iota((cells, WIN), 0).astype(F32) == at


def hot_z(rows):
    here = iota((N3, WIN), 0).astype(F32) == rows[3:4]
    return here.astype(F32).astype(BF16)


def scatter_window(data_ref, s, base, tile, cells):
    rows = data_ref[s, :, pl.ds(base, WIN)]
    hot = hot_rows(rows, tile, cells)
    both = [jnp.where(hot, rows[0:1], 0.0), jnp.where(hot, rows[1:2], 0.0)]
    return dot_nt(jnp.concatenate(both, axis=0).astype(BF16), hot_z(rows))


def plane_of(parts, t, ny):
    cells = TILE * ny
    rows = [p[b * cells + t * ny : b * cells + (t + 1) * ny] for b in range(2) for p in parts]
    return jnp.concatenate(rows, axis=0)


def tile_planes(starts_ref, data_ref, tile):
    slabs = data_ref.shape[0]
    ny = N2 // slabs
    parts = [
        scatter_window(data_ref, s, window_base(starts_ref, s, tile), tile, TILE * ny)
        for s in range(slabs)
    ]
    return [plane_of(parts, t, ny) for t in range(TILE)]


def more_planes(starts_ref, data_ref, tile):
    slabs = data_ref.shape[0]
    ny = N2 // slabs
    cells = TILE * ny
    parts = []
    for s in range(slabs):
        base = window_base(starts_ref, s, tile)

        def more(i, acc):
            at = pl.multiple_of(base + i * WIN, LANES)
            return acc + scatter_window(data_ref, s, at, tile, cells)

        windows = (starts_ref[s, 0, tile + 1] - base + WIN - 1) // WIN
        parts.append(lax.fori_loop(1, windows, more, jnp.zeros((2 * cells, N3), F32)))
    return [plane_of(parts, t, ny) for t in range(TILE)]


def zy_kernel(starts_ref, data_ref, tab_ref, turned_ref, plane_ref):
    inv_y = transposed(tab_ref[...])
    inv_z = dot(tab_ref[...], ones_at(N3, LANES)).astype(BF16)
    width = 32
    over = overflow(starts_ref, data_ref.shape[0])

    def transform(planes, first):
        done = []
        for plane in planes:
            z_done = dot(plane, inv_z).astype(BF16)
            done.append(dot(inv_y, jnp.concatenate([z_done[:N2], z_done[N2:]], axis=1)).astype(BF16))
        turned_ref[:, pl.ds(first, width), :] = jnp.swapaxes(jnp.stack(done, axis=0), 0, 1)

    @pl.when(jnp.logical_not(over))
    def _():
        @pl.loop(0, N1 // width)
        def _(group):
            first = pl.multiple_of(group * width, width)
            planes = []
            for u in range(width // TILE):
                tile = group * (width // TILE) + u
                planes += [plane.astype(BF16) for plane in tile_planes(starts_ref, data_ref, tile)]
            transform(planes, first)

    @pl.when(over)
    def _():
        @pl.loop(0, TILES)
        def _(tile):
            planes = tile_planes(starts_ref, data_ref, tile)
            added = more_planes(starts_ref, data_ref, tile)
            for t in range(TILE):
                plane_ref[tile * TILE + t] = (planes[t] + added[t]).astype(BF16)

        @pl.loop(0, N1 // width)
        def _(group):
            first = pl.multiple_of(group * width, width)
            transform([plane_ref[first + u] for u in range(width)], first)


def gather_window(data_ref, planes, s, base, tile):
    ny = N2 // data_ref.shape[0]
    cells = TILE * ny
    rows = data_ref[s, :, pl.ds(base, WIN)]
    hot = hot_rows(rows, tile, cells)
    mine = [plane[b * N2 + s * ny : b * N2 + (s + 1) * ny] for b in range(2) for plane in planes]
    picked = dot(jnp.concatenate(mine, axis=0).astype(BF16), hot_z(rows))
    found = [
        jnp.sum(jnp.where(hot, picked[b * cells : (b + 1) * cells], 0.0), axis=0, keepdims=True)
        for b in range(2)
    ]
    return jnp.concatenate(found, axis=0)


def gather_kernel(starts_ref, data_ref, back_ref, tab_ref, out_ref, sum_ref):
    slabs = data_ref.shape[0]
    sum_ref[...] = jnp.zeros_like(sum_ref)
    fwd_z = dot_nt(ones_at(LANES, N3), tab_ref[...]).astype(BF16)
    several = 16

    def wave_planes(tile, count):
        done = []
        for t in range(count):
            y_done = dot(tab_ref[...], back_ref[tile * TILE + t]).astype(BF16)
            done += [y_done[:, :LANES], y_done[:, LANES:]]
        waves = dot(jnp.concatenate(done, axis=0), fwd_z)
        return [waves[2 * N2 * t : 2 * N2 * (t + 1)] for t in range(count)]

    @pl.loop(0, TILES // several)
    def _(group):
        all_planes = wave_planes(group * several, several * TILE)
        found = []
        for u in range(several):
            tile = group * several + u
            planes = all_planes[TILE * u : TILE * (u + 1)]
            for s in range(slabs):
                base = window_base(starts_ref, s, tile)
                found.append((s, base, gather_window(data_ref, planes, s, base, tile)))
        for s, base, value in found:
            sum_ref[s, :, pl.ds(base, WIN)] += value

    @pl.when(overflow(starts_ref, slabs))
    def _():
        @pl.loop(0, TILES)
        def _(tile):
            planes = wave_planes(tile, TILE)
            for s in range(slabs):
                base = window_base(starts_ref, s, tile)

                @pl.loop(1, (starts_ref[s, 0, tile + 1] - base + WIN - 1) // WIN)
                def _(i):
                    at = pl.multiple_of(base + i * WIN, LANES)
                    sum_ref[s, :, pl.ds(at, WIN)] += gather_window(data_ref, planes, s, at, tile)

    part = out_ref.shape[3]
    for q in range(out_ref.shape[1]):
        out_ref[:, q] = sum_ref[:, :, q * part : (q + 1) * part].astype(out_ref.dtype)


SMEM = pl.BlockSpec(memory_space=pltpu.SMEM)
VMEM = pl.BlockSpec(memory_space=pltpu.VMEM)
HBM = pl.BlockSpec(memory_space=pltpu.HBM)
LIMIT = 32 * 1024 * 1024


def greet(peers):
    barrier = pltpu.get_barrier_semaphore()
    for peer in peers:
        pl.semaphore_signal(barrier, inc=1, device_id=peer, device_id_type=MESH)
    pl.semaphore_wait(barrier, len(peers))


def remote(src, dst, send_sem, recv_sem, peer):
    return pltpu.make_async_remote_copy(
        src_ref=src, dst_ref=dst, send_sem=send_sem, recv_sem=recv_sem, device_id=peer, device_id_type=MESH
    )


def send(src, dst, send_sem, recv_sem, peer):
    copy = remote(src, dst, send_sem, recv_sem, peer)
    copy.start()
    return copy


def wait_all(copies):
    for copy in copies:
        copy.wait()


def slab_peers(slabs):
    me = lax.axis_index("slab")
    return [lax.rem(me + d, slabs) for d in range(1, slabs)]


def place():
    band, slab = lax.axis_index("band"), lax.axis_index("slab")
    return band // 4, slab // 2, lax.rem(band, 4), lax.rem(slab, 2)


def device(y_hi, y_lo, z, core):
    return {"band": y_hi * 4 + z, "slab": y_lo * 2 + core}


def start_kernel(
    coef_ref, map_ref, data_ref, starts_ref, own_coef, own_map, coefs_ref, maps_ref, send_sem, recv_sem
):
    slabs, two, npw = coefs_ref.shape
    ny = N2 // slabs
    me = lax.axis_index("slab")
    peers = slab_peers(slabs)
    chunk = 1536
    for r in range(npw // LANES):
        own_map[0:1, r * LANES : (r + 1) * LANES] = map_ref[r : r + 1, :]
    for i in range(npw // chunk):
        at = pl.ds(i * chunk, chunk)
        block = coef_ref[:, at].astype(F32)
        for t in range(slabs):
            own_coef[t, :, at] = block[two * t : two * (t + 1)].astype(BF16)
    greet([{"slab": peer} for peer in peers])
    coef_copies = []
    for i, peer in enumerate(peers):
        to = {"slab": peer}
        coef_copies.append(send(own_coef.at[peer], coefs_ref.at[me], send_sem.at[0, i], recv_sem.at[0, i], to))
    coefs_ref[me] = own_coef[me]
    edges = iota((56, LANES), 0) * (TILE * ny * N3)
    below = jnp.zeros((56, LANES), jnp.int32)
    for r in range(npw // LANES):
        below = below + (own_map[0:1, r * LANES : (r + 1) * LANES] < edges).astype(jnp.int32)
    count = jnp.sum(below.astype(F32), axis=1, keepdims=True)
    spread = jnp.where(iota((56, LANES), 0) == iota((56, LANES), 1), count, 0.0)
    starts = jnp.sum(spread, axis=0, keepdims=True).astype(jnp.int32)
    after = pltpu.roll(starts, LANES - 1, 1)
    lane = iota((1, LANES), 1)
    over = (after > jnp.bitwise_and(starts, -LANES) + WIN) & (lane < TILES)
    flag = jnp.max(over.astype(F32), axis=1, keepdims=True).astype(jnp.int32)
    own_map[0:1, npw : npw + LANES] = jnp.where(lane == TILES + 1, flag, starts)
    copies = []
    for i, peer in enumerate(peers):
        to = {"slab": peer}
        copies.append(send(own_map, maps_ref.at[me], send_sem.at[1, i], recv_sem.at[1, i], to))
    maps_ref[me] = own_map[...]
    data_ref[...] = jnp.full(data_ref.shape, -1.0, F32)
    wait_all(copies)
    for s in range(slabs):
        starts_ref[s] = maps_ref[s, :, npw : npw + LANES]
    y_first = (iota((slabs, 1), 0) * ny).astype(F32)
    for i in range(npw // chunk):
        at = pl.ds(i * chunk, chunk)
        cell = jnp.concatenate([maps_ref[s, :, at] for s in range(slabs)], axis=0).astype(F32)
        row = jnp.floor((cell + 0.5) * (1.0 / N3))
        zpos = cell - row * N3
        xpos = jnp.floor((row + 0.5) * (1.0 / ny))
        ypos = row - xpos * ny + y_first
        kin = 2.0 * (xpos * xpos / (N1 * N1) + ypos * ypos / (N2 * N2) + zpos * zpos / (N3 * N3))
        for s in range(slabs):
            lines = [part[s : s + 1] for part in (row, zpos, kin)]
            data_ref[s, 2:5, at] = jnp.concatenate(lines, axis=0)
    wait_all(coef_copies)
    for s in range(slabs):
        for i in range(npw // chunk):
            at = pl.ds(i * chunk, chunk)
            data_ref[s, 0:2, at] = coefs_ref[s, :, at].astype(F32)


def dense_kernel(
    turned_ref, pot_ref, coef_ref, tab_ref, psi_out, back_ref, bands_ref,
    psi_ref, pots_ref, send_sem, recv_sem, coef_send, coef_recv, psi_sem,
):
    slabs = pots_ref.shape[0]
    y_hi, y_lo, z, core = place()
    me = lax.axis_index("slab")
    y = y_hi * 2 + y_lo
    sibling = device(y_hi, y_lo, z, 1 - core)

    def around(step):
        to = lax.rem(y + step + 4, 4)
        return device(to // 2, lax.rem(to, 2), z, core)

    for i in range(3):
        at = pl.ds(i * 3072, 3072)
        pots_ref[me, :, at] = pot_ref[:, at].astype(BF16)
    steps = [(a, b) for a in range(2) for b in range(4) if a + b > 0]
    others = [(lax.rem(y_hi + a, 2), lax.rem(z + b, 4)) for a, b in steps]
    members = [device(a, y_lo, b, core) for a, b in others]
    greet([sibling, around(-1), around(1)] + members)
    mine = pots_ref.at[me]
    to_far = send(mine, mine, send_sem.at[0], recv_sem.at[0], around(2 * core - 1))
    to_near = send(mine, mine, send_sem.at[1], recv_sem.at[1], sibling)

    inv_x = transposed(tab_ref[...])
    unroll = 8

    def psi_rows(first, last):
        @pl.loop(first, last)
        def _(group):
            rows = [group * unroll + u for u in range(unroll)]
            done = [dot(inv_x, turned_ref[row]).astype(BF16) for row in rows]
            for row, value in zip(rows, done):
                psi_ref[row] = value

    groups = N2 // unroll
    psi_rows(0, groups - 3)
    to_far.wait_send()
    slot = pots_ref.at[(1 - y_lo) * 2 + core]
    remote(slot, slot, send_sem.at[0], recv_sem.at[0], sibling).wait_recv()
    passed = send(slot, slot, send_sem.at[2], recv_sem.at[2], sibling)
    part = bands_ref.shape[3]
    quarter = pl.ds(pl.multiple_of(lax.axis_index("pert") * part, LANES), part)
    bands_ref[y_hi, z] = coef_ref[:, quarter]
    copies = []
    for i, member in enumerate(members):
        src = coef_ref.at[:, quarter]
        copies.append(send(src, bands_ref.at[y_hi, z], coef_send.at[i], coef_recv.at[i], member))
    psi_rows(groups - 3, groups)
    store = pltpu.make_async_copy(psi_ref, psi_out, psi_sem)
    store.start()
    to_near.wait()
    passed.wait_send()
    slot = pots_ref.at[(1 - y_lo) * 2 + 1 - core]
    remote(slot, slot, send_sem.at[2], recv_sem.at[2], sibling).wait_recv()

    width = 16
    lane = iota((N1 // slabs, LANES), 1)

    @pl.loop(0, N2 // width)
    def _(group):
        first = pl.multiple_of(group * width, width)
        done = []
        for v in range(width // 4):
            quads = [[], [], [], []]
            for s in range(slabs):
                parts = []
                for j in range(3):
                    off = pl.multiple_of(group * (width * N3) + (3 * v + j) * LANES, LANES)
                    parts.append(pots_ref[s, :, pl.ds(off, LANES)].astype(F32))
                a, b, c = parts
                quads[0].append(a)
                quads[1].append(jnp.where(lane < 32, pltpu.roll(a, 32, 1), pltpu.roll(b, 32, 1)))
                quads[2].append(jnp.where(lane < 64, pltpu.roll(b, 64, 1), pltpu.roll(c, 64, 1)))
                quads[3].append(pltpu.roll(c, 96, 1))
            for u in range(4):
                pot = jnp.concatenate(quads[u], axis=0)
                psi = psi_ref[first + 4 * v + u].astype(F32)
                product = jnp.concatenate([pot * psi[:, :LANES], pot * psi[:, LANES:]], axis=1)
                done.append(dot(tab_ref[...], product.astype(BF16)).astype(BF16))
        back_ref[:, pl.ds(first, width), :] = jnp.swapaxes(jnp.stack(done, axis=0), 0, 1)

    store.wait()
    wait_all(copies)


def middle_kernel(
    waves_ref, bands_ref, index_ref, energy_ref, data_ref, step_ref,
    got_ref, corr_ref, rhs_ref, back_ref, total_ref, send_sem, recv_sem,
):
    slabs, quarters, two, part = waves_ref.shape
    half, zs, bands, _ = bands_ref.shape
    chunk = 1152
    pert, slab = lax.axis_index("pert"), lax.axis_index("slab")
    steps = [(a, b) for a in range(quarters) for b in range(slabs) if a + b > 0]
    others = [(lax.rem(pert + a, quarters), lax.rem(slab + b, slabs)) for a, b in steps]
    peers = [{"pert": c, "slab": t} for c, t in others]
    greet(peers)
    copies = []
    for i, (c, t) in enumerate(others):
        src, dst = waves_ref.at[t, c], got_ref.at[pert, slab]
        copies.append(send(src, dst, send_sem.at[0, i], recv_sem.at[0, i], peers[i]))
    got_ref[pert, slab] = waves_ref[slab, pert]
    data_ref[...] = index_ref[...]
    wait_all(copies)

    def waves_at(at):
        parts = [got_ref[c, t, :, at].astype(F32) for c in range(quarters) for t in range(slabs)]
        return jnp.concatenate(parts, axis=0)

    def bands_at(at):
        parts = [bands_ref[a, c, :, at].astype(F32) for a in range(half) for c in range(zs)]
        return jnp.concatenate(parts, axis=0).astype(BF16)

    rows, count = quarters * slabs * two, half * zs * bands
    total = jnp.zeros((rows, count), F32)
    for i in range(part // chunk):
        at = pl.ds(i * chunk, chunk)
        total = total + dot_nt(waves_at(at).astype(BF16), bands_at(at))
    total_ref[...] = jnp.concatenate([total[: rows // 2], total[rows // 2 :]], axis=1)

    copies = []
    for i, peer in enumerate(peers):
        copies.append(send(total_ref, corr_ref.at[i], send_sem.at[1, i], recv_sem.at[1, i], peer))
    wait_all(copies)
    total = total_ref[...]
    for i in range(len(peers)):
        total = total + corr_ref[i]
    correlation = jnp.concatenate([total[:, :count], total[:, count:]], axis=0).astype(BF16)

    overlap = jnp.zeros((rows, rows), F32)
    for i in range(part // chunk):
        at = pl.ds(i * chunk, chunk)
        waves = waves_at(at)
        rhs = (waves - dot(correlation, bands_at(at))).astype(BF16)
        overlap = overlap + dot_nt(rhs, waves.astype(BF16))
        rhs = rhs.astype(F32)
        for c in range(quarters):
            for t in range(slabs):
                first = two * (c * slabs + t)
                rhs_ref[c, t, :, at] = rhs[first : first + two].astype(BF16)
    own = rows // quarters
    same = lax.rem(iota((rows, rows), 0), own) == lax.rem(iota((rows, rows), 1), own)
    kept = jnp.where(same, overlap, 0.0)
    lane = iota((rows, LANES), 1)
    tail = jnp.zeros((rows, LANES), F32)
    for p in range(quarters):
        mine = jnp.sum(kept[:, p * own : (p + 1) * own], axis=1, keepdims=True)
        high = mine.astype(BF16).astype(F32)
        tail = jnp.where(lane == p, high, tail)
        tail = jnp.where(lane == quarters + p, mine - high, tail)
    for c in range(quarters):
        for t in range(slabs):
            first = two * (c * slabs + t)
            rhs_ref[c, t, :, part:] = tail[first : first + two].astype(BF16)

    copies = []
    for i, (c, t) in enumerate(others):
        src, dst = rhs_ref.at[c, t], back_ref.at[slab, pert]
        copies.append(send(src, dst, send_sem.at[2, i], recv_sem.at[2, i], peers[i]))
    back_ref[slab, pert] = rhs_ref[pert, slab]
    wait_all(copies)

    numer = jnp.zeros((two, chunk), F32)
    denom = jnp.zeros((two, chunk), F32)
    tail = jnp.zeros((two, LANES), F32)
    energy = jnp.concatenate([jnp.full((1, chunk), energy_ref[b], F32) for b in range(two)], axis=0)
    for s in range(slabs):
        for q in range(quarters):
            tail = tail + back_ref[s, q, :, part:].astype(F32)
            for i in range(part // chunk):
                at = pl.ds(q * part + i * chunk, chunk)
                mine = back_ref[s, q, :, i * chunk : (i + 1) * chunk].astype(F32)
                data_ref[s, 0:2, at] = mine
                squares = mine * mine
                numer = numer + squares
                denom = denom + (index_ref[s, 4:5, at] - energy) * squares
    step = -jnp.sum(numer, axis=1, keepdims=True) / jnp.sum(denom, axis=1, keepdims=True)
    step = step * (4.0 * N1 * N2 * N3 / count)
    tail = step * (tail + pltpu.roll(tail, LANES - quarters, 1))
    tail = jnp.sum(tail, axis=0, keepdims=True)
    wide = jnp.broadcast_to(step, (two, LANES))
    step_ref[...] = jnp.concatenate([wide, tail, jnp.zeros((8 - two - 1, LANES), F32)], axis=0)


PART_A = 5
PART_B = 4
PARTS = PART_A + PART_B


def end_kernel(
    turned_ref, psi_ref, step_ref, pot_ref, tab_ref, out_ref, projected_ref,
    dens_ref, from_core, a_ref, b_ref, a_from_y, b_from_z, a_sum, b_sum, a_from_z, b_from_y,
    pots_ref, sums_ref, from_sums, core_send, core_recv, pot_send, pot_recv, a_send, a_recv, b_send, b_recv,
    a2_send, a2_recv, b2_send, b2_recv, sum_send, sum_recv,
):
    perts, planes, width = pots_ref.shape
    slabs = dens_ref.shape[0]
    y_hi, y_lo, z, core = place()
    pert, band = lax.axis_index("pert"), lax.axis_index("band")
    sibling = device(y_hi, y_lo, z, 1 - core)
    y_coords = [(1 - y_hi, y_lo), (1 - y_hi, 1 - y_lo), (y_hi, 1 - y_lo)]
    y_peers = [device(a, b, z, core) for a, b in y_coords]
    y_others = [device(a, b, z, 1 - core) for a, b in y_coords]
    z_coords = [lax.rem(z + d, 4) for d in range(1, 4)]
    z_peers = [device(y_hi, y_lo, c, core) for c in z_coords]
    p_peers = [{"pert": lax.rem(pert + d, perts)} for d in range(1, perts)]
    greet([sibling] + y_peers + y_others + z_peers + p_peers)

    pots_ref[pert] = pot_ref[:, pl.ds(pl.multiple_of(band * width, LANES), width)]
    pot_copies = []
    for i, peer in enumerate(p_peers):
        mine = pots_ref.at[pert]
        pot_copies.append(send(mine, mine, pot_send.at[i], pot_recv.at[i], peer))

    inv_x = transposed(tab_ref[...])
    lane = iota((N1, LANES), 1)
    half = 4 * PARTS

    def density_part(h, first, last):
        @pl.loop(first, last)
        def _(group):
            done = []
            for v in range(2):
                quad = h * 12 + group * 2 + v
                parts = []
                for u in range(4):
                    row = quad * 4 + u
                    field = dot(inv_x, turned_ref[row]).astype(BF16).astype(F32)
                    terms = psi_ref[row].astype(F32) * field
                    parts.append(step_ref[0:1] * terms[:, :LANES] + step_ref[1:2] * terms[:, LANES:])
                one, two, three = [pltpu.roll(parts[u], LANES - 32 * u, 1) for u in (1, 2, 3)]
                tiles = [
                    jnp.where(lane < 96, parts[0], one),
                    jnp.where(lane < 64, one, two),
                    jnp.where(lane < 32, two, three),
                ]
                done += [(quad * 3 + j, tile) for j, tile in enumerate(tiles)]
            for at, tile in done:
                for s in range(slabs):
                    dens_ref[s, at] = tile[s * planes : (s + 1) * planes].astype(BF16)

    halves = [1 - y_hi, y_hi]
    core_copies, a_copies, b_copies = [], [], []

    def to_sibling(k):
        h = halves[k]
        for l in range(2):
            src = dens_ref.at[l * 2 + 1 - core, pl.ds(h * half, half)]
            core_copies.append(
                send(src, from_core.at[k, l], core_send.at[k, l], core_recv.at[k, l], sibling)
            )

    def to_others(k):
        h = halves[k]
        wait_all(core_copies[2 * k : 2 * k + 2])
        for l in range(2):
            @pl.loop(0, 4)
            def _(c):
                done = []
                for j in range(PARTS):
                    at = c * PARTS + j
                    total = dens_ref[l * 2 + core, h * half + at].astype(F32) + from_core[k, l, at].astype(F32)
                    done.append(total.astype(BF16))
                for j in range(PARTS):
                    if j < PART_A:
                        a_ref[k, l, c, j] = done[j]
                    else:
                        b_ref[k, c, l, j - PART_A] = done[j]
        targets = [(0, y_lo), (1, 1 - y_lo)] if k == 0 else [(2, 1 - y_lo)]
        for i, l in targets:
            a_copies.append(send(a_ref.at[k, l], a_from_y.at[i], a_send.at[i], a_recv.at[i], y_peers[i]))
        for i, c in enumerate(z_coords):
            b_copies.append(
                send(b_ref.at[k, c], b_from_z.at[k, i], b_send.at[k, i], b_recv.at[k, i], z_peers[i])
            )

    density_part(halves[0], 0, 6)
    to_sibling(0)
    density_part(halves[1], 0, 3)
    to_others(0)
    density_part(halves[1], 3, 6)
    to_sibling(1)

    def total_of(pair):
        total = sum(pair(j) for j in range(PARTS))
        total = total[0:8] + total[8:16] + total[16:24]
        return jnp.sum(total, axis=0, keepdims=True)

    def pot(p, j):
        return pots_ref[p, :, j * LANES : (j + 1) * LANES]

    wait_all(pot_copies)
    pairs = [(p, q) for p in range(perts) for q in range(p + 1)]
    sums = [total_of(lambda j: pot(p, j) * pot(q, j)) for p, q in pairs]
    line = iota((1, LANES), 1)
    sums += [jnp.where(line == p, step_ref[2:3], 0.0) for p in range(perts)]
    sums += [jnp.zeros((1, LANES), F32)] * (16 - len(sums))
    sums_ref[0] = jnp.concatenate(sums, axis=0)
    to_others(1)

    def sum_sends(level, first, group):
        copies = []
        for i, peer in enumerate(group):
            k = first + i
            copies.append(send(sums_ref.at[level], from_sums.at[k], sum_send.at[k], sum_recv.at[k], peer))
        return copies

    def sum_up(level, first, copies):
        wait_all(copies)
        total = sums_ref[level]
        for i in range(len(copies)):
            total = total + from_sums[first + i]
        sums_ref[level + 1] = total

    near = [sibling] + y_peers + y_others
    near_copies = sum_sends(0, 0, near)

    wait_all(a_copies)

    @pl.loop(0, 4)
    def _(c):
        done = []
        for j in range(PART_A):
            total = a_ref[1, y_lo, c, j].astype(F32)
            for i in range(3):
                total = total + a_from_y[i, c, j].astype(F32)
            done.append(total.astype(BF16))
        for j in range(PART_A):
            a_sum[c, j] = done[j]

    copies = []
    for i, c in enumerate(z_coords):
        copies.append(send(a_sum.at[c], a_from_z.at[i], a2_send.at[i], a2_recv.at[i], z_peers[i]))
    wait_all(b_copies)
    spots = [(k, l, j) for k in range(2) for l in range(2) for j in range(PART_B)]
    done = []
    for k, l, j in spots:
        total = b_ref[k, z, l, j].astype(F32)
        for i in range(3):
            total = total + b_from_z[k, i, l, j].astype(F32)
        done.append(total.astype(BF16))
    for (k, l, j), value in zip(spots, done):
        b_sum[k, l, j] = value
    for i, (k, l) in enumerate([(0, y_lo), (0, 1 - y_lo), (1, 1 - y_lo)]):
        copies.append(send(b_sum.at[k, l], b_from_y.at[i], b2_send.at[i], b2_recv.at[i], y_peers[i]))
    sum_up(0, 0, near_copies)
    far_copies = sum_sends(1, len(near), z_peers)
    wait_all(copies)
    density = []
    for j in range(PARTS):
        if j < PART_A:
            total = a_sum[z, j].astype(F32)
            for i in range(3):
                total = total + a_from_z[i, j].astype(F32)
        else:
            total = b_sum[1, y_lo, j - PART_A].astype(F32)
            for i in range(3):
                total = total + b_from_y[i, j - PART_A].astype(F32)
        density.append(total)
    sum_up(1, len(near), far_copies)

    cells = 1.0 / (N1 * N2 * N3)
    totals = jnp.broadcast_to(jnp.sum(sums_ref[2], axis=1, keepdims=True) * cells, (16, LANES))
    gram = {pair: totals[k : k + 1] for k, pair in enumerate(pairs)}
    rhs = [totals[len(pairs) + p : len(pairs) + p + 1] for p in range(perts)]
    factor = {}
    for p in range(perts):
        for q in range(p + 1):
            value = gram[p, q]
            for k in range(q):
                value = value - factor[p, k] * factor[q, k]
            factor[p, q] = jnp.sqrt(value) if p == q else value / factor[q, q]
    coeffs = []
    for p in range(perts):
        value = rhs[p]
        for k in range(p):
            value = value - factor[p, k] * coeffs[k]
        coeffs.append(value / factor[p, p])
    for p in reversed(range(perts)):
        value = coeffs[p]
        for k in range(p + 1, perts):
            value = value - factor[k, p] * coeffs[k]
        coeffs[p] = value / factor[p, p]
    for j in range(PARTS):
        value = density[j]
        for p in range(perts):
            value = value - coeffs[p] * pot(p, j)
        out_ref[:, j * LANES : (j + 1) * LANES] = value
    projected_ref[...] = jnp.concatenate(rhs + rhs, axis=0)


def cost(flops, moved):
    return pl.CostEstimate(flops=int(flops), bytes_accessed=int(moved), transcendentals=0)


def params(collective=None):
    if collective is None:
        return pltpu.CompilerParams(vmem_limit_bytes=LIMIT)
    return pltpu.CompilerParams(vmem_limit_bytes=LIMIT, collective_id=collective, has_side_effects=True)


def shape(dims, kind):
    return jax.ShapeDtypeStruct(dims, kind)


def sems(*dims):
    return [pltpu.SemaphoreType.DMA(dims)] * 2


def start_of(coefs, wave_map, slabs):
    bands, npw = coefs.shape
    block = (slabs, bands // slabs, npw)
    return pl.pallas_call(
        start_kernel,
        out_shape=(shape((slabs, 8, npw + 2 * WIN), F32), shape((slabs, 1, LANES), jnp.int32)),
        in_specs=[VMEM] * 2,
        out_specs=(VMEM, VMEM),
        scratch_shapes=[
            pltpu.VMEM(block, BF16),
            pltpu.VMEM((1, npw + LANES), jnp.int32),
            pltpu.VMEM(block, BF16),
            pltpu.VMEM((slabs, 1, npw + LANES), jnp.int32),
        ]
        + sems(2, slabs - 1),
        compiler_params=params(1),
        name="start",
    )(coefs, wave_map.reshape(npw // LANES, LANES))


def zy_of(starts, data, tab):
    return pl.pallas_call(
        zy_kernel,
        out_shape=shape((N2, N1, 2 * LANES), BF16),
        in_specs=[SMEM] + [VMEM] * 2,
        out_specs=VMEM,
        scratch_shapes=[pltpu.VMEM((N1, 2 * N2, N3), BF16)],
        compiler_params=params(),
        cost_estimate=cost(2e10, 8e6),
        name="scatter_zy",
    )(starts, data, tab)


def dense_of(turned, pot, coefs, tab, slabs):
    bands, npw = coefs.shape
    return pl.pallas_call(
        dense_kernel,
        out_shape=(
            shape((N2, N1, 2 * LANES), BF16),
            shape((N1, N2, 2 * LANES), BF16),
            shape((2, 4, bands, npw // QUARTERS), BF16),
        ),
        in_specs=[VMEM] * 4,
        out_specs=(HBM, VMEM, VMEM),
        scratch_shapes=[
            pltpu.VMEM((N2, N1, 2 * LANES), BF16),
            pltpu.VMEM((slabs,) + pot.shape, BF16),
        ]
        + sems(3)
        + sems(7)
        + [pltpu.SemaphoreType.DMA(())],
        compiler_params=params(4),
        cost_estimate=cost(2e10, 8e6),
        name="dense",
    )(turned, pot, coefs, tab)


def gather_of(starts, data, back, tab, npw):
    slabs = data.shape[0]
    return pl.pallas_call(
        gather_kernel,
        out_shape=shape((slabs, QUARTERS, 2, npw // QUARTERS), BF16),
        in_specs=[SMEM] + [VMEM] * 3,
        out_specs=VMEM,
        scratch_shapes=[pltpu.VMEM((slabs, 2, data.shape[2]), F32)],
        compiler_params=params(),
        cost_estimate=cost(2e10, 8e6),
        name="gather",
    )(starts, data, back, tab)


def middle_of(waves, bands, index, energies):
    slabs, quarters, two, part = waves.shape
    peers = slabs * quarters - 1
    small = (slabs * quarters * two // 2, LANES)
    longer = pltpu.VMEM((slabs, quarters, two, part + LANES), BF16)
    return pl.pallas_call(
        middle_kernel,
        out_shape=(shape(index.shape, F32), shape((8, LANES), F32)),
        in_specs=[VMEM] * 3 + [SMEM],
        out_specs=(VMEM, VMEM),
        scratch_shapes=[
            pltpu.VMEM(waves.shape, BF16),
            pltpu.VMEM((peers,) + small, F32),
            longer,
            longer,
            pltpu.VMEM(small, F32),
        ]
        + sems(3, peers),
        compiler_params=params(2),
        name="middle",
    )(waves, bands, index, energies)


def end_of(turned, psi, step, pot, tab, slabs, perts):
    planes, cross = pot.shape
    width = cross // 8
    tile = (planes, LANES)
    return pl.pallas_call(
        end_kernel,
        out_shape=(shape((planes, width), F32), shape((8, LANES), F32)),
        in_specs=[VMEM] * 5,
        out_specs=(VMEM, VMEM),
        scratch_shapes=[
            pltpu.VMEM((slabs, 8 * PARTS) + tile, BF16),
            pltpu.VMEM((2, 2, 4 * PARTS) + tile, BF16),
            pltpu.VMEM((2, 2, 4, PART_A) + tile, BF16),
            pltpu.VMEM((2, 4, 2, PART_B) + tile, BF16),
            pltpu.VMEM((3, 4, PART_A) + tile, BF16),
            pltpu.VMEM((2, 3, 2, PART_B) + tile, BF16),
            pltpu.VMEM((4, PART_A) + tile, BF16),
            pltpu.VMEM((2, 2, PART_B) + tile, BF16),
            pltpu.VMEM((3, PART_A) + tile, BF16),
            pltpu.VMEM((3, PART_B) + tile, BF16),
            pltpu.VMEM((perts, planes, width), F32),
            pltpu.VMEM((3, 16, LANES), F32),
            pltpu.VMEM((10, 16, LANES), F32),
        ]
        + sems(2, 2)
        + sems(3)
        + sems(3)
        + sems(2, 3)
        + sems(3)
        + sems(3)
        + sems(10),
        compiler_params=params(3),
        name="density",
    )(turned, psi, step, pot, tab)


def per_device(wave_coeffs, band_energies, trial_potentials, wave_map):
    slabs = lax.axis_size("slab")
    me = lax.axis_index("slab")
    bands, npw = wave_coeffs.shape
    planes, cross = trial_potentials.shape[1:]
    tab = cosines(N1)
    pot = trial_potentials.reshape(planes, cross)
    energies = lax.dynamic_slice_in_dim(band_energies, me * (bands // slabs), bands // slabs, 0)
    data, starts = start_of(wave_coeffs, wave_map, slabs)
    turned = zy_of(starts, data, tab)
    psi, back, all_bands = dense_of(turned, pot, wave_coeffs, tab, slabs)
    waves = gather_of(starts, data, back, tab, npw)
    data, step = middle_of(waves, all_bands, data, energies)
    turned = zy_of(starts, data, tab)
    residual, projected = end_of(turned, psi, step, pot, tab, slabs, lax.axis_size("pert"))
    return (residual.reshape(1, planes, -1), projected[: lax.axis_size("pert"), :1])


def solution(mesh):
    return jax.shard_map(
        per_device,
        mesh=mesh,
        in_specs=(P("band", "slab"), P("band"), P("pert", "slab", None), P("slab")),
        out_specs=(P("pert", "slab", "band"), P(None, "pert")),
        check_vma=False,
    )
```

```python
import jax
import jax.numpy as jnp
from jax import lax
from jax.experimental import pallas as pl
from jax.experimental.pallas import tpu as pltpu
from jax.sharding import PartitionSpec as P

N1 = 96
N2 = 96
N3 = 96
LANES = 128
WIN = 512
TILE = 2
TILES = N1 // TILE
QUARTERS = 4
F32 = jnp.float32
BF16 = jnp.bfloat16
NT = (((1,), (1,)), ((), ()))
MESH = pl.DeviceIdType.MESH


def cosines(n):
    rows = jnp.arange(n, dtype=jnp.int32).astype(jnp.float32)[:, None]
    cols = jnp.arange(n, dtype=jnp.int32).astype(jnp.float32)[None, :]
    table = jnp.sqrt(2.0 / n) * jnp.cos(jnp.pi * rows * (cols + 0.5) / n)
    table = table * jnp.where(rows == 0, jnp.sqrt(0.5), 1.0)
    return table.astype(jnp.bfloat16)


def dot(a, b):
    return jnp.dot(a, b, preferred_element_type=F32)


def dot_nt(a, b):
    return lax.dot_general(a, b, NT, preferred_element_type=F32)


def iota(dims, axis):
    return lax.broadcasted_iota(jnp.int32, dims, axis)


def ones_at(rows, cols):
    return (iota((rows, cols), 0) == iota((rows, cols), 1)).astype(F32).astype(BF16)


def transposed(table):
    return dot_nt(ones_at(table.shape[1], table.shape[1]), table).astype(BF16)


def window_base(starts_ref, s, tile):
    return pl.multiple_of((starts_ref[s, 0, tile] // LANES) * LANES, LANES)


def overflow(starts_ref, slabs):
    total = starts_ref[0, 0, TILES + 1]
    for s in range(1, slabs):
        total = total + starts_ref[s, 0, TILES + 1]
    return total > 0


def hot_rows(rows, tile, cells):
    at = rows[2:3] - (tile * cells).astype(F32)
    return iota((cells, WIN), 0).astype(F32) == at


def hot_z(rows):
    here = iota((N3, WIN), 0).astype(F32) == rows[3:4]
    return here.astype(F32).astype(BF16)


def scatter_window(data_ref, s, base, tile, cells):
    rows = data_ref[s, :, pl.ds(base, WIN)]
    hot = hot_rows(rows, tile, cells)
    both = [jnp.where(hot, rows[0:1], 0.0), jnp.where(hot, rows[1:2], 0.0)]
    return dot_nt(jnp.concatenate(both, axis=0).astype(BF16), hot_z(rows))


def plane_of(parts, t, ny):
    cells = TILE * ny
    rows = [p[b * cells + t * ny : b * cells + (t + 1) * ny] for b in range(2) for p in parts]
    return jnp.concatenate(rows, axis=0)


def tile_planes(starts_ref, data_ref, tile):
    slabs = data_ref.shape[0]
    ny = N2 // slabs
    parts = [
        scatter_window(data_ref, s, window_base(starts_ref, s, tile), tile, TILE * ny)
        for s in range(slabs)
    ]
    return [plane_of(parts, t, ny) for t in range(TILE)]


def more_planes(starts_ref, data_ref, tile):
    slabs = data_ref.shape[0]
    ny = N2 // slabs
    cells = TILE * ny
    parts = []
    for s in range(slabs):
        base = window_base(starts_ref, s, tile)

        def more(i, acc):
            at = pl.multiple_of(base + i * WIN, LANES)
            return acc + scatter_window(data_ref, s, at, tile, cells)

        windows = (starts_ref[s, 0, tile + 1] - base + WIN - 1) // WIN
        parts.append(lax.fori_loop(1, windows, more, jnp.zeros((2 * cells, N3), F32)))
    return [plane_of(parts, t, ny) for t in range(TILE)]


def zy_kernel(starts_ref, data_ref, tab_ref, turned_ref, plane_ref):
    inv_y = transposed(tab_ref[...])
    inv_z = dot(tab_ref[...], ones_at(N3, LANES)).astype(BF16)
    width = 32
    over = overflow(starts_ref, data_ref.shape[0])

    def transform(planes, first):
        done = []
        for plane in planes:
            z_done = dot(plane, inv_z).astype(BF16)
            done.append(dot(inv_y, jnp.concatenate([z_done[:N2], z_done[N2:]], axis=1)).astype(BF16))
        turned_ref[:, pl.ds(first, width), :] = jnp.swapaxes(jnp.stack(done, axis=0), 0, 1)

    @pl.when(jnp.logical_not(over))
    def _():
        @pl.loop(0, N1 // width)
        def _(group):
            first = pl.multiple_of(group * width, width)
            planes = []
            for u in range(width // TILE):
                tile = group * (width // TILE) + u
                planes += [plane.astype(BF16) for plane in tile_planes(starts_ref, data_ref, tile)]
            transform(planes, first)

    @pl.when(over)
    def _():
        @pl.loop(0, TILES)
        def _(tile):
            planes = tile_planes(starts_ref, data_ref, tile)
            added = more_planes(starts_ref, data_ref, tile)
            for t in range(TILE):
                plane_ref[tile * TILE + t] = (planes[t] + added[t]).astype(BF16)

        @pl.loop(0, N1 // width)
        def _(group):
            first = pl.multiple_of(group * width, width)
            transform([plane_ref[first + u] for u in range(width)], first)


def gather_window(data_ref, planes, s, base, tile):
    ny = N2 // data_ref.shape[0]
    cells = TILE * ny
    rows = data_ref[s, :, pl.ds(base, WIN)]
    hot = hot_rows(rows, tile, cells)
    mine = [plane[b * N2 + s * ny : b * N2 + (s + 1) * ny] for b in range(2) for plane in planes]
    picked = dot(jnp.concatenate(mine, axis=0).astype(BF16), hot_z(rows))
    found = [
        jnp.sum(jnp.where(hot, picked[b * cells : (b + 1) * cells], 0.0), axis=0, keepdims=True)
        for b in range(2)
    ]
    return jnp.concatenate(found, axis=0)


def gather_kernel(starts_ref, data_ref, back_ref, tab_ref, out_ref, sum_ref):
    slabs = data_ref.shape[0]
    sum_ref[...] = jnp.zeros_like(sum_ref)
    fwd_z = dot_nt(ones_at(LANES, N3), tab_ref[...]).astype(BF16)
    several = 16

    def wave_planes(tile, count):
        done = []
        for t in range(count):
            y_done = dot(tab_ref[...], back_ref[tile * TILE + t]).astype(BF16)
            done += [y_done[:, :LANES], y_done[:, LANES:]]
        waves = dot(jnp.concatenate(done, axis=0), fwd_z)
        return [waves[2 * N2 * t : 2 * N2 * (t + 1)] for t in range(count)]

    @pl.loop(0, TILES // several)
    def _(group):
        all_planes = wave_planes(group * several, several * TILE)
        found = []
        for u in range(several):
            tile = group * several + u
            planes = all_planes[TILE * u : TILE * (u + 1)]
            for s in range(slabs):
                base = window_base(starts_ref, s, tile)
                found.append((s, base, gather_window(data_ref, planes, s, base, tile)))
        for s, base, value in found:
            sum_ref[s, :, pl.ds(base, WIN)] += value

    @pl.when(overflow(starts_ref, slabs))
    def _():
        @pl.loop(0, TILES)
        def _(tile):
            planes = wave_planes(tile, TILE)
            for s in range(slabs):
                base = window_base(starts_ref, s, tile)

                @pl.loop(1, (starts_ref[s, 0, tile + 1] - base + WIN - 1) // WIN)
                def _(i):
                    at = pl.multiple_of(base + i * WIN, LANES)
                    sum_ref[s, :, pl.ds(at, WIN)] += gather_window(data_ref, planes, s, at, tile)

    part = out_ref.shape[3]
    for q in range(out_ref.shape[1]):
        out_ref[:, q] = sum_ref[:, :, q * part : (q + 1) * part].astype(out_ref.dtype)


SMEM = pl.BlockSpec(memory_space=pltpu.SMEM)
VMEM = pl.BlockSpec(memory_space=pltpu.VMEM)
LIMIT = 32 * 1024 * 1024


def greet(peers):
    for peer in peers:
        pl.semaphore_signal(pltpu.get_barrier_semaphore(), inc=1, device_id=peer, device_id_type=MESH)


def greeted(peers):
    pl.semaphore_wait(pltpu.get_barrier_semaphore(), len(peers))


def remote(src, dst, send_sem, recv_sem, peer):
    return pltpu.make_async_remote_copy(
        src_ref=src, dst_ref=dst, send_sem=send_sem, recv_sem=recv_sem, device_id=peer, device_id_type=MESH
    )


def send(src, dst, send_sem, recv_sem, peer):
    copy = remote(src, dst, send_sem, recv_sem, peer)
    copy.start()
    return copy


def wait_all(copies):
    for copy in copies:
        copy.wait()


def slab_peers(slabs):
    me = lax.axis_index("slab")
    return [lax.rem(me + d, slabs) for d in range(1, slabs)]


def place():
    band, slab = lax.axis_index("band"), lax.axis_index("slab")
    return band // 4, slab // 2, lax.rem(band, 4), lax.rem(slab, 2)


def device(y_hi, y_lo, z, core):
    return {"band": y_hi * 4 + z, "slab": y_lo * 2 + core}


def start_kernel(
    coef_ref, map_ref, pot_ref, data_ref, starts_ref, narrow_ref,
    own_coef, own_map, coefs_ref, maps_ref, send_sem, recv_sem,
):
    slabs, two, npw = coefs_ref.shape
    ny = N2 // slabs
    me = lax.axis_index("slab")
    peers = slab_peers(slabs)
    chunk = 1536
    greet([{"slab": peer} for peer in peers])
    for r in range(npw // LANES):
        own_map[0:1, r * LANES : (r + 1) * LANES] = map_ref[r : r + 1, :]
    for i in range(npw // chunk):
        at = pl.ds(i * chunk, chunk)
        block = coef_ref[:, at].astype(F32)
        for t in range(slabs):
            own_coef[t, :, at] = block[two * t : two * (t + 1)].astype(BF16)
    greeted(peers)
    coef_copies = []
    for i, peer in enumerate(peers):
        to = {"slab": peer}
        coef_copies.append(send(own_coef.at[peer], coefs_ref.at[me], send_sem.at[0, i], recv_sem.at[0, i], to))
    coefs_ref[me] = own_coef[me]
    edges = iota((56, LANES), 0) * (TILE * ny * N3)
    below = jnp.zeros((56, LANES), jnp.int32)
    for r in range(npw // LANES):
        below = below + (own_map[0:1, r * LANES : (r + 1) * LANES] < edges).astype(jnp.int32)
    count = jnp.sum(below.astype(F32), axis=1, keepdims=True)
    spread = jnp.where(iota((56, LANES), 0) == iota((56, LANES), 1), count, 0.0)
    starts = jnp.sum(spread, axis=0, keepdims=True).astype(jnp.int32)
    after = pltpu.roll(starts, LANES - 1, 1)
    lane = iota((1, LANES), 1)
    over = (after > jnp.bitwise_and(starts, -LANES) + WIN) & (lane < TILES)
    flag = jnp.max(over.astype(F32), axis=1, keepdims=True).astype(jnp.int32)
    own_map[0:1, npw : npw + LANES] = jnp.where(lane == TILES + 1, flag, starts)
    copies = []
    for i, peer in enumerate(peers):
        to = {"slab": peer}
        copies.append(send(own_map, maps_ref.at[me], send_sem.at[1, i], recv_sem.at[1, i], to))
    maps_ref[me] = own_map[...]
    data_ref[...] = jnp.full(data_ref.shape, -1.0, F32)
    narrow_ref[...] = pot_ref[...].astype(BF16)
    wait_all(copies)
    for s in range(slabs):
        starts_ref[s] = maps_ref[s, :, npw : npw + LANES]
    y_first = (iota((slabs, 1), 0) * ny).astype(F32)
    for i in range(npw // chunk):
        at = pl.ds(i * chunk, chunk)
        cell = jnp.concatenate([maps_ref[s, :, at] for s in range(slabs)], axis=0).astype(F32)
        row = jnp.floor((cell + 0.5) * (1.0 / N3))
        zpos = cell - row * N3
        xpos = jnp.floor((row + 0.5) * (1.0 / ny))
        ypos = row - xpos * ny + y_first
        kin = 2.0 * (xpos * xpos / (N1 * N1) + ypos * ypos / (N2 * N2) + zpos * zpos / (N3 * N3))
        for s in range(slabs):
            lines = [part[s : s + 1] for part in (row, zpos, kin)]
            data_ref[s, 2:5, at] = jnp.concatenate(lines, axis=0)
    wait_all(coef_copies)
    for s in range(slabs):
        for i in range(npw // chunk):
            at = pl.ds(i * chunk, chunk)
            data_ref[s, 0:2, at] = coefs_ref[s, :, at].astype(F32)


def dense_kernel(
    turned_ref, pot_ref, far_ref, coef_ref, tab_ref, psi_ref, back_ref, bands_ref,
    pots_ref, send_sem, recv_sem, coef_send, coef_recv,
):
    slabs = pots_ref.shape[0]
    y_hi, y_lo, z, core = place()
    me = lax.axis_index("slab")
    distant = (1 - y_lo) * 2 + core
    sibling = device(y_hi, y_lo, z, 1 - core)
    steps = [(a, b) for a in range(2) for b in range(4) if a + b > 0]
    others = [(lax.rem(y_hi + a, 2), lax.rem(z + b, 4)) for a, b in steps]
    members = [device(a, y_lo, b, core) for a, b in others]
    greet([sibling] + members)
    part = bands_ref.shape[3]
    quarter = pl.ds(pl.multiple_of(lax.axis_index("pert") * part, LANES), part)
    bands_ref[y_hi, z] = coef_ref[:, quarter]
    pots_ref[me] = pot_ref[...]
    pots_ref[distant] = far_ref[...]
    greeted([sibling] + members)
    copies = []
    for i, member in enumerate(members):
        src = coef_ref.at[:, quarter]
        copies.append(send(src, bands_ref.at[y_hi, z], coef_send.at[i], coef_recv.at[i], member))
    near = [
        send(pot_ref, pots_ref.at[me], send_sem.at[0], recv_sem.at[0], sibling),
        send(far_ref, pots_ref.at[distant], send_sem.at[1], recv_sem.at[1], sibling),
    ]

    inv_x = transposed(tab_ref[...])
    unroll = 16

    @pl.loop(0, N2 // unroll)
    def _(group):
        rows = [group * unroll + u for u in range(unroll)]
        done = [dot(inv_x, turned_ref[row]).astype(BF16) for row in rows]
        for row, value in zip(rows, done):
            psi_ref[row] = value

    wait_all(near)

    width = 16
    lane = iota((N1 // slabs, LANES), 1)

    @pl.loop(0, N2 // width)
    def _(group):
        first = pl.multiple_of(group * width, width)
        done = []
        for v in range(width // 4):
            quads = [[], [], [], []]
            for s in range(slabs):
                parts = []
                for j in range(3):
                    off = pl.multiple_of(group * (width * N3) + (3 * v + j) * LANES, LANES)
                    parts.append(pots_ref[s, :, pl.ds(off, LANES)].astype(F32))
                a, b, c = parts
                quads[0].append(a)
                quads[1].append(jnp.where(lane < 32, pltpu.roll(a, 32, 1), pltpu.roll(b, 32, 1)))
                quads[2].append(jnp.where(lane < 64, pltpu.roll(b, 64, 1), pltpu.roll(c, 64, 1)))
                quads[3].append(pltpu.roll(c, 96, 1))
            for u in range(4):
                pot = jnp.concatenate(quads[u], axis=0)
                psi = psi_ref[first + 4 * v + u].astype(F32)
                product = jnp.concatenate([pot * psi[:, :LANES], pot * psi[:, LANES:]], axis=1)
                done.append(dot(tab_ref[...], product.astype(BF16)).astype(BF16))
        back_ref[:, pl.ds(first, width), :] = jnp.swapaxes(jnp.stack(done, axis=0), 0, 1)

    wait_all(copies)


def middle_kernel(
    waves_ref, bands_ref, index_ref, energy_ref, data_ref, step_ref,
    got_ref, corr_ref, rhs_ref, back_ref, total_ref, send_sem, recv_sem,
):
    slabs, quarters, two, part = waves_ref.shape
    half, zs, bands, _ = bands_ref.shape
    chunk = 1152
    pert, slab = lax.axis_index("pert"), lax.axis_index("slab")
    steps = [(a, b) for a in range(quarters) for b in range(slabs) if a + b > 0]
    others = [(lax.rem(pert + a, quarters), lax.rem(slab + b, slabs)) for a, b in steps]
    peers = [{"pert": c, "slab": t} for c, t in others]
    greet(peers)
    greeted(peers)
    copies = []
    for i, (c, t) in enumerate(others):
        src, dst = waves_ref.at[t, c], got_ref.at[pert, slab]
        copies.append(send(src, dst, send_sem.at[0, i], recv_sem.at[0, i], peers[i]))
    got_ref[pert, slab] = waves_ref[slab, pert]
    data_ref[...] = index_ref[...]
    wait_all(copies)

    def waves_at(at):
        parts = [got_ref[c, t, :, at].astype(F32) for c in range(quarters) for t in range(slabs)]
        return jnp.concatenate(parts, axis=0)

    def bands_at(at):
        parts = [bands_ref[a, c, :, at].astype(F32) for a in range(half) for c in range(zs)]
        return jnp.concatenate(parts, axis=0).astype(BF16)

    rows, count = quarters * slabs * two, half * zs * bands
    total = jnp.zeros((rows, count), F32)
    for i in range(part // chunk):
        at = pl.ds(i * chunk, chunk)
        total = total + dot_nt(waves_at(at).astype(BF16), bands_at(at))
    total_ref[...] = jnp.concatenate([total[: rows // 2], total[rows // 2 :]], axis=1)

    copies = []
    for i, peer in enumerate(peers):
        copies.append(send(total_ref, corr_ref.at[i], send_sem.at[1, i], recv_sem.at[1, i], peer))
    wait_all(copies)
    total = total_ref[...]
    for i in range(len(peers)):
        total = total + corr_ref[i]
    correlation = jnp.concatenate([total[:, :count], total[:, count:]], axis=0).astype(BF16)

    overlap = jnp.zeros((rows, rows), F32)
    for i in range(part // chunk):
        at = pl.ds(i * chunk, chunk)
        waves = waves_at(at)
        rhs = (waves - dot(correlation, bands_at(at))).astype(BF16)
        overlap = overlap + dot_nt(rhs, waves.astype(BF16))
        rhs = rhs.astype(F32)
        for c in range(quarters):
            for t in range(slabs):
                first = two * (c * slabs + t)
                rhs_ref[c, t, :, at] = rhs[first : first + two].astype(BF16)
    own = rows // quarters
    same = lax.rem(iota((rows, rows), 0), own) == lax.rem(iota((rows, rows), 1), own)
    kept = jnp.where(same, overlap, 0.0)
    lane = iota((rows, LANES), 1)
    tail = jnp.zeros((rows, LANES), F32)
    for p in range(quarters):
        mine = jnp.sum(kept[:, p * own : (p + 1) * own], axis=1, keepdims=True)
        high = mine.astype(BF16).astype(F32)
        tail = jnp.where(lane == p, high, tail)
        tail = jnp.where(lane == quarters + p, mine - high, tail)
    for c in range(quarters):
        for t in range(slabs):
            first = two * (c * slabs + t)
            rhs_ref[c, t, :, part:] = tail[first : first + two].astype(BF16)

    copies = []
    for i, (c, t) in enumerate(others):
        src, dst = rhs_ref.at[c, t], back_ref.at[slab, pert]
        copies.append(send(src, dst, send_sem.at[2, i], recv_sem.at[2, i], peers[i]))
    back_ref[slab, pert] = rhs_ref[pert, slab]
    wait_all(copies)

    numer = jnp.zeros((two, chunk), F32)
    denom = jnp.zeros((two, chunk), F32)
    tail = jnp.zeros((two, LANES), F32)
    energy = [jnp.full((1, chunk), energy_ref[slab * two + b], F32) for b in range(two)]
    energy = jnp.concatenate(energy, axis=0)
    for s in range(slabs):
        for q in range(quarters):
            tail = tail + back_ref[s, q, :, part:].astype(F32)
            for i in range(part // chunk):
                at = pl.ds(q * part + i * chunk, chunk)
                mine = back_ref[s, q, :, i * chunk : (i + 1) * chunk].astype(F32)
                data_ref[s, 0:2, at] = mine
                squares = mine * mine
                numer = numer + squares
                denom = denom + (index_ref[s, 4:5, at] - energy) * squares
    step = -jnp.sum(numer, axis=1, keepdims=True) / jnp.sum(denom, axis=1, keepdims=True)
    step = step * (4.0 * N1 * N2 * N3 / count)
    tail = step * (tail + pltpu.roll(tail, LANES - quarters, 1))
    tail = jnp.sum(tail, axis=0, keepdims=True)
    wide = jnp.broadcast_to(step, (two, LANES))
    step_ref[...] = jnp.concatenate([wide, tail, jnp.zeros((8 - two - 1, LANES), F32)], axis=0)


PART_A = 5
PART_B = 4
PARTS = PART_A + PART_B


def end_kernel(
    turned_ref, psi_ref, step_ref, pot_ref, tab_ref, out_ref, projected_ref,
    dens_ref, from_core, a_ref, b_ref, a_from_y, b_from_z, a_sum, b_sum, a_from_z, b_from_y,
    pots_ref, sums_ref, from_sums, core_send, core_recv, pot_send, pot_recv, a_send, a_recv, b_send, b_recv,
    a2_send, a2_recv, b2_send, b2_recv, sum_send, sum_recv,
):
    perts, planes, width = pots_ref.shape
    slabs = dens_ref.shape[0]
    y_hi, y_lo, z, core = place()
    pert, band = lax.axis_index("pert"), lax.axis_index("band")
    sibling = device(y_hi, y_lo, z, 1 - core)
    y_coords = [(1 - y_hi, y_lo), (1 - y_hi, 1 - y_lo), (y_hi, 1 - y_lo)]
    y_peers = [device(a, b, z, core) for a, b in y_coords]
    y_others = [device(a, b, z, 1 - core) for a, b in y_coords]
    z_coords = [lax.rem(z + d, 4) for d in range(1, 4)]
    z_peers = [device(y_hi, y_lo, c, core) for c in z_coords]
    p_peers = [{"pert": lax.rem(pert + d, perts)} for d in range(1, perts)]
    everyone = [sibling] + y_peers + y_others + z_peers + p_peers
    greet(everyone)
    pots_ref[pert] = pot_ref[:, pl.ds(pl.multiple_of(band * width, LANES), width)]

    inv_x = transposed(tab_ref[...])
    lane = iota((N1, LANES), 1)
    half = 4 * PARTS

    def density_part(h, first, last):
        @pl.loop(first, last)
        def _(group):
            done = []
            for v in range(4):
                quad = h * 12 + group * 4 + v
                parts = []
                for u in range(4):
                    row = quad * 4 + u
                    field = dot(inv_x, turned_ref[row]).astype(BF16).astype(F32)
                    terms = psi_ref[row].astype(F32) * field
                    parts.append(step_ref[0:1] * terms[:, :LANES] + step_ref[1:2] * terms[:, LANES:])
                one, two, three = [pltpu.roll(parts[u], LANES - 32 * u, 1) for u in (1, 2, 3)]
                tiles = [
                    jnp.where(lane < 96, parts[0], one),
                    jnp.where(lane < 64, one, two),
                    jnp.where(lane < 32, two, three),
                ]
                done += [(quad * 3 + j, tile) for j, tile in enumerate(tiles)]
            for at, tile in done:
                for s in range(slabs):
                    dens_ref[s, at] = tile[s * planes : (s + 1) * planes].astype(BF16)

    halves = [1 - y_hi, y_hi]
    core_copies, a_copies, b_copies = [], [], []

    def to_sibling(k):
        h = halves[k]
        for l in range(2):
            src = dens_ref.at[l * 2 + 1 - core, pl.ds(h * half, half)]
            core_copies.append(
                send(src, from_core.at[k, l], core_send.at[k, l], core_recv.at[k, l], sibling)
            )

    def to_others(k):
        h = halves[k]
        wait_all(core_copies[2 * k : 2 * k + 2])
        for l in range(2):
            @pl.loop(0, 4)
            def _(c):
                done = []
                for j in range(PARTS):
                    at = c * PARTS + j
                    total = dens_ref[l * 2 + core, h * half + at].astype(F32) + from_core[k, l, at].astype(F32)
                    done.append(total.astype(BF16))
                for j in range(PARTS):
                    if j < PART_A:
                        a_ref[k, l, c, j] = done[j]
                    else:
                        b_ref[k, c, l, j - PART_A] = done[j]
        targets = [(0, y_lo), (1, 1 - y_lo)] if k == 0 else [(2, 1 - y_lo)]
        for i, l in targets:
            a_copies.append(send(a_ref.at[k, l], a_from_y.at[i], a_send.at[i], a_recv.at[i], y_peers[i]))
        for i, c in enumerate(z_coords):
            b_copies.append(
                send(b_ref.at[k, c], b_from_z.at[k, i], b_send.at[k, i], b_recv.at[k, i], z_peers[i])
            )

    density_part(halves[0], 0, 3)
    greeted(everyone)
    to_sibling(0)
    pot_copies = []
    for i, peer in enumerate(p_peers):
        mine = pots_ref.at[pert]
        pot_copies.append(send(mine, mine, pot_send.at[i], pot_recv.at[i], peer))
    density_part(halves[1], 0, 1)
    to_others(0)
    density_part(halves[1], 1, 3)
    to_sibling(1)

    def total_of(pair):
        total = sum(pair(j) for j in range(PARTS))
        total = total[0:8] + total[8:16] + total[16:24]
        return jnp.sum(total, axis=0, keepdims=True)

    def pot(p, j):
        return pots_ref[p, :, j * LANES : (j + 1) * LANES]

    wait_all(pot_copies)
    pairs = [(p, q) for p in range(perts) for q in range(p + 1)]
    sums = [total_of(lambda j: pot(p, j) * pot(q, j)) for p, q in pairs]
    line = iota((1, LANES), 1)
    sums += [jnp.where(line == p, step_ref[2:3], 0.0) for p in range(perts)]
    sums += [jnp.zeros((1, LANES), F32)] * (16 - len(sums))
    sums_ref[0] = jnp.concatenate(sums, axis=0)
    to_others(1)

    def sum_sends(level, first, group):
        copies = []
        for i, peer in enumerate(group):
            k = first + i
            copies.append(send(sums_ref.at[level], from_sums.at[k], sum_send.at[k], sum_recv.at[k], peer))
        return copies

    def sum_up(level, first, copies):
        wait_all(copies)
        total = sums_ref[level]
        for i in range(len(copies)):
            total = total + from_sums[first + i]
        sums_ref[level + 1] = total

    near = [sibling] + y_peers + y_others
    near_copies = sum_sends(0, 0, near)

    wait_all(a_copies)

    @pl.loop(0, 4)
    def _(c):
        done = []
        for j in range(PART_A):
            total = a_ref[1, y_lo, c, j].astype(F32)
            for i in range(3):
                total = total + a_from_y[i, c, j].astype(F32)
            done.append(total.astype(BF16))
        for j in range(PART_A):
            a_sum[c, j] = done[j]

    copies = []
    for i, c in enumerate(z_coords):
        copies.append(send(a_sum.at[c], a_from_z.at[i], a2_send.at[i], a2_recv.at[i], z_peers[i]))
    wait_all(b_copies)
    spots = [(k, l, j) for k in range(2) for l in range(2) for j in range(PART_B)]
    done = []
    for k, l, j in spots:
        total = b_ref[k, z, l, j].astype(F32)
        for i in range(3):
            total = total + b_from_z[k, i, l, j].astype(F32)
        done.append(total.astype(BF16))
    for (k, l, j), value in zip(spots, done):
        b_sum[k, l, j] = value
    for i, (k, l) in enumerate([(0, y_lo), (0, 1 - y_lo), (1, 1 - y_lo)]):
        copies.append(send(b_sum.at[k, l], b_from_y.at[i], b2_send.at[i], b2_recv.at[i], y_peers[i]))
    sum_up(0, 0, near_copies)
    far_copies = sum_sends(1, len(near), z_peers)
    wait_all(copies)
    density = []
    for j in range(PARTS):
        if j < PART_A:
            total = a_sum[z, j].astype(F32)
            for i in range(3):
                total = total + a_from_z[i, j].astype(F32)
        else:
            total = b_sum[1, y_lo, j - PART_A].astype(F32)
            for i in range(3):
                total = total + b_from_y[i, j - PART_A].astype(F32)
        density.append(total)
    sum_up(1, len(near), far_copies)

    cells = 1.0 / (N1 * N2 * N3)
    totals = jnp.broadcast_to(jnp.sum(sums_ref[2], axis=1, keepdims=True) * cells, (16, LANES))
    gram = {pair: totals[k : k + 1] for k, pair in enumerate(pairs)}
    rhs = [totals[len(pairs) + p : len(pairs) + p + 1] for p in range(perts)]
    factor = {}
    for p in range(perts):
        for q in range(p + 1):
            value = gram[p, q]
            for k in range(q):
                value = value - factor[p, k] * factor[q, k]
            factor[p, q] = jnp.sqrt(value) if p == q else value / factor[q, q]
    coeffs = []
    for p in range(perts):
        value = rhs[p]
        for k in range(p):
            value = value - factor[p, k] * coeffs[k]
        coeffs.append(value / factor[p, p])
    for p in reversed(range(perts)):
        value = coeffs[p]
        for k in range(p + 1, perts):
            value = value - factor[k, p] * coeffs[k]
        coeffs[p] = value / factor[p, p]
    for j in range(PARTS):
        value = density[j]
        for p in range(perts):
            value = value - coeffs[p] * pot(p, j)
        out_ref[:, j * LANES : (j + 1) * LANES] = value
    projected_ref[...] = jnp.concatenate(rhs + rhs, axis=0)


def cost(flops, moved):
    return pl.CostEstimate(flops=int(flops), bytes_accessed=int(moved), transcendentals=0)


def params(collective=None):
    if collective is None:
        return pltpu.CompilerParams(vmem_limit_bytes=LIMIT)
    return pltpu.CompilerParams(vmem_limit_bytes=LIMIT, collective_id=collective, has_side_effects=True)


def shape(dims, kind):
    return jax.ShapeDtypeStruct(dims, kind)


def sems(*dims):
    return [pltpu.SemaphoreType.DMA(dims)] * 2


def start_of(coefs, wave_map, pot, slabs):
    bands, npw = coefs.shape
    block = (slabs, bands // slabs, npw)
    return pl.pallas_call(
        start_kernel,
        out_shape=(
            shape((slabs, 8, npw + 2 * WIN), F32),
            shape((slabs, 1, LANES), jnp.int32),
            shape(pot.shape, BF16),
        ),
        in_specs=[VMEM] * 3,
        out_specs=(VMEM, VMEM, VMEM),
        scratch_shapes=[
            pltpu.VMEM(block, BF16),
            pltpu.VMEM((1, npw + LANES), jnp.int32),
            pltpu.VMEM(block, BF16),
            pltpu.VMEM((slabs, 1, npw + LANES), jnp.int32),
        ]
        + sems(2, slabs - 1),
        compiler_params=params(1),
        name="start",
    )(coefs, wave_map.reshape(npw // LANES, LANES), pot)


def zy_of(starts, data, tab):
    return pl.pallas_call(
        zy_kernel,
        out_shape=shape((N2, N1, 2 * LANES), BF16),
        in_specs=[SMEM] + [VMEM] * 2,
        out_specs=VMEM,
        scratch_shapes=[pltpu.VMEM((N1, 2 * N2, N3), BF16)],
        compiler_params=params(),
        cost_estimate=cost(2e10, 8e6),
        name="scatter_zy",
    )(starts, data, tab)


def dense_of(turned, pot, far, coefs, tab, slabs):
    bands, npw = coefs.shape
    return pl.pallas_call(
        dense_kernel,
        out_shape=(
            shape((N2, N1, 2 * LANES), BF16),
            shape((N1, N2, 2 * LANES), BF16),
            shape((2, 4, bands, npw // QUARTERS), BF16),
        ),
        in_specs=[VMEM] * 5,
        out_specs=(VMEM, VMEM, VMEM),
        scratch_shapes=[
            pltpu.VMEM((slabs,) + pot.shape, BF16),
        ]
        + sems(2)
        + sems(7),
        compiler_params=params(4),
        cost_estimate=cost(2e10, 8e6),
        name="dense",
    )(turned, pot, far, coefs, tab)


def gather_of(starts, data, back, tab, npw):
    slabs = data.shape[0]
    return pl.pallas_call(
        gather_kernel,
        out_shape=shape((slabs, QUARTERS, 2, npw // QUARTERS), BF16),
        in_specs=[SMEM] + [VMEM] * 3,
        out_specs=VMEM,
        scratch_shapes=[pltpu.VMEM((slabs, 2, data.shape[2]), F32)],
        compiler_params=params(),
        cost_estimate=cost(2e10, 8e6),
        name="gather",
    )(starts, data, back, tab)


def middle_of(waves, bands, index, energies):
    slabs, quarters, two, part = waves.shape
    peers = slabs * quarters - 1
    small = (slabs * quarters * two // 2, LANES)
    longer = pltpu.VMEM((slabs, quarters, two, part + LANES), BF16)
    return pl.pallas_call(
        middle_kernel,
        out_shape=(shape(index.shape, F32), shape((8, LANES), F32)),
        in_specs=[VMEM] * 3 + [SMEM],
        out_specs=(VMEM, VMEM),
        scratch_shapes=[
            pltpu.VMEM(waves.shape, BF16),
            pltpu.VMEM((peers,) + small, F32),
            longer,
            longer,
            pltpu.VMEM(small, F32),
        ]
        + sems(3, peers),
        compiler_params=params(2),
        name="middle",
    )(waves, bands, index, energies)


def end_of(turned, psi, step, pot, tab, slabs, perts):
    planes, cross = pot.shape
    width = cross // 8
    tile = (planes, LANES)
    return pl.pallas_call(
        end_kernel,
        out_shape=(shape((planes, width), F32), shape((8, LANES), F32)),
        in_specs=[VMEM] * 5,
        out_specs=(VMEM, VMEM),
        scratch_shapes=[
            pltpu.VMEM((slabs, 8 * PARTS) + tile, BF16),
            pltpu.VMEM((2, 2, 4 * PARTS) + tile, BF16),
            pltpu.VMEM((2, 2, 4, PART_A) + tile, BF16),
            pltpu.VMEM((2, 4, 2, PART_B) + tile, BF16),
            pltpu.VMEM((3, 4, PART_A) + tile, BF16),
            pltpu.VMEM((2, 3, 2, PART_B) + tile, BF16),
            pltpu.VMEM((4, PART_A) + tile, BF16),
            pltpu.VMEM((2, 2, PART_B) + tile, BF16),
            pltpu.VMEM((3, PART_A) + tile, BF16),
            pltpu.VMEM((3, PART_B) + tile, BF16),
            pltpu.VMEM((perts, planes, width), F32),
            pltpu.VMEM((3, 16, LANES), F32),
            pltpu.VMEM((10, 16, LANES), F32),
        ]
        + sems(2, 2)
        + sems(3)
        + sems(3)
        + sems(2, 3)
        + sems(3)
        + sems(3)
        + sems(10),
        compiler_params=params(3),
        name="density",
    )(turned, psi, step, pot, tab)


def next_chip():
    pairs = []
    for band in range(8):
        for slab in range(4):
            core = slab % 2
            to = (band // 4 * 2 + slab // 2 + 2 * core - 1) % 4
            pairs.append((band * 4 + slab, (to // 2 * 4 + band % 4) * 4 + to % 2 * 2 + core))
    return pairs


def per_device(wave_coeffs, band_energies, trial_potentials, wave_map):
    slabs = lax.axis_size("slab")
    npw = wave_coeffs.shape[1]
    planes, cross = trial_potentials.shape[1:]
    tab = cosines(N1)
    pot = trial_potentials.reshape(planes, cross)
    data, starts, narrow = start_of(wave_coeffs, wave_map, pot, slabs)
    far = lax.ppermute(narrow, ("band", "slab"), next_chip())
    turned = zy_of(starts, data, tab)
    psi, back, all_bands = dense_of(turned, narrow, far, wave_coeffs, tab, slabs)
    waves = gather_of(starts, data, back, tab, npw)
    data, step = middle_of(waves, all_bands, data, band_energies)
    turned = zy_of(starts, data, tab)
    residual, projected = end_of(turned, psi, step, pot, tab, slabs, lax.axis_size("pert"))
    return (residual.reshape(1, planes, -1), projected[: lax.axis_size("pert"), :1])


def solution(mesh):
    return jax.shard_map(
        per_device,
        mesh=mesh,
        in_specs=(P("band", "slab"), P("band"), P("pert", "slab", None), P("slab")),
        out_specs=(P("pert", "slab", "band"), P(None, "pert")),
        check_vma=False,
    )
```

```python
import jax
import jax.numpy as jnp
from jax import lax
from jax.experimental import pallas as pl
from jax.experimental.pallas import tpu as pltpu
from jax.sharding import PartitionSpec as P

N1 = 96
N2 = 96
N3 = 96
LANES = 128
WIN = 512
NEAR = WIN - LANES
TILE = 2
TILES = N1 // TILE
QUARTERS = 4
PART_A = 5
PART_B = 4
PARTS = PART_A + PART_B
F32 = jnp.float32
BF16 = jnp.bfloat16
NT = (((1,), (1,)), ((), ()))
MESH = pl.DeviceIdType.MESH


def cosines(n):
    rows = jnp.arange(n, dtype=jnp.int32).astype(jnp.float32)[:, None]
    cols = jnp.arange(n, dtype=jnp.int32).astype(jnp.float32)[None, :]
    table = jnp.sqrt(2.0 / n) * jnp.cos(jnp.pi * rows * (cols + 0.5) / n)
    table = table * jnp.where(rows == 0, jnp.sqrt(0.5), 1.0)
    return table.astype(jnp.bfloat16)


def dot(a, b):
    return jnp.dot(a, b, preferred_element_type=F32)


def dot_nt(a, b):
    return lax.dot_general(a, b, NT, preferred_element_type=F32)


def iota(dims, axis):
    return lax.broadcasted_iota(jnp.int32, dims, axis)


def ones_at(rows, cols):
    return (iota((rows, cols), 0) == iota((rows, cols), 1)).astype(F32).astype(BF16)


def transposed(table):
    return dot_nt(ones_at(table.shape[1], table.shape[1]), table).astype(BF16)


def window_base(starts_ref, s, tile):
    return pl.multiple_of((starts_ref[s, 0, tile] // LANES) * LANES, LANES)


def overflow(starts_ref, slabs):
    total = starts_ref[0, 0, TILES + 1]
    for s in range(1, slabs):
        total = total + starts_ref[s, 0, TILES + 1]
    return total > 0


def near_at(starts_ref, s, tile, i=0):
    first = starts_ref[s, 0, tile]
    base = (first // LANES) * LANES
    return pl.multiple_of(base + i * NEAR, LANES), first - base


def hot_rows(rows, tile, cells):
    at = rows[2:3] - (tile * cells).astype(F32)
    return iota((cells, rows.shape[1]), 0).astype(F32) == at


def hot_z(rows):
    here = iota((N3, rows.shape[1]), 0).astype(F32) == rows[3:4]
    return here.astype(F32).astype(BF16)


def scatter_window(data_ref, s, base, tile, cells):
    rows = data_ref[s, :, pl.ds(base, WIN)]
    hot = hot_rows(rows, tile, cells)
    both = [jnp.where(hot, rows[0:1], 0.0), jnp.where(hot, rows[1:2], 0.0)]
    return dot_nt(jnp.concatenate(both, axis=0).astype(BF16), hot_z(rows))


def plane_of(parts, t, ny):
    cells = TILE * ny
    rows = [p[b * cells + t * ny : b * cells + (t + 1) * ny] for b in range(2) for p in parts]
    return jnp.concatenate(rows, axis=0)


def tile_planes(starts_ref, data_ref, tile):
    slabs = data_ref.shape[0]
    ny = N2 // slabs
    parts = [
        scatter_window(data_ref, s, window_base(starts_ref, s, tile), tile, TILE * ny)
        for s in range(slabs)
    ]
    return [plane_of(parts, t, ny) for t in range(TILE)]


def more_planes(starts_ref, data_ref, tile):
    slabs = data_ref.shape[0]
    ny = N2 // slabs
    cells = TILE * ny
    parts = []
    for s in range(slabs):
        base = window_base(starts_ref, s, tile)

        def more(i, acc):
            at = pl.multiple_of(base + i * WIN, LANES)
            return acc + scatter_window(data_ref, s, at, tile, cells)

        windows = (starts_ref[s, 0, tile + 1] - base + WIN - 1) // WIN
        parts.append(lax.fori_loop(1, windows, more, jnp.zeros((2 * cells, N3), F32)))
    return [plane_of(parts, t, ny) for t in range(TILE)]


def zy_kernel(starts_ref, data_ref, tab_ref, turned_ref, plane_ref):
    inv_y = transposed(tab_ref[...])
    inv_z = dot(tab_ref[...], ones_at(N3, LANES)).astype(BF16)
    width = 32
    over = overflow(starts_ref, data_ref.shape[0])

    def transform(planes, first):
        done = []
        for plane in planes:
            z_done = dot(plane, inv_z).astype(BF16)
            done.append(dot(inv_y, jnp.concatenate([z_done[:N2], z_done[N2:]], axis=1)).astype(BF16))
        turned_ref[:, pl.ds(first, width), :] = jnp.swapaxes(jnp.stack(done, axis=0), 0, 1)

    @pl.when(jnp.logical_not(over))
    def _():
        @pl.loop(0, N1 // width)
        def _(group):
            first = pl.multiple_of(group * width, width)
            planes = []
            for u in range(width // TILE):
                tile = group * (width // TILE) + u
                planes += [plane.astype(BF16) for plane in tile_planes(starts_ref, data_ref, tile)]
            transform(planes, first)

    @pl.when(over)
    def _():
        @pl.loop(0, TILES)
        def _(tile):
            planes = tile_planes(starts_ref, data_ref, tile)
            added = more_planes(starts_ref, data_ref, tile)
            for t in range(TILE):
                plane_ref[tile * TILE + t] = (planes[t] + added[t]).astype(BF16)

        @pl.loop(0, N1 // width)
        def _(group):
            first = pl.multiple_of(group * width, width)
            transform([plane_ref[first + u] for u in range(width)], first)


def gather_window(data_ref, planes, s, at, tile):
    ny = N2 // data_ref.shape[0]
    cells = TILE * ny
    base, off = at
    rows = pltpu.roll(data_ref[s, :, pl.ds(base, WIN)], WIN - off, 1)[:, :NEAR]
    hot = hot_rows(rows, tile, cells)
    mine = [plane[b * N2 + s * ny : b * N2 + (s + 1) * ny] for b in range(2) for plane in planes]
    picked = dot(jnp.concatenate(mine, axis=0).astype(BF16), hot_z(rows))
    found = [
        jnp.sum(jnp.where(hot, picked[b * cells : (b + 1) * cells], 0.0), axis=0, keepdims=True)
        for b in range(2)
    ]
    found = jnp.concatenate(found + [jnp.zeros((6, NEAR), F32)], axis=0)
    found = jnp.concatenate([found, jnp.zeros((8, WIN - NEAR), F32)], axis=1)
    return pltpu.roll(found, off, 1)[:2]


def gather_kernel(starts_ref, data_ref, back_ref, tab_ref, out_ref, sum_ref):
    slabs = data_ref.shape[0]
    sum_ref[...] = jnp.zeros_like(sum_ref)
    fwd_z = dot_nt(ones_at(LANES, N3), tab_ref[...]).astype(BF16)
    several = 16

    def wave_planes(tile, count):
        done = []
        for t in range(count):
            y_done = dot(tab_ref[...], back_ref[tile * TILE + t]).astype(BF16)
            done += [y_done[:, :LANES], y_done[:, LANES:]]
        waves = dot(jnp.concatenate(done, axis=0), fwd_z)
        return [waves[2 * N2 * t : 2 * N2 * (t + 1)] for t in range(count)]

    @pl.loop(0, TILES // several)
    def _(group):
        all_planes = wave_planes(group * several, several * TILE)
        found = []
        for u in range(several):
            tile = group * several + u
            planes = all_planes[TILE * u : TILE * (u + 1)]
            for s in range(slabs):
                at = near_at(starts_ref, s, tile)
                found.append((s, at[0], gather_window(data_ref, planes, s, at, tile)))
        for s, base, value in found:
            sum_ref[s, :, pl.ds(base, WIN)] += value

    @pl.when(overflow(starts_ref, slabs))
    def _():
        @pl.loop(0, TILES)
        def _(tile):
            planes = wave_planes(tile, TILE)
            for s in range(slabs):
                count = starts_ref[s, 0, tile + 1] - starts_ref[s, 0, tile]

                @pl.loop(1, (count + NEAR - 1) // NEAR)
                def _(i):
                    at = near_at(starts_ref, s, tile, i)
                    sum_ref[s, :, pl.ds(at[0], WIN)] += gather_window(data_ref, planes, s, at, tile)

    part = out_ref.shape[3]
    for q in range(out_ref.shape[1]):
        out_ref[:, q] = sum_ref[:, :, q * part : (q + 1) * part].astype(out_ref.dtype)


SMEM = pl.BlockSpec(memory_space=pltpu.SMEM)
VMEM = pl.BlockSpec(memory_space=pltpu.VMEM)
LIMIT = 32 * 1024 * 1024


def greet(peers):
    for peer in peers:
        pl.semaphore_signal(pltpu.get_barrier_semaphore(), inc=1, device_id=peer, device_id_type=MESH)


def greeted(peers):
    pl.semaphore_wait(pltpu.get_barrier_semaphore(), len(peers))


def remote(src, dst, send_sem, recv_sem, peer):
    return pltpu.make_async_remote_copy(
        src_ref=src, dst_ref=dst, send_sem=send_sem, recv_sem=recv_sem, device_id=peer, device_id_type=MESH
    )


def send(src, dst, send_sem, recv_sem, peer):
    copy = remote(src, dst, send_sem, recv_sem, peer)
    copy.start()
    return copy


def wait_all(copies):
    for copy in copies:
        copy.wait()


def slab_peers(slabs):
    me = lax.axis_index("slab")
    return [lax.rem(me + d, slabs) for d in range(1, slabs)]


def place():
    band, slab = lax.axis_index("band"), lax.axis_index("slab")
    return band // 4, slab // 2, lax.rem(band, 4), lax.rem(slab, 2)


def device(y_hi, y_lo, z, core):
    return {"band": y_hi * 4 + z, "slab": y_lo * 2 + core}


def pairs_of(perts):
    return [(p, q) for p in range(perts) for q in range(p + 1)]


def total_of(one, two):
    total = sum(a * b for a, b in zip(one, two))
    total = total[0:8] + total[8:16] + total[16:24]
    return jnp.sum(total, axis=0, keepdims=True)


def start_kernel(
    coef_ref, map_ref, pot_ref, data_ref, starts_ref, narrow_ref, share_ref,
    own_coef, own_map, coefs_ref, maps_ref, send_sem, recv_sem,
):
    slabs, two, npw = coefs_ref.shape
    ny = N2 // slabs
    me = lax.axis_index("slab")
    peers = slab_peers(slabs)
    chunk = 1536
    greet([{"slab": peer} for peer in peers])
    for r in range(npw // LANES):
        own_map[0:1, r * LANES : (r + 1) * LANES] = map_ref[r : r + 1, :]
    for i in range(npw // chunk):
        at = pl.ds(i * chunk, chunk)
        block = coef_ref[:, at].astype(F32)
        for t in range(slabs):
            own_coef[t, :, at] = block[two * t : two * (t + 1)].astype(BF16)
    greeted(peers)
    coef_copies = []
    for i, peer in enumerate(peers):
        to = {"slab": peer}
        coef_copies.append(send(own_coef.at[peer], coefs_ref.at[me], send_sem.at[0, i], recv_sem.at[0, i], to))
    coefs_ref[me] = own_coef[me]
    edges = iota((56, LANES), 0) * (TILE * ny * N3)
    below = jnp.zeros((56, LANES), jnp.int32)
    for r in range(npw // LANES):
        below = below + (own_map[0:1, r * LANES : (r + 1) * LANES] < edges).astype(jnp.int32)
    count = jnp.sum(below.astype(F32), axis=1, keepdims=True)
    spread = jnp.where(iota((56, LANES), 0) == iota((56, LANES), 1), count, 0.0)
    starts = jnp.sum(spread, axis=0, keepdims=True).astype(jnp.int32)
    after = pltpu.roll(starts, LANES - 1, 1)
    lane = iota((1, LANES), 1)
    over = (after > starts + NEAR) & (lane < TILES)
    flag = jnp.max(over.astype(F32), axis=1, keepdims=True).astype(jnp.int32)
    own_map[0:1, npw : npw + LANES] = jnp.where(lane == TILES + 1, flag, starts)
    copies = []
    for i, peer in enumerate(peers):
        to = {"slab": peer}
        copies.append(send(own_map, maps_ref.at[me], send_sem.at[1, i], recv_sem.at[1, i], to))
    maps_ref[me] = own_map[...]
    data_ref[...] = jnp.full(data_ref.shape, -1.0, F32)
    narrow_ref[...] = pot_ref[...].astype(BF16)
    width = share_ref.shape[1]
    share_ref[...] = pot_ref[:, pl.ds(pl.multiple_of(lax.axis_index("band") * width, LANES), width)]
    wait_all(copies)
    for s in range(slabs):
        starts_ref[s] = maps_ref[s, :, npw : npw + LANES]
    y_first = (iota((slabs, 1), 0) * ny).astype(F32)
    for i in range(npw // chunk):
        at = pl.ds(i * chunk, chunk)
        cell = jnp.concatenate([maps_ref[s, :, at] for s in range(slabs)], axis=0).astype(F32)
        row = jnp.floor((cell + 0.5) * (1.0 / N3))
        zpos = cell - row * N3
        xpos = jnp.floor((row + 0.5) * (1.0 / ny))
        ypos = row - xpos * ny + y_first
        kin = 2.0 * (xpos * xpos / (N1 * N1) + ypos * ypos / (N2 * N2) + zpos * zpos / (N3 * N3))
        for s in range(slabs):
            lines = [part[s : s + 1] for part in (row, zpos, kin)]
            data_ref[s, 2:5, at] = jnp.concatenate(lines, axis=0)
    wait_all(coef_copies)
    for s in range(slabs):
        for i in range(npw // chunk):
            at = pl.ds(i * chunk, chunk)
            data_ref[s, 0:2, at] = coefs_ref[s, :, at].astype(F32)


def dense_kernel(
    turned_ref, pot_ref, far_ref, share_ref, coef_ref, tab_ref,
    psi_ref, back_ref, bands_ref, shares_ref, gram_ref,
    pots_ref, send_sem, recv_sem, coef_send, coef_recv, share_send, share_recv,
):
    slabs = pots_ref.shape[0]
    y_hi, y_lo, z, core = place()
    me = lax.axis_index("slab")
    distant = (1 - y_lo) * 2 + core
    sibling = device(y_hi, y_lo, z, 1 - core)
    steps = [(a, b) for a in range(2) for b in range(4) if a + b > 0]
    others = [(lax.rem(y_hi + a, 2), lax.rem(z + b, 4)) for a, b in steps]
    members = [device(a, y_lo, b, core) for a, b in others]
    perts = shares_ref.shape[0]
    pert = lax.axis_index("pert")
    p_peers = [{"pert": lax.rem(pert + d, perts)} for d in range(1, perts)]
    everyone = [sibling] + members + p_peers
    greet(everyone)
    part = bands_ref.shape[3]
    quarter = pl.ds(pl.multiple_of(lax.axis_index("pert") * part, LANES), part)
    bands_ref[y_hi, z] = coef_ref[:, quarter]
    pots_ref[me] = pot_ref[...]
    pots_ref[distant] = far_ref[...]
    shares_ref[pert] = share_ref[...]
    greeted(everyone)
    copies = []
    for i, member in enumerate(members):
        src = coef_ref.at[:, quarter]
        copies.append(send(src, bands_ref.at[y_hi, z], coef_send.at[i], coef_recv.at[i], member))
    near = [
        send(pot_ref, pots_ref.at[me], send_sem.at[0], recv_sem.at[0], sibling),
        send(far_ref, pots_ref.at[distant], send_sem.at[1], recv_sem.at[1], sibling),
    ]
    for i, peer in enumerate(p_peers):
        copies.append(send(share_ref, shares_ref.at[pert], share_send.at[i], share_recv.at[i], peer))

    inv_x = transposed(tab_ref[...])
    unroll = 16

    @pl.loop(0, N2 // unroll)
    def _(group):
        rows = [group * unroll + u for u in range(unroll)]
        done = [dot(inv_x, turned_ref[row]).astype(BF16) for row in rows]
        for row, value in zip(rows, done):
            psi_ref[row] = value

    wait_all(near)

    width = 16
    lane = iota((N1 // slabs, LANES), 1)

    @pl.loop(0, N2 // width)
    def _(group):
        first = pl.multiple_of(group * width, width)
        done = []
        for v in range(width // 4):
            quads = [[], [], [], []]
            for s in range(slabs):
                parts = []
                for j in range(3):
                    off = pl.multiple_of(group * (width * N3) + (3 * v + j) * LANES, LANES)
                    parts.append(pots_ref[s, :, pl.ds(off, LANES)].astype(F32))
                a, b, c = parts
                quads[0].append(a)
                quads[1].append(jnp.where(lane < 32, pltpu.roll(a, 32, 1), pltpu.roll(b, 32, 1)))
                quads[2].append(jnp.where(lane < 64, pltpu.roll(b, 64, 1), pltpu.roll(c, 64, 1)))
                quads[3].append(pltpu.roll(c, 96, 1))
            for u in range(4):
                pot = jnp.concatenate(quads[u], axis=0)
                psi = psi_ref[first + 4 * v + u].astype(F32)
                product = jnp.concatenate([pot * psi[:, :LANES], pot * psi[:, LANES:]], axis=1)
                done.append(dot(tab_ref[...], product.astype(BF16)).astype(BF16))
        back_ref[:, pl.ds(first, width), :] = jnp.swapaxes(jnp.stack(done, axis=0), 0, 1)

    wait_all(copies)
    parts = [[shares_ref[p, :, j * LANES : (j + 1) * LANES] for j in range(PARTS)] for p in range(perts)]
    sums = [total_of(parts[p], parts[q]) for p, q in pairs_of(perts)]
    sums.append(jnp.zeros((16 - len(sums), LANES), F32))
    gram_ref[...] = jnp.concatenate(sums, axis=0)


def middle_kernel(
    waves_ref, bands_ref, index_ref, energy_ref, data_ref, step_ref,
    got_ref, corr_ref, rhs_ref, back_ref, total_ref, send_sem, recv_sem,
):
    slabs, quarters, two, part = waves_ref.shape
    half, zs, bands, _ = bands_ref.shape
    chunk = 1152
    pert, slab = lax.axis_index("pert"), lax.axis_index("slab")
    steps = [(a, b) for a in range(quarters) for b in range(slabs) if a + b > 0]
    others = [(lax.rem(pert + a, quarters), lax.rem(slab + b, slabs)) for a, b in steps]
    peers = [{"pert": c, "slab": t} for c, t in others]
    greet(peers)
    greeted(peers)
    copies = []
    for i, (c, t) in enumerate(others):
        src, dst = waves_ref.at[t, c], got_ref.at[pert, slab]
        copies.append(send(src, dst, send_sem.at[0, i], recv_sem.at[0, i], peers[i]))
    got_ref[pert, slab] = waves_ref[slab, pert]
    data_ref[...] = index_ref[...]
    wait_all(copies)

    def waves_at(at):
        parts = [got_ref[c, t, :, at].astype(F32) for c in range(quarters) for t in range(slabs)]
        return jnp.concatenate(parts, axis=0)

    def bands_at(at):
        parts = [bands_ref[a, c, :, at].astype(F32) for a in range(half) for c in range(zs)]
        return jnp.concatenate(parts, axis=0).astype(BF16)

    rows, count = quarters * slabs * two, half * zs * bands
    total = jnp.zeros((rows, count), F32)
    for i in range(part // chunk):
        at = pl.ds(i * chunk, chunk)
        total = total + dot_nt(waves_at(at).astype(BF16), bands_at(at))
    total_ref[...] = jnp.concatenate([total[: rows // 2], total[rows // 2 :]], axis=1)

    copies = []
    for i, peer in enumerate(peers):
        copies.append(send(total_ref, corr_ref.at[i], send_sem.at[1, i], recv_sem.at[1, i], peer))
    wait_all(copies)
    total = total_ref[...]
    for i in range(len(peers)):
        total = total + corr_ref[i]
    correlation = jnp.concatenate([total[:, :count], total[:, count:]], axis=0).astype(BF16)

    overlap = jnp.zeros((rows, rows), F32)
    for i in range(part // chunk):
        at = pl.ds(i * chunk, chunk)
        waves = waves_at(at)
        rhs = (waves - dot(correlation, bands_at(at))).astype(BF16)
        overlap = overlap + dot_nt(rhs, waves.astype(BF16))
        rhs = rhs.astype(F32)
        for c in range(quarters):
            for t in range(slabs):
                first = two * (c * slabs + t)
                rhs_ref[c, t, :, at] = rhs[first : first + two].astype(BF16)
    own = rows // quarters
    same = lax.rem(iota((rows, rows), 0), own) == lax.rem(iota((rows, rows), 1), own)
    kept = jnp.where(same, overlap, 0.0)
    lane = iota((rows, LANES), 1)
    tail = jnp.zeros((rows, LANES), F32)
    for p in range(quarters):
        mine = jnp.sum(kept[:, p * own : (p + 1) * own], axis=1, keepdims=True)
        high = mine.astype(BF16).astype(F32)
        tail = jnp.where(lane == p, high, tail)
        tail = jnp.where(lane == quarters + p, mine - high, tail)
    for c in range(quarters):
        for t in range(slabs):
            first = two * (c * slabs + t)
            rhs_ref[c, t, :, part:] = tail[first : first + two].astype(BF16)

    copies = []
    for i, (c, t) in enumerate(others):
        src, dst = rhs_ref.at[c, t], back_ref.at[slab, pert]
        copies.append(send(src, dst, send_sem.at[2, i], recv_sem.at[2, i], peers[i]))
    back_ref[slab, pert] = rhs_ref[pert, slab]
    wait_all(copies)

    numer = jnp.zeros((two, chunk), F32)
    denom = jnp.zeros((two, chunk), F32)
    tail = jnp.zeros((two, LANES), F32)
    energy = [jnp.full((1, chunk), energy_ref[slab * two + b], F32) for b in range(two)]
    energy = jnp.concatenate(energy, axis=0)
    for s in range(slabs):
        for q in range(quarters):
            tail = tail + back_ref[s, q, :, part:].astype(F32)
            for i in range(part // chunk):
                at = pl.ds(q * part + i * chunk, chunk)
                mine = back_ref[s, q, :, i * chunk : (i + 1) * chunk].astype(F32)
                data_ref[s, 0:2, at] = mine
                squares = mine * mine
                numer = numer + squares
                denom = denom + (index_ref[s, 4:5, at] - energy) * squares
    step = -jnp.sum(numer, axis=1, keepdims=True) / jnp.sum(denom, axis=1, keepdims=True)
    step = step * (4.0 * N1 * N2 * N3 / count)
    tail = step * (tail + pltpu.roll(tail, LANES - quarters, 1))
    tail = jnp.sum(tail, axis=0, keepdims=True)
    wide = jnp.broadcast_to(step, (two, LANES))
    step_ref[...] = jnp.concatenate([wide, tail, jnp.zeros((8 - two - 1, LANES), F32)], axis=0)


def end_kernel(
    turned_ref, psi_ref, step_ref, pots_ref, gram_ref, tab_ref, out_ref, projected_ref,
    dens_ref, from_core, a_ref, b_ref, a_from_y, b_from_z, a_sum, b_sum, a_from_z, b_from_y,
    sums_ref, from_sums, core_send, core_recv, a_send, a_recv, b_send, b_recv,
    a2_send, a2_recv, b2_send, b2_recv, sum_send, sum_recv,
):
    perts, planes, _ = pots_ref.shape
    slabs = dens_ref.shape[0]
    y_hi, y_lo, z, core = place()
    sibling = device(y_hi, y_lo, z, 1 - core)
    y_coords = [(1 - y_hi, y_lo), (1 - y_hi, 1 - y_lo), (y_hi, 1 - y_lo)]
    y_peers = [device(a, b, z, core) for a, b in y_coords]
    y_others = [device(a, b, z, 1 - core) for a, b in y_coords]
    z_coords = [lax.rem(z + d, 4) for d in range(1, 4)]
    z_peers = [device(y_hi, y_lo, c, core) for c in z_coords]
    everyone = [sibling] + y_peers + y_others + z_peers
    greet(everyone)
    pairs = pairs_of(perts)
    line = iota((1, LANES), 1)
    sums = [gram_ref[0 : len(pairs)]]
    sums += [jnp.where(line == p, step_ref[2:3], 0.0) for p in range(perts)]
    sums.append(jnp.zeros((16 - len(pairs) - perts, LANES), F32))
    sums_ref[0] = jnp.concatenate(sums, axis=0)

    inv_x = transposed(tab_ref[...])
    lane = iota((N1, LANES), 1)
    half = 4 * PARTS

    def density_part(h, first, last):
        @pl.loop(first, last)
        def _(group):
            done = []
            for v in range(4):
                quad = h * 12 + group * 4 + v
                parts = []
                for u in range(4):
                    row = quad * 4 + u
                    field = dot(inv_x, turned_ref[row]).astype(BF16).astype(F32)
                    terms = psi_ref[row].astype(F32) * field
                    parts.append(step_ref[0:1] * terms[:, :LANES] + step_ref[1:2] * terms[:, LANES:])
                one, two, three = [pltpu.roll(parts[u], LANES - 32 * u, 1) for u in (1, 2, 3)]
                tiles = [
                    jnp.where(lane < 96, parts[0], one),
                    jnp.where(lane < 64, one, two),
                    jnp.where(lane < 32, two, three),
                ]
                done += [(quad * 3 + j, tile) for j, tile in enumerate(tiles)]
            for at, tile in done:
                for s in range(slabs):
                    dens_ref[s, at] = tile[s * planes : (s + 1) * planes].astype(BF16)

    halves = [1 - y_hi, y_hi]
    core_copies, a_copies, b_copies = [], [], []

    def to_sibling(k):
        h = halves[k]
        for l in range(2):
            src = dens_ref.at[l * 2 + 1 - core, pl.ds(h * half, half)]
            core_copies.append(
                send(src, from_core.at[k, l], core_send.at[k, l], core_recv.at[k, l], sibling)
            )

    def to_others(k):
        h = halves[k]
        wait_all(core_copies[2 * k : 2 * k + 2])
        for l in range(2):
            @pl.loop(0, 4)
            def _(c):
                done = []
                for j in range(PARTS):
                    at = c * PARTS + j
                    total = dens_ref[l * 2 + core, h * half + at].astype(F32) + from_core[k, l, at].astype(F32)
                    done.append(total.astype(BF16))
                for j in range(PARTS):
                    if j < PART_A:
                        a_ref[k, l, c, j] = done[j]
                    else:
                        b_ref[k, c, l, j - PART_A] = done[j]
        targets = [(0, y_lo), (1, 1 - y_lo)] if k == 0 else [(2, 1 - y_lo)]
        for i, l in targets:
            a_copies.append(send(a_ref.at[k, l], a_from_y.at[i], a_send.at[i], a_recv.at[i], y_peers[i]))
        for i, c in enumerate(z_coords):
            b_copies.append(
                send(b_ref.at[k, c], b_from_z.at[k, i], b_send.at[k, i], b_recv.at[k, i], z_peers[i])
            )

    def sum_sends(level, first, group):
        copies = []
        for i, peer in enumerate(group):
            k = first + i
            copies.append(send(sums_ref.at[level], from_sums.at[k], sum_send.at[k], sum_recv.at[k], peer))
        return copies

    def sum_up(level, first, copies):
        wait_all(copies)
        total = sums_ref[level]
        for i in range(len(copies)):
            total = total + from_sums[first + i]
        sums_ref[level + 1] = total

    density_part(halves[0], 0, 3)
    greeted(everyone)
    to_sibling(0)
    near = [sibling] + y_peers + y_others
    near_copies = sum_sends(0, 0, near)
    density_part(halves[1], 0, 1)
    to_others(0)
    density_part(halves[1], 1, 3)
    to_sibling(1)

    def pot(p, j):
        return pots_ref[p, :, j * LANES : (j + 1) * LANES]

    to_others(1)

    sum_up(0, 0, near_copies)
    far_copies = sum_sends(1, len(near), z_peers)
    wait_all(a_copies)

    @pl.loop(0, 4)
    def _(c):
        done = []
        for j in range(PART_A):
            total = a_ref[1, y_lo, c, j].astype(F32)
            for i in range(3):
                total = total + a_from_y[i, c, j].astype(F32)
            done.append(total.astype(BF16))
        for j in range(PART_A):
            a_sum[c, j] = done[j]

    copies = []
    for i, c in enumerate(z_coords):
        copies.append(send(a_sum.at[c], a_from_z.at[i], a2_send.at[i], a2_recv.at[i], z_peers[i]))
    wait_all(b_copies)
    spots = [(k, l, j) for k in range(2) for l in range(2) for j in range(PART_B)]
    done = []
    for k, l, j in spots:
        total = b_ref[k, z, l, j].astype(F32)
        for i in range(3):
            total = total + b_from_z[k, i, l, j].astype(F32)
        done.append(total.astype(BF16))
    for (k, l, j), value in zip(spots, done):
        b_sum[k, l, j] = value
    for i, (k, l) in enumerate([(0, y_lo), (0, 1 - y_lo), (1, 1 - y_lo)]):
        copies.append(send(b_sum.at[k, l], b_from_y.at[i], b2_send.at[i], b2_recv.at[i], y_peers[i]))
    wait_all(copies)
    density = []
    for j in range(PARTS):
        if j < PART_A:
            total = a_sum[z, j].astype(F32)
            for i in range(3):
                total = total + a_from_z[i, j].astype(F32)
        else:
            total = b_sum[1, y_lo, j - PART_A].astype(F32)
            for i in range(3):
                total = total + b_from_y[i, j - PART_A].astype(F32)
        density.append(total)
    sum_up(1, len(near), far_copies)

    cells = 1.0 / (N1 * N2 * N3)
    totals = jnp.broadcast_to(jnp.sum(sums_ref[2], axis=1, keepdims=True) * cells, (16, LANES))
    gram = {pair: totals[k : k + 1] for k, pair in enumerate(pairs)}
    rhs = [totals[len(pairs) + p : len(pairs) + p + 1] for p in range(perts)]
    factor = {}
    for p in range(perts):
        for q in range(p + 1):
            value = gram[p, q]
            for k in range(q):
                value = value - factor[p, k] * factor[q, k]
            factor[p, q] = jnp.sqrt(value) if p == q else value / factor[q, q]
    coeffs = []
    for p in range(perts):
        value = rhs[p]
        for k in range(p):
            value = value - factor[p, k] * coeffs[k]
        coeffs.append(value / factor[p, p])
    for p in reversed(range(perts)):
        value = coeffs[p]
        for k in range(p + 1, perts):
            value = value - factor[k, p] * coeffs[k]
        coeffs[p] = value / factor[p, p]
    for j in range(PARTS):
        value = density[j]
        for p in range(perts):
            value = value - coeffs[p] * pot(p, j)
        out_ref[:, j * LANES : (j + 1) * LANES] = value
    projected_ref[...] = jnp.concatenate(rhs + rhs, axis=0)


def cost(flops, moved):
    return pl.CostEstimate(flops=int(flops), bytes_accessed=int(moved), transcendentals=0)


def params(collective=None):
    if collective is None:
        return pltpu.CompilerParams(vmem_limit_bytes=LIMIT)
    return pltpu.CompilerParams(vmem_limit_bytes=LIMIT, collective_id=collective, has_side_effects=True)


def shape(dims, kind):
    return jax.ShapeDtypeStruct(dims, kind)


def sems(*dims):
    return [pltpu.SemaphoreType.DMA(dims)] * 2


def start_of(coefs, wave_map, pot, slabs):
    bands, npw = coefs.shape
    block = (slabs, bands // slabs, npw)
    return pl.pallas_call(
        start_kernel,
        out_shape=(
            shape((slabs, 8, npw + 2 * WIN), F32),
            shape((slabs, 1, LANES), jnp.int32),
            shape(pot.shape, BF16),
            shape((pot.shape[0], pot.shape[1] // 8), F32),
        ),
        in_specs=[VMEM] * 3,
        out_specs=(VMEM,) * 4,
        scratch_shapes=[
            pltpu.VMEM(block, BF16),
            pltpu.VMEM((1, npw + LANES), jnp.int32),
            pltpu.VMEM(block, BF16),
            pltpu.VMEM((slabs, 1, npw + LANES), jnp.int32),
        ]
        + sems(2, slabs - 1),
        compiler_params=params(1),
        name="start",
    )(coefs, wave_map.reshape(npw // LANES, LANES), pot)


def zy_of(starts, data, tab):
    return pl.pallas_call(
        zy_kernel,
        out_shape=shape((N2, N1, 2 * LANES), BF16),
        in_specs=[SMEM] + [VMEM] * 2,
        out_specs=VMEM,
        scratch_shapes=[pltpu.VMEM((N1, 2 * N2, N3), BF16)],
        compiler_params=params(),
        cost_estimate=cost(2e10, 8e6),
        name="scatter_zy",
    )(starts, data, tab)


def dense_of(turned, pot, far, share, coefs, tab, slabs, perts):
    bands, npw = coefs.shape
    return pl.pallas_call(
        dense_kernel,
        out_shape=(
            shape((N2, N1, 2 * LANES), BF16),
            shape((N1, N2, 2 * LANES), BF16),
            shape((2, 4, bands, npw // QUARTERS), BF16),
            shape((perts,) + share.shape, F32),
            shape((16, LANES), F32),
        ),
        in_specs=[VMEM] * 6,
        out_specs=(VMEM,) * 5,
        scratch_shapes=[
            pltpu.VMEM((slabs,) + pot.shape, BF16),
        ]
        + sems(2)
        + sems(7)
        + sems(perts - 1),
        compiler_params=params(4),
        cost_estimate=cost(2e10, 8e6),
        name="dense",
    )(turned, pot, far, share, coefs, tab)


def gather_of(starts, data, back, tab, npw):
    slabs = data.shape[0]
    return pl.pallas_call(
        gather_kernel,
        out_shape=shape((slabs, QUARTERS, 2, npw // QUARTERS), BF16),
        in_specs=[SMEM] + [VMEM] * 3,
        out_specs=VMEM,
        scratch_shapes=[pltpu.VMEM((slabs, 2, data.shape[2]), F32)],
        compiler_params=params(),
        cost_estimate=cost(2e10, 8e6),
        name="gather",
    )(starts, data, back, tab)


def middle_of(waves, bands, index, energies):
    slabs, quarters, two, part = waves.shape
    peers = slabs * quarters - 1
    small = (slabs * quarters * two // 2, LANES)
    longer = pltpu.VMEM((slabs, quarters, two, part + LANES), BF16)
    return pl.pallas_call(
        middle_kernel,
        out_shape=(shape(index.shape, F32), shape((8, LANES), F32)),
        in_specs=[VMEM] * 3 + [SMEM],
        out_specs=(VMEM, VMEM),
        scratch_shapes=[
            pltpu.VMEM(waves.shape, BF16),
            pltpu.VMEM((peers,) + small, F32),
            longer,
            longer,
            pltpu.VMEM(small, F32),
        ]
        + sems(3, peers),
        compiler_params=params(2),
        name="middle",
    )(waves, bands, index, energies)


def end_of(turned, psi, step, pots, gram, tab, slabs):
    _, planes, width = pots.shape
    tile = (planes, LANES)
    return pl.pallas_call(
        end_kernel,
        out_shape=(shape((planes, width), F32), shape((8, LANES), F32)),
        in_specs=[VMEM] * 6,
        out_specs=(VMEM, VMEM),
        scratch_shapes=[
            pltpu.VMEM((slabs, 8 * PARTS) + tile, BF16),
            pltpu.VMEM((2, 2, 4 * PARTS) + tile, BF16),
            pltpu.VMEM((2, 2, 4, PART_A) + tile, BF16),
            pltpu.VMEM((2, 4, 2, PART_B) + tile, BF16),
            pltpu.VMEM((3, 4, PART_A) + tile, BF16),
            pltpu.VMEM((2, 3, 2, PART_B) + tile, BF16),
            pltpu.VMEM((4, PART_A) + tile, BF16),
            pltpu.VMEM((2, 2, PART_B) + tile, BF16),
            pltpu.VMEM((3, PART_A) + tile, BF16),
            pltpu.VMEM((3, PART_B) + tile, BF16),
            pltpu.VMEM((3, 16, LANES), F32),
            pltpu.VMEM((10, 16, LANES), F32),
        ]
        + sems(2, 2)
        + sems(3)
        + sems(2, 3)
        + sems(3)
        + sems(3)
        + sems(10),
        compiler_params=params(3),
        name="density",
    )(turned, psi, step, pots, gram, tab)


def next_chip():
    pairs = []
    for band in range(8):
        for slab in range(4):
            core = slab % 2
            to = (band // 4 * 2 + slab // 2 + 2 * core - 1) % 4
            pairs.append((band * 4 + slab, (to // 2 * 4 + band % 4) * 4 + to % 2 * 2 + core))
    return pairs


def per_device(wave_coeffs, band_energies, trial_potentials, wave_map):
    slabs = lax.axis_size("slab")
    npw = wave_coeffs.shape[1]
    planes, cross = trial_potentials.shape[1:]
    tab = cosines(N1)
    pot = trial_potentials.reshape(planes, cross)
    data, starts, narrow, share = start_of(wave_coeffs, wave_map, pot, slabs)
    far = lax.ppermute(narrow, ("band", "slab"), next_chip())
    turned = zy_of(starts, data, tab)
    perts = lax.axis_size("pert")
    psi, back, all_bands, pots, gram = dense_of(turned, narrow, far, share, wave_coeffs, tab, slabs, perts)
    waves = gather_of(starts, data, back, tab, npw)
    data, step = middle_of(waves, all_bands, data, band_energies)
    turned = zy_of(starts, data, tab)
    residual, projected = end_of(turned, psi, step, pots, gram, tab, slabs)
    return (residual.reshape(1, planes, -1), projected[:perts, :1])


def solution(mesh):
    return jax.shard_map(
        per_device,
        mesh=mesh,
        in_specs=(P("band", "slab"), P("band"), P("pert", "slab", None), P("slab")),
        out_specs=(P("pert", "slab", "band"), P(None, "pert")),
        check_vma=False,
    )
```

```python
import jax
import jax.numpy as jnp
from jax import lax
from jax.experimental import pallas as pl
from jax.experimental.pallas import tpu as pltpu
from jax.sharding import PartitionSpec as P

N1 = 96
N2 = 96
N3 = 96
LANES = 128
WIN = 512
NEAR = WIN - LANES
TILE = 2
TILES = N1 // TILE
QUARTERS = 4
PART_A = 5
PART_B = 4
PARTS = PART_A + PART_B
F32 = jnp.float32
BF16 = jnp.bfloat16
NT = (((1,), (1,)), ((), ()))
MESH = pl.DeviceIdType.MESH


def cosines(n):
    rows = jnp.arange(n, dtype=jnp.int32).astype(jnp.float32)[:, None]
    cols = jnp.arange(n, dtype=jnp.int32).astype(jnp.float32)[None, :]
    table = jnp.sqrt(2.0 / n) * jnp.cos(jnp.pi * rows * (cols + 0.5) / n)
    table = table * jnp.where(rows == 0, jnp.sqrt(0.5), 1.0)
    return table.astype(jnp.bfloat16)


def dot(a, b):
    return jnp.dot(a, b, preferred_element_type=F32)


def dot_nt(a, b):
    return lax.dot_general(a, b, NT, preferred_element_type=F32)


def iota(dims, axis):
    return lax.broadcasted_iota(jnp.int32, dims, axis)


def ones_at(rows, cols):
    return (iota((rows, cols), 0) == iota((rows, cols), 1)).astype(F32).astype(BF16)


def transposed(table):
    return dot_nt(ones_at(table.shape[1], table.shape[1]), table).astype(BF16)


def window_base(starts_ref, s, tile):
    return pl.multiple_of((starts_ref[s, 0, tile] // LANES) * LANES, LANES)


def overflow(starts_ref, slabs):
    total = starts_ref[0, 0, TILES + 1]
    for s in range(1, slabs):
        total = total + starts_ref[s, 0, TILES + 1]
    return total > 0


def near_at(starts_ref, s, tile, i=0):
    first = starts_ref[s, 0, tile]
    base = (first // LANES) * LANES
    return pl.multiple_of(base + i * NEAR, LANES), first - base


def hot_rows(rows, tile, cells):
    at = rows[2:3] - (tile * cells).astype(F32)
    return iota((cells, rows.shape[1]), 0).astype(F32) == at


def hot_z(rows):
    here = iota((N3, rows.shape[1]), 0).astype(F32) == rows[3:4]
    return here.astype(F32).astype(BF16)


def scatter_window(data_ref, s, base, tile, cells):
    rows = data_ref[s, :, pl.ds(base, WIN)]
    hot = hot_rows(rows, tile, cells)
    both = [jnp.where(hot, rows[0:1], 0.0), jnp.where(hot, rows[1:2], 0.0)]
    return dot_nt(jnp.concatenate(both, axis=0).astype(BF16), hot_z(rows))


def plane_of(parts, t, ny):
    cells = TILE * ny
    rows = [p[b * cells + t * ny : b * cells + (t + 1) * ny] for b in range(2) for p in parts]
    return jnp.concatenate(rows, axis=0)


def tile_planes(starts_ref, data_ref, tile):
    slabs = data_ref.shape[0]
    ny = N2 // slabs
    parts = [
        scatter_window(data_ref, s, window_base(starts_ref, s, tile), tile, TILE * ny)
        for s in range(slabs)
    ]
    return [plane_of(parts, t, ny) for t in range(TILE)]


def more_planes(starts_ref, data_ref, tile):
    slabs = data_ref.shape[0]
    ny = N2 // slabs
    cells = TILE * ny
    parts = []
    for s in range(slabs):
        base = window_base(starts_ref, s, tile)

        def more(i, acc):
            at = pl.multiple_of(base + i * WIN, LANES)
            return acc + scatter_window(data_ref, s, at, tile, cells)

        windows = (starts_ref[s, 0, tile + 1] - base + WIN - 1) // WIN
        parts.append(lax.fori_loop(1, windows, more, jnp.zeros((2 * cells, N3), F32)))
    return [plane_of(parts, t, ny) for t in range(TILE)]


def zy_kernel(starts_ref, data_ref, tab_ref, turned_ref, plane_ref):
    inv_y = transposed(tab_ref[...])
    inv_z = dot(tab_ref[...], ones_at(N3, LANES)).astype(BF16)
    width = 32
    over = overflow(starts_ref, data_ref.shape[0])

    def transform(planes, first):
        done = []
        for plane in planes:
            z_done = dot(plane, inv_z).astype(BF16)
            done.append(dot(inv_y, jnp.concatenate([z_done[:N2], z_done[N2:]], axis=1)).astype(BF16))
        turned_ref[:, pl.ds(first, width), :] = jnp.swapaxes(jnp.stack(done, axis=0), 0, 1)

    @pl.when(jnp.logical_not(over))
    def _():
        @pl.loop(0, N1 // width)
        def _(group):
            first = pl.multiple_of(group * width, width)
            planes = []
            for u in range(width // TILE):
                tile = group * (width // TILE) + u
                planes += [plane.astype(BF16) for plane in tile_planes(starts_ref, data_ref, tile)]
            transform(planes, first)

    @pl.when(over)
    def _():
        @pl.loop(0, TILES)
        def _(tile):
            planes = tile_planes(starts_ref, data_ref, tile)
            added = more_planes(starts_ref, data_ref, tile)
            for t in range(TILE):
                plane_ref[tile * TILE + t] = (planes[t] + added[t]).astype(BF16)

        @pl.loop(0, N1 // width)
        def _(group):
            first = pl.multiple_of(group * width, width)
            transform([plane_ref[first + u] for u in range(width)], first)


def gather_window(data_ref, planes, s, at, tile):
    ny = N2 // data_ref.shape[0]
    cells = TILE * ny
    base, off = at
    rows = pltpu.roll(data_ref[s, :, pl.ds(base, WIN)], WIN - off, 1)[:, :NEAR]
    hot = hot_rows(rows, tile, cells)
    mine = [plane[b * N2 + s * ny : b * N2 + (s + 1) * ny] for b in range(2) for plane in planes]
    picked = dot(jnp.concatenate(mine, axis=0).astype(BF16), hot_z(rows))
    found = [
        jnp.sum(jnp.where(hot, picked[b * cells : (b + 1) * cells], 0.0), axis=0, keepdims=True)
        for b in range(2)
    ]
    found = jnp.concatenate(found + [jnp.zeros((6, NEAR), F32)], axis=0)
    found = jnp.concatenate([found, jnp.zeros((8, WIN - NEAR), F32)], axis=1)
    return pltpu.roll(found, off, 1)[:2]


def gather_kernel(starts_ref, data_ref, back_ref, tab_ref, out_ref, sum_ref):
    slabs = data_ref.shape[0]
    sum_ref[...] = jnp.zeros_like(sum_ref)
    fwd_z = dot_nt(ones_at(LANES, N3), tab_ref[...]).astype(BF16)
    several = 16

    def wave_planes(tile, count):
        done = []
        for t in range(count):
            y_done = dot(tab_ref[...], back_ref[tile * TILE + t]).astype(BF16)
            done += [y_done[:, :LANES], y_done[:, LANES:]]
        waves = dot(jnp.concatenate(done, axis=0), fwd_z)
        return [waves[2 * N2 * t : 2 * N2 * (t + 1)] for t in range(count)]

    @pl.loop(0, TILES // several)
    def _(group):
        all_planes = wave_planes(group * several, several * TILE)
        found = []
        for u in range(several):
            tile = group * several + u
            planes = all_planes[TILE * u : TILE * (u + 1)]
            for s in range(slabs):
                at = near_at(starts_ref, s, tile)
                found.append((s, at[0], gather_window(data_ref, planes, s, at, tile)))
        for s, base, value in found:
            sum_ref[s, :, pl.ds(base, WIN)] += value

    @pl.when(overflow(starts_ref, slabs))
    def _():
        @pl.loop(0, TILES)
        def _(tile):
            planes = wave_planes(tile, TILE)
            for s in range(slabs):
                count = starts_ref[s, 0, tile + 1] - starts_ref[s, 0, tile]

                @pl.loop(1, (count + NEAR - 1) // NEAR)
                def _(i):
                    at = near_at(starts_ref, s, tile, i)
                    sum_ref[s, :, pl.ds(at[0], WIN)] += gather_window(data_ref, planes, s, at, tile)

    part = out_ref.shape[3]
    for q in range(out_ref.shape[1]):
        out_ref[:, q] = sum_ref[:, :, q * part : (q + 1) * part].astype(out_ref.dtype)


SMEM = pl.BlockSpec(memory_space=pltpu.SMEM)
VMEM = pl.BlockSpec(memory_space=pltpu.VMEM)
LIMIT = 32 * 1024 * 1024


def greet(peers):
    for peer in peers:
        pl.semaphore_signal(pltpu.get_barrier_semaphore(), inc=1, device_id=peer, device_id_type=MESH)


def greeted(peers):
    pl.semaphore_wait(pltpu.get_barrier_semaphore(), len(peers))


def remote(src, dst, send_sem, recv_sem, peer):
    return pltpu.make_async_remote_copy(
        src_ref=src, dst_ref=dst, send_sem=send_sem, recv_sem=recv_sem, device_id=peer, device_id_type=MESH
    )


def send(src, dst, send_sem, recv_sem, peer):
    copy = remote(src, dst, send_sem, recv_sem, peer)
    copy.start()
    return copy


def wait_all(copies):
    for copy in copies:
        copy.wait()


def slab_peers(slabs):
    me = lax.axis_index("slab")
    return [lax.rem(me + d, slabs) for d in range(1, slabs)]


def place():
    band, slab = lax.axis_index("band"), lax.axis_index("slab")
    return band // 4, slab // 2, lax.rem(band, 4), lax.rem(slab, 2)


def device(y_hi, y_lo, z, core):
    return {"band": y_hi * 4 + z, "slab": y_lo * 2 + core}


def pairs_of(perts):
    return [(p, q) for p in range(perts) for q in range(p + 1)]


def total_of(one, two):
    total = sum(a * b for a, b in zip(one, two))
    total = total[0:8] + total[8:16] + total[16:24]
    return jnp.sum(total, axis=0, keepdims=True)


def start_kernel(
    coef_ref, map_ref, pot_ref, data_ref, starts_ref, narrow_ref, share_ref,
    own_coef, own_map, coefs_ref, maps_ref, send_sem, recv_sem,
):
    slabs, two, npw = coefs_ref.shape
    ny = N2 // slabs
    me = lax.axis_index("slab")
    peers = slab_peers(slabs)
    chunk = 1536
    y_hi, y_lo, z, core = place()

    def around(step, other):
        to = lax.rem(y_hi * 2 + y_lo + step + 4, 4)
        return device(to // 2, lax.rem(to, 2), z, other)

    chips = [around(step, other) for step in (-1, 1) for other in (0, 1)]
    everyone = [device(y_hi, y_lo, z, 1 - core)] + chips
    greet(everyone)
    for r in range(npw // LANES):
        own_map[0:1, r * LANES : (r + 1) * LANES] = map_ref[r : r + 1, :]
    for i in range(npw // chunk):
        at = pl.ds(i * chunk, chunk)
        block = coef_ref[:, at].astype(F32)
        for t in range(slabs):
            own_coef[t, :, at] = block[two * t : two * (t + 1)].astype(BF16)
    greeted(everyone)
    coef_copies = []
    for i, peer in enumerate(peers):
        to = {"slab": peer}
        coef_copies.append(send(own_coef.at[peer], coefs_ref.at[me], send_sem.at[0, i], recv_sem.at[0, i], to))
    coefs_ref[me] = own_coef[me]
    edges = iota((56, LANES), 0) * (TILE * ny * N3)
    below = jnp.zeros((56, LANES), jnp.int32)
    for r in range(npw // LANES):
        below = below + (own_map[0:1, r * LANES : (r + 1) * LANES] < edges).astype(jnp.int32)
    count = jnp.sum(below.astype(F32), axis=1, keepdims=True)
    spread = jnp.where(iota((56, LANES), 0) == iota((56, LANES), 1), count, 0.0)
    starts = jnp.sum(spread, axis=0, keepdims=True).astype(jnp.int32)
    after = pltpu.roll(starts, LANES - 1, 1)
    lane = iota((1, LANES), 1)
    over = (after > starts + NEAR) & (lane < TILES)
    flag = jnp.max(over.astype(F32), axis=1, keepdims=True).astype(jnp.int32)
    own_map[0:1, npw : npw + LANES] = jnp.where(lane == TILES + 1, flag, starts)
    near = send(own_map, maps_ref.at[me], send_sem.at[1, 2], recv_sem.at[1, 2], everyone[0])
    copies = []
    for other in (0, 1):
        to = around(2 * core - 1, other)
        copies.append(send(own_map, maps_ref.at[me], send_sem.at[1, other], recv_sem.at[1, core], to))
    maps_ref[me] = own_map[...]
    data_ref[...] = jnp.full(data_ref.shape, -1.0, F32)
    narrow_ref[...] = pot_ref[...].astype(BF16)
    width = share_ref.shape[1]
    share_ref[...] = pot_ref[:, pl.ds(pl.multiple_of(lax.axis_index("band") * width, LANES), width)]
    near.wait()
    for other in (0, 1):
        copies[other].wait_send()
        slot = maps_ref.at[(1 - y_lo) * 2 + other]
        remote(own_map, slot, send_sem.at[1, other], recv_sem.at[1, other], everyone[0]).wait_recv()
    for s in range(slabs):
        starts_ref[s] = maps_ref[s, :, npw : npw + LANES]
    y_first = (iota((slabs, 1), 0) * ny).astype(F32)
    for i in range(npw // chunk):
        at = pl.ds(i * chunk, chunk)
        cell = jnp.concatenate([maps_ref[s, :, at] for s in range(slabs)], axis=0).astype(F32)
        row = jnp.floor((cell + 0.5) * (1.0 / N3))
        zpos = cell - row * N3
        xpos = jnp.floor((row + 0.5) * (1.0 / ny))
        ypos = row - xpos * ny + y_first
        kin = 2.0 * (xpos * xpos / (N1 * N1) + ypos * ypos / (N2 * N2) + zpos * zpos / (N3 * N3))
        for s in range(slabs):
            lines = [part[s : s + 1] for part in (row, zpos, kin)]
            data_ref[s, 2:5, at] = jnp.concatenate(lines, axis=0)
    wait_all(coef_copies)
    for s in range(slabs):
        for i in range(npw // chunk):
            at = pl.ds(i * chunk, chunk)
            data_ref[s, 0:2, at] = coefs_ref[s, :, at].astype(F32)


def dense_kernel(
    turned_ref, pot_ref, far_ref, share_ref, coef_ref, tab_ref,
    psi_ref, back_ref, bands_ref, shares_ref, gram_ref,
    pots_ref, send_sem, recv_sem, coef_send, coef_recv, share_send, share_recv,
):
    slabs = pots_ref.shape[0]
    y_hi, y_lo, z, core = place()
    me = lax.axis_index("slab")
    distant = (1 - y_lo) * 2 + core
    sibling = device(y_hi, y_lo, z, 1 - core)
    steps = [(a, b) for a in range(2) for b in range(4) if a + b > 0]
    others = [(lax.rem(y_hi + a, 2), lax.rem(z + b, 4)) for a, b in steps]
    members = [device(a, y_lo, b, core) for a, b in others]
    perts = shares_ref.shape[0]
    pert = lax.axis_index("pert")
    p_peers = [{"pert": lax.rem(pert + d, perts)} for d in range(1, perts)]
    everyone = [sibling] + members + p_peers
    greet(everyone)
    part = bands_ref.shape[3]
    quarter = pl.ds(pl.multiple_of(lax.axis_index("pert") * part, LANES), part)
    bands_ref[y_hi, z] = coef_ref[:, quarter]
    pots_ref[me] = pot_ref[...]
    pots_ref[distant] = far_ref[...]
    shares_ref[pert] = share_ref[...]
    greeted(everyone)
    copies = []
    for i, member in enumerate(members):
        src = coef_ref.at[:, quarter]
        copies.append(send(src, bands_ref.at[y_hi, z], coef_send.at[i], coef_recv.at[i], member))
    near = [
        send(pot_ref, pots_ref.at[me], send_sem.at[0], recv_sem.at[0], sibling),
        send(far_ref, pots_ref.at[distant], send_sem.at[1], recv_sem.at[1], sibling),
    ]
    for i, peer in enumerate(p_peers):
        copies.append(send(share_ref, shares_ref.at[pert], share_send.at[i], share_recv.at[i], peer))

    inv_x = transposed(tab_ref[...])
    unroll = 16

    @pl.loop(0, N2 // unroll)
    def _(group):
        rows = [group * unroll + u for u in range(unroll)]
        done = [dot(inv_x, turned_ref[row]).astype(BF16) for row in rows]
        for row, value in zip(rows, done):
            psi_ref[row] = value

    wait_all(near)

    width = 16
    lane = iota((N1 // slabs, LANES), 1)

    @pl.loop(0, N2 // width)
    def _(group):
        first = pl.multiple_of(group * width, width)
        done = []
        for v in range(width // 4):
            quads = [[], [], [], []]
            for s in range(slabs):
                parts = []
                for j in range(3):
                    off = pl.multiple_of(group * (width * N3) + (3 * v + j) * LANES, LANES)
                    parts.append(pots_ref[s, :, pl.ds(off, LANES)].astype(F32))
                a, b, c = parts
                quads[0].append(a)
                quads[1].append(jnp.where(lane < 32, pltpu.roll(a, 32, 1), pltpu.roll(b, 32, 1)))
                quads[2].append(jnp.where(lane < 64, pltpu.roll(b, 64, 1), pltpu.roll(c, 64, 1)))
                quads[3].append(pltpu.roll(c, 96, 1))
            for u in range(4):
                pot = jnp.concatenate(quads[u], axis=0)
                psi = psi_ref[first + 4 * v + u].astype(F32)
                product = jnp.concatenate([pot * psi[:, :LANES], pot * psi[:, LANES:]], axis=1)
                done.append(dot(tab_ref[...], product.astype(BF16)).astype(BF16))
        back_ref[:, pl.ds(first, width), :] = jnp.swapaxes(jnp.stack(done, axis=0), 0, 1)

    wait_all(copies)
    parts = [[shares_ref[p, :, j * LANES : (j + 1) * LANES] for j in range(PARTS)] for p in range(perts)]
    sums = [total_of(parts[p], parts[q]) for p, q in pairs_of(perts)]
    sums.append(jnp.zeros((16 - len(sums), LANES), F32))
    gram_ref[...] = jnp.concatenate(sums, axis=0)


def middle_kernel(
    waves_ref, bands_ref, index_ref, energy_ref, data_ref, step_ref,
    got_ref, corr_ref, rhs_ref, back_ref, total_ref, send_sem, recv_sem,
):
    slabs, quarters, two, part = waves_ref.shape
    half, zs, bands, _ = bands_ref.shape
    chunk = 1152
    pert, slab = lax.axis_index("pert"), lax.axis_index("slab")
    steps = [(a, b) for a in range(quarters) for b in range(slabs) if a + b > 0]
    others = [(lax.rem(pert + a, quarters), lax.rem(slab + b, slabs)) for a, b in steps]
    peers = [{"pert": c, "slab": t} for c, t in others]
    greet(peers)
    greeted(peers)
    copies = []
    for i, (c, t) in enumerate(others):
        src, dst = waves_ref.at[t, c], got_ref.at[pert, slab]
        copies.append(send(src, dst, send_sem.at[0, i], recv_sem.at[0, i], peers[i]))
    got_ref[pert, slab] = waves_ref[slab, pert]
    data_ref[...] = index_ref[...]
    wait_all(copies)

    def waves_at(at):
        parts = [got_ref[c, t, :, at].astype(F32) for c in range(quarters) for t in range(slabs)]
        return jnp.concatenate(parts, axis=0)

    def bands_at(at):
        parts = [bands_ref[a, c, :, at].astype(F32) for a in range(half) for c in range(zs)]
        return jnp.concatenate(parts, axis=0).astype(BF16)

    rows, count = quarters * slabs * two, half * zs * bands
    total = jnp.zeros((rows, count), F32)
    for i in range(part // chunk):
        at = pl.ds(i * chunk, chunk)
        total = total + dot_nt(waves_at(at).astype(BF16), bands_at(at))
    total_ref[...] = jnp.concatenate([total[: rows // 2], total[rows // 2 :]], axis=1).astype(BF16)

    copies = []
    for i, peer in enumerate(peers):
        copies.append(send(total_ref, corr_ref.at[i], send_sem.at[1, i], recv_sem.at[1, i], peer))
    wait_all(copies)
    total = total_ref[...].astype(F32)
    for i in range(len(peers)):
        total = total + corr_ref[i].astype(F32)
    correlation = jnp.concatenate([total[:, :count], total[:, count:]], axis=0).astype(BF16)

    overlap = jnp.zeros((rows, rows), F32)
    for i in range(part // chunk):
        at = pl.ds(i * chunk, chunk)
        waves = waves_at(at)
        rhs = (waves - dot(correlation, bands_at(at))).astype(BF16)
        overlap = overlap + dot_nt(rhs, waves.astype(BF16))
        rhs = rhs.astype(F32)
        for c in range(quarters):
            for t in range(slabs):
                first = two * (c * slabs + t)
                rhs_ref[c, t, :, at] = rhs[first : first + two].astype(BF16)
    own = rows // quarters
    same = lax.rem(iota((rows, rows), 0), own) == lax.rem(iota((rows, rows), 1), own)
    kept = jnp.where(same, overlap, 0.0)
    lane = iota((rows, LANES), 1)
    tail = jnp.zeros((rows, LANES), F32)
    for p in range(quarters):
        mine = jnp.sum(kept[:, p * own : (p + 1) * own], axis=1, keepdims=True)
        high = mine.astype(BF16).astype(F32)
        tail = jnp.where(lane == p, high, tail)
        tail = jnp.where(lane == quarters + p, mine - high, tail)
    for c in range(quarters):
        for t in range(slabs):
            first = two * (c * slabs + t)
            rhs_ref[c, t, :, part:] = tail[first : first + two].astype(BF16)

    copies = []
    for i, (c, t) in enumerate(others):
        src, dst = rhs_ref.at[c, t], back_ref.at[slab, pert]
        copies.append(send(src, dst, send_sem.at[2, i], recv_sem.at[2, i], peers[i]))
    back_ref[slab, pert] = rhs_ref[pert, slab]
    wait_all(copies)

    numer = jnp.zeros((two, chunk), F32)
    denom = jnp.zeros((two, chunk), F32)
    tail = jnp.zeros((two, LANES), F32)
    energy = [jnp.full((1, chunk), energy_ref[slab * two + b], F32) for b in range(two)]
    energy = jnp.concatenate(energy, axis=0)
    for s in range(slabs):
        for q in range(quarters):
            tail = tail + back_ref[s, q, :, part:].astype(F32)
            for i in range(part // chunk):
                at = pl.ds(q * part + i * chunk, chunk)
                mine = back_ref[s, q, :, i * chunk : (i + 1) * chunk].astype(F32)
                data_ref[s, 0:2, at] = mine
                squares = mine * mine
                numer = numer + squares
                denom = denom + (index_ref[s, 4:5, at] - energy) * squares
    step = -jnp.sum(numer, axis=1, keepdims=True) / jnp.sum(denom, axis=1, keepdims=True)
    step = step * (4.0 * N1 * N2 * N3 / count)
    tail = step * (tail + pltpu.roll(tail, LANES - quarters, 1))
    tail = jnp.sum(tail, axis=0, keepdims=True)
    wide = jnp.broadcast_to(step, (two, LANES))
    step_ref[...] = jnp.concatenate([wide, tail, jnp.zeros((8 - two - 1, LANES), F32)], axis=0)


def end_kernel(
    turned_ref, psi_ref, step_ref, pots_ref, gram_ref, tab_ref, out_ref, projected_ref,
    dens_ref, from_core, a_ref, b_ref, a_from_y, b_from_z, a_sum, b_sum, a_from_z, b_from_y,
    sums_ref, from_sums, core_send, core_recv, a_send, a_recv, b_send, b_recv,
    a2_send, a2_recv, b2_send, b2_recv, sum_send, sum_recv,
):
    perts, planes, _ = pots_ref.shape
    slabs = dens_ref.shape[0]
    y_hi, y_lo, z, core = place()
    sibling = device(y_hi, y_lo, z, 1 - core)
    y_coords = [(1 - y_hi, y_lo), (1 - y_hi, 1 - y_lo), (y_hi, 1 - y_lo)]
    y_peers = [device(a, b, z, core) for a, b in y_coords]
    y_others = [device(a, b, z, 1 - core) for a, b in y_coords]
    z_coords = [lax.rem(z + d, 4) for d in range(1, 4)]
    z_peers = [device(y_hi, y_lo, c, core) for c in z_coords]
    everyone = [sibling] + y_peers + y_others + z_peers
    greet(everyone)
    pairs = pairs_of(perts)
    line = iota((1, LANES), 1)
    sums = [gram_ref[0 : len(pairs)]]
    sums += [jnp.where(line == p, step_ref[2:3], 0.0) for p in range(perts)]
    sums.append(jnp.zeros((16 - len(pairs) - perts, LANES), F32))
    sums_ref[0] = jnp.concatenate(sums, axis=0)

    inv_x = transposed(tab_ref[...])
    lane = iota((N1, LANES), 1)
    half = 4 * PARTS

    def density_part(h, first, last):
        @pl.loop(first, last)
        def _(group):
            done = []
            for v in range(4):
                quad = h * 12 + group * 4 + v
                parts = []
                for u in range(4):
                    row = quad * 4 + u
                    field = dot(inv_x, turned_ref[row]).astype(BF16).astype(F32)
                    terms = psi_ref[row].astype(F32) * field
                    parts.append(step_ref[0:1] * terms[:, :LANES] + step_ref[1:2] * terms[:, LANES:])
                one, two, three = [pltpu.roll(parts[u], LANES - 32 * u, 1) for u in (1, 2, 3)]
                tiles = [
                    jnp.where(lane < 96, parts[0], one),
                    jnp.where(lane < 64, one, two),
                    jnp.where(lane < 32, two, three),
                ]
                done += [(quad * 3 + j, tile) for j, tile in enumerate(tiles)]
            for at, tile in done:
                for s in range(slabs):
                    dens_ref[s, at] = tile[s * planes : (s + 1) * planes].astype(BF16)

    halves = [1 - y_hi, y_hi]
    core_copies, a_copies, b_copies = [], [], []

    def to_sibling(k):
        h = halves[k]
        for l in range(2):
            src = dens_ref.at[l * 2 + 1 - core, pl.ds(h * half, half)]
            core_copies.append(
                send(src, from_core.at[k, l], core_send.at[k, l], core_recv.at[k, l], sibling)
            )

    def to_others(k):
        h = halves[k]
        wait_all(core_copies[2 * k : 2 * k + 2])
        for l in range(2):
            @pl.loop(0, 4)
            def _(c):
                done = []
                for j in range(PARTS):
                    at = c * PARTS + j
                    total = dens_ref[l * 2 + core, h * half + at].astype(F32) + from_core[k, l, at].astype(F32)
                    done.append(total.astype(BF16))
                for j in range(PARTS):
                    if j < PART_A:
                        a_ref[k, l, c, j] = done[j]
                    else:
                        b_ref[k, c, l, j - PART_A] = done[j]
        targets = [(0, y_lo), (1, 1 - y_lo)] if k == 0 else [(2, 1 - y_lo)]
        for i, l in targets:
            a_copies.append(send(a_ref.at[k, l], a_from_y.at[i], a_send.at[i], a_recv.at[i], y_peers[i]))
        for i, c in enumerate(z_coords):
            b_copies.append(
                send(b_ref.at[k, c], b_from_z.at[k, i], b_send.at[k, i], b_recv.at[k, i], z_peers[i])
            )

    def sum_sends(level, first, group):
        copies = []
        for i, peer in enumerate(group):
            k = first + i
            copies.append(send(sums_ref.at[level], from_sums.at[k], sum_send.at[k], sum_recv.at[k], peer))
        return copies

    def sum_up(level, first, copies):
        wait_all(copies)
        total = sums_ref[level]
        for i in range(len(copies)):
            total = total + from_sums[first + i]
        sums_ref[level + 1] = total

    density_part(halves[0], 0, 3)
    greeted(everyone)
    to_sibling(0)
    near = [sibling] + y_peers + y_others
    near_copies = sum_sends(0, 0, near)
    density_part(halves[1], 0, 1)
    to_others(0)
    density_part(halves[1], 1, 3)
    to_sibling(1)

    def pot(p, j):
        return pots_ref[p, :, j * LANES : (j + 1) * LANES]

    to_others(1)

    sum_up(0, 0, near_copies)
    far_copies = sum_sends(1, len(near), z_peers)
    wait_all(a_copies)

    @pl.loop(0, 4)
    def _(c):
        done = []
        for j in range(PART_A):
            total = a_ref[1, y_lo, c, j].astype(F32)
            for i in range(3):
                total = total + a_from_y[i, c, j].astype(F32)
            done.append(total.astype(BF16))
        for j in range(PART_A):
            a_sum[c, j] = done[j]

    copies = []
    for i, c in enumerate(z_coords):
        copies.append(send(a_sum.at[c], a_from_z.at[i], a2_send.at[i], a2_recv.at[i], z_peers[i]))
    wait_all(b_copies)
    spots = [(k, l, j) for k in range(2) for l in range(2) for j in range(PART_B)]
    done = []
    for k, l, j in spots:
        total = b_ref[k, z, l, j].astype(F32)
        for i in range(3):
            total = total + b_from_z[k, i, l, j].astype(F32)
        done.append(total.astype(BF16))
    for (k, l, j), value in zip(spots, done):
        b_sum[k, l, j] = value
    for i, (k, l) in enumerate([(0, y_lo), (0, 1 - y_lo), (1, 1 - y_lo)]):
        copies.append(send(b_sum.at[k, l], b_from_y.at[i], b2_send.at[i], b2_recv.at[i], y_peers[i]))
    wait_all(copies)
    density = []
    for j in range(PARTS):
        if j < PART_A:
            total = a_sum[z, j].astype(F32)
            for i in range(3):
                total = total + a_from_z[i, j].astype(F32)
        else:
            total = b_sum[1, y_lo, j - PART_A].astype(F32)
            for i in range(3):
                total = total + b_from_y[i, j - PART_A].astype(F32)
        density.append(total)
    sum_up(1, len(near), far_copies)

    cells = 1.0 / (N1 * N2 * N3)
    totals = jnp.broadcast_to(jnp.sum(sums_ref[2], axis=1, keepdims=True) * cells, (16, LANES))
    gram = {pair: totals[k : k + 1] for k, pair in enumerate(pairs)}
    rhs = [totals[len(pairs) + p : len(pairs) + p + 1] for p in range(perts)]
    factor = {}
    for p in range(perts):
        for q in range(p + 1):
            value = gram[p, q]
            for k in range(q):
                value = value - factor[p, k] * factor[q, k]
            factor[p, q] = jnp.sqrt(value) if p == q else value / factor[q, q]
    coeffs = []
    for p in range(perts):
        value = rhs[p]
        for k in range(p):
            value = value - factor[p, k] * coeffs[k]
        coeffs.append(value / factor[p, p])
    for p in reversed(range(perts)):
        value = coeffs[p]
        for k in range(p + 1, perts):
            value = value - factor[k, p] * coeffs[k]
        coeffs[p] = value / factor[p, p]
    for j in range(PARTS):
        value = density[j]
        for p in range(perts):
            value = value - coeffs[p] * pot(p, j)
        out_ref[:, j * LANES : (j + 1) * LANES] = value
    projected_ref[...] = jnp.concatenate(rhs + rhs, axis=0)


def cost(flops, moved):
    return pl.CostEstimate(flops=int(flops), bytes_accessed=int(moved), transcendentals=0)


def params(collective=None):
    if collective is None:
        return pltpu.CompilerParams(vmem_limit_bytes=LIMIT)
    return pltpu.CompilerParams(vmem_limit_bytes=LIMIT, collective_id=collective, has_side_effects=True)


def shape(dims, kind):
    return jax.ShapeDtypeStruct(dims, kind)


def sems(*dims):
    return [pltpu.SemaphoreType.DMA(dims)] * 2


def start_of(coefs, wave_map, pot, slabs):
    bands, npw = coefs.shape
    block = (slabs, bands // slabs, npw)
    return pl.pallas_call(
        start_kernel,
        out_shape=(
            shape((slabs, 8, npw + 2 * WIN), F32),
            shape((slabs, 1, LANES), jnp.int32),
            shape(pot.shape, BF16),
            shape((pot.shape[0], pot.shape[1] // 8), F32),
        ),
        in_specs=[VMEM] * 3,
        out_specs=(VMEM,) * 4,
        scratch_shapes=[
            pltpu.VMEM(block, BF16),
            pltpu.VMEM((1, npw + LANES), jnp.int32),
            pltpu.VMEM(block, BF16),
            pltpu.VMEM((slabs, 1, npw + LANES), jnp.int32),
        ]
        + sems(2, slabs - 1),
        compiler_params=params(1),
        name="start",
    )(coefs, wave_map.reshape(npw // LANES, LANES), pot)


def zy_of(starts, data, tab):
    return pl.pallas_call(
        zy_kernel,
        out_shape=shape((N2, N1, 2 * LANES), BF16),
        in_specs=[SMEM] + [VMEM] * 2,
        out_specs=VMEM,
        scratch_shapes=[pltpu.VMEM((N1, 2 * N2, N3), BF16)],
        compiler_params=params(),
        cost_estimate=cost(2e10, 8e6),
        name="scatter_zy",
    )(starts, data, tab)


def dense_of(turned, pot, far, share, coefs, tab, slabs, perts):
    bands, npw = coefs.shape
    return pl.pallas_call(
        dense_kernel,
        out_shape=(
            shape((N2, N1, 2 * LANES), BF16),
            shape((N1, N2, 2 * LANES), BF16),
            shape((2, 4, bands, npw // QUARTERS), BF16),
            shape((perts,) + share.shape, F32),
            shape((16, LANES), F32),
        ),
        in_specs=[VMEM] * 6,
        out_specs=(VMEM,) * 5,
        scratch_shapes=[
            pltpu.VMEM((slabs,) + pot.shape, BF16),
        ]
        + sems(2)
        + sems(7)
        + sems(perts - 1),
        compiler_params=params(4),
        cost_estimate=cost(2e10, 8e6),
        name="dense",
    )(turned, pot, far, share, coefs, tab)


def gather_of(starts, data, back, tab, npw):
    slabs = data.shape[0]
    return pl.pallas_call(
        gather_kernel,
        out_shape=shape((slabs, QUARTERS, 2, npw // QUARTERS), BF16),
        in_specs=[SMEM] + [VMEM] * 3,
        out_specs=VMEM,
        scratch_shapes=[pltpu.VMEM((slabs, 2, data.shape[2]), F32)],
        compiler_params=params(),
        cost_estimate=cost(2e10, 8e6),
        name="gather",
    )(starts, data, back, tab)


def middle_of(waves, bands, index, energies):
    slabs, quarters, two, part = waves.shape
    peers = slabs * quarters - 1
    small = (slabs * quarters * two // 2, LANES)
    longer = pltpu.VMEM((slabs, quarters, two, part + LANES), BF16)
    return pl.pallas_call(
        middle_kernel,
        out_shape=(shape(index.shape, F32), shape((8, LANES), F32)),
        in_specs=[VMEM] * 3 + [SMEM],
        out_specs=(VMEM, VMEM),
        scratch_shapes=[
            pltpu.VMEM(waves.shape, BF16),
            pltpu.VMEM((peers,) + small, BF16),
            longer,
            longer,
            pltpu.VMEM(small, BF16),
        ]
        + sems(3, peers),
        compiler_params=params(2),
        name="middle",
    )(waves, bands, index, energies)


def end_of(turned, psi, step, pots, gram, tab, slabs):
    _, planes, width = pots.shape
    tile = (planes, LANES)
    return pl.pallas_call(
        end_kernel,
        out_shape=(shape((planes, width), F32), shape((8, LANES), F32)),
        in_specs=[VMEM] * 6,
        out_specs=(VMEM, VMEM),
        scratch_shapes=[
            pltpu.VMEM((slabs, 8 * PARTS) + tile, BF16),
            pltpu.VMEM((2, 2, 4 * PARTS) + tile, BF16),
            pltpu.VMEM((2, 2, 4, PART_A) + tile, BF16),
            pltpu.VMEM((2, 4, 2, PART_B) + tile, BF16),
            pltpu.VMEM((3, 4, PART_A) + tile, BF16),
            pltpu.VMEM((2, 3, 2, PART_B) + tile, BF16),
            pltpu.VMEM((4, PART_A) + tile, BF16),
            pltpu.VMEM((2, 2, PART_B) + tile, BF16),
            pltpu.VMEM((3, PART_A) + tile, BF16),
            pltpu.VMEM((3, PART_B) + tile, BF16),
            pltpu.VMEM((3, 16, LANES), F32),
            pltpu.VMEM((10, 16, LANES), F32),
        ]
        + sems(2, 2)
        + sems(3)
        + sems(2, 3)
        + sems(3)
        + sems(3)
        + sems(10),
        compiler_params=params(3),
        name="density",
    )(turned, psi, step, pots, gram, tab)


def next_chip():
    pairs = []
    for band in range(8):
        for slab in range(4):
            core = slab % 2
            to = (band // 4 * 2 + slab // 2 + 2 * core - 1) % 4
            pairs.append((band * 4 + slab, (to // 2 * 4 + band % 4) * 4 + to % 2 * 2 + core))
    return pairs


def per_device(wave_coeffs, band_energies, trial_potentials, wave_map):
    slabs = lax.axis_size("slab")
    npw = wave_coeffs.shape[1]
    planes, cross = trial_potentials.shape[1:]
    tab = cosines(N1)
    pot = trial_potentials.reshape(planes, cross)
    data, starts, narrow, share = start_of(wave_coeffs, wave_map, pot, slabs)
    far = lax.ppermute(narrow, ("band", "slab"), next_chip())
    turned = zy_of(starts, data, tab)
    perts = lax.axis_size("pert")
    psi, back, all_bands, pots, gram = dense_of(turned, narrow, far, share, wave_coeffs, tab, slabs, perts)
    waves = gather_of(starts, data, back, tab, npw)
    data, step = middle_of(waves, all_bands, data, band_energies)
    turned = zy_of(starts, data, tab)
    residual, projected = end_of(turned, psi, step, pots, gram, tab, slabs)
    return (residual.reshape(1, planes, -1), projected[:perts, :1])


def solution(mesh):
    return jax.shard_map(
        per_device,
        mesh=mesh,
        in_specs=(P("band", "slab"), P("band"), P("pert", "slab", None), P("slab")),
        out_specs=(P("pert", "slab", "band"), P(None, "pert")),
        check_vma=False,
    )
```

```python
import jax
import jax.numpy as jnp
from jax import lax
from jax.experimental import pallas as pl
from jax.experimental.pallas import tpu as pltpu
from jax.sharding import PartitionSpec as P

N1 = 96
N2 = 96
N3 = 96
LANES = 128
WIN = 512
NEAR = WIN - LANES
TILE = 2
TILES = N1 // TILE
QUARTERS = 4
PART_A = 5
PART_B = 4
PARTS = PART_A + PART_B
F32 = jnp.float32
BF16 = jnp.bfloat16
NT = (((1,), (1,)), ((), ()))
MESH = pl.DeviceIdType.MESH


def cosines(n):
    rows = jnp.arange(n, dtype=jnp.int32).astype(jnp.float32)[:, None]
    cols = jnp.arange(n, dtype=jnp.int32).astype(jnp.float32)[None, :]
    table = jnp.sqrt(2.0 / n) * jnp.cos(jnp.pi * rows * (cols + 0.5) / n)
    table = table * jnp.where(rows == 0, jnp.sqrt(0.5), 1.0)
    return table.astype(jnp.bfloat16)


def dot(a, b):
    return jnp.dot(a, b, preferred_element_type=F32)


def dot_nt(a, b):
    return lax.dot_general(a, b, NT, preferred_element_type=F32)


def iota(dims, axis):
    return lax.broadcasted_iota(jnp.int32, dims, axis)


def ones_at(rows, cols):
    return (iota((rows, cols), 0) == iota((rows, cols), 1)).astype(F32).astype(BF16)


def transposed(table):
    return dot_nt(ones_at(table.shape[1], table.shape[1]), table).astype(BF16)


def window_base(starts_ref, s, tile):
    return pl.multiple_of((starts_ref[s, 0, tile] // LANES) * LANES, LANES)


def overflow(starts_ref, slabs):
    total = starts_ref[0, 0, TILES + 1]
    for s in range(1, slabs):
        total = total + starts_ref[s, 0, TILES + 1]
    return total > 0


def near_at(starts_ref, s, tile, i=0):
    first = starts_ref[s, 0, tile]
    base = (first // LANES) * LANES
    return pl.multiple_of(base + i * NEAR, LANES), first - base


def hot_rows(rows, tile, cells):
    at = rows[2:3] - (tile * cells).astype(F32)
    return iota((cells, rows.shape[1]), 0).astype(F32) == at


def hot_z(rows):
    here = iota((N3, rows.shape[1]), 0).astype(F32) == rows[3:4]
    return here.astype(F32).astype(BF16)


def scatter_window(data_ref, s, base, tile, cells):
    rows = data_ref[s, :, pl.ds(base, WIN)]
    hot = hot_rows(rows, tile, cells)
    both = [jnp.where(hot, rows[0:1], 0.0), jnp.where(hot, rows[1:2], 0.0)]
    return dot_nt(jnp.concatenate(both, axis=0).astype(BF16), hot_z(rows))


def plane_of(parts, t, ny):
    cells = TILE * ny
    rows = [p[b * cells + t * ny : b * cells + (t + 1) * ny] for b in range(2) for p in parts]
    return jnp.concatenate(rows, axis=0)


def tile_planes(starts_ref, data_ref, tile):
    slabs = data_ref.shape[0]
    ny = N2 // slabs
    parts = [
        scatter_window(data_ref, s, window_base(starts_ref, s, tile), tile, TILE * ny)
        for s in range(slabs)
    ]
    return [plane_of(parts, t, ny) for t in range(TILE)]


def more_planes(starts_ref, data_ref, tile):
    slabs = data_ref.shape[0]
    ny = N2 // slabs
    cells = TILE * ny
    parts = []
    for s in range(slabs):
        base = window_base(starts_ref, s, tile)

        def more(i, acc):
            at = pl.multiple_of(base + i * WIN, LANES)
            return acc + scatter_window(data_ref, s, at, tile, cells)

        windows = (starts_ref[s, 0, tile + 1] - base + WIN - 1) // WIN
        parts.append(lax.fori_loop(1, windows, more, jnp.zeros((2 * cells, N3), F32)))
    return [plane_of(parts, t, ny) for t in range(TILE)]


def zy_kernel(starts_ref, data_ref, tab_ref, turned_ref, plane_ref):
    inv_y = transposed(tab_ref[...])
    inv_z = dot(tab_ref[...], ones_at(N3, LANES)).astype(BF16)
    width = 48
    over = overflow(starts_ref, data_ref.shape[0])

    def transform(planes, first):
        done = []
        for plane in planes:
            z_done = dot(plane, inv_z).astype(BF16)
            done.append(dot(inv_y, jnp.concatenate([z_done[:N2], z_done[N2:]], axis=1)).astype(BF16))
        turned_ref[:, pl.ds(first, width), :] = jnp.swapaxes(jnp.stack(done, axis=0), 0, 1)

    @pl.when(jnp.logical_not(over))
    def _():
        @pl.loop(0, N1 // width)
        def _(group):
            first = pl.multiple_of(group * width, width)
            planes = []
            for u in range(width // TILE):
                tile = group * (width // TILE) + u
                planes += [plane.astype(BF16) for plane in tile_planes(starts_ref, data_ref, tile)]
            transform(planes, first)

    @pl.when(over)
    def _():
        @pl.loop(0, TILES)
        def _(tile):
            planes = tile_planes(starts_ref, data_ref, tile)
            added = more_planes(starts_ref, data_ref, tile)
            for t in range(TILE):
                plane_ref[tile * TILE + t] = (planes[t] + added[t]).astype(BF16)

        @pl.loop(0, N1 // width)
        def _(group):
            first = pl.multiple_of(group * width, width)
            transform([plane_ref[first + u] for u in range(width)], first)


def gather_window(data_ref, planes, s, at, tile):
    ny = N2 // data_ref.shape[0]
    cells = TILE * ny
    base, off = at
    rows = pltpu.roll(data_ref[s, :, pl.ds(base, WIN)], WIN - off, 1)[:, :NEAR]
    hot = hot_rows(rows, tile, cells)
    mine = [plane[b * N2 + s * ny : b * N2 + (s + 1) * ny] for b in range(2) for plane in planes]
    picked = dot(jnp.concatenate(mine, axis=0).astype(BF16), hot_z(rows))
    found = [
        jnp.sum(jnp.where(hot, picked[b * cells : (b + 1) * cells], 0.0), axis=0, keepdims=True)
        for b in range(2)
    ]
    found = jnp.concatenate(found + [jnp.zeros((6, NEAR), F32)], axis=0)
    found = jnp.concatenate([found, jnp.zeros((8, WIN - NEAR), F32)], axis=1)
    return pltpu.roll(found, off, 1)[:2]


def gather_kernel(starts_ref, data_ref, back_ref, tab_ref, out_ref, sum_ref):
    slabs = data_ref.shape[0]
    sum_ref[...] = jnp.zeros_like(sum_ref)
    fwd_z = dot_nt(ones_at(LANES, N3), tab_ref[...]).astype(BF16)
    several = 16

    def wave_planes(tile, count):
        done = []
        for t in range(count):
            y_done = dot(tab_ref[...], back_ref[tile * TILE + t]).astype(BF16)
            done += [y_done[:, :LANES], y_done[:, LANES:]]
        waves = dot(jnp.concatenate(done, axis=0), fwd_z)
        return [waves[2 * N2 * t : 2 * N2 * (t + 1)] for t in range(count)]

    @pl.loop(0, TILES // several)
    def _(group):
        all_planes = wave_planes(group * several, several * TILE)
        found = []
        for u in range(several):
            tile = group * several + u
            planes = all_planes[TILE * u : TILE * (u + 1)]
            for s in range(slabs):
                at = near_at(starts_ref, s, tile)
                found.append((s, at[0], gather_window(data_ref, planes, s, at, tile)))
        for s, base, value in found:
            sum_ref[s, :, pl.ds(base, WIN)] += value

    @pl.when(overflow(starts_ref, slabs))
    def _():
        @pl.loop(0, TILES)
        def _(tile):
            planes = wave_planes(tile, TILE)
            for s in range(slabs):
                count = starts_ref[s, 0, tile + 1] - starts_ref[s, 0, tile]

                @pl.loop(1, (count + NEAR - 1) // NEAR)
                def _(i):
                    at = near_at(starts_ref, s, tile, i)
                    sum_ref[s, :, pl.ds(at[0], WIN)] += gather_window(data_ref, planes, s, at, tile)

    part = out_ref.shape[3]
    for q in range(out_ref.shape[1]):
        out_ref[:, q] = sum_ref[:, :, q * part : (q + 1) * part].astype(out_ref.dtype)


SMEM = pl.BlockSpec(memory_space=pltpu.SMEM)
VMEM = pl.BlockSpec(memory_space=pltpu.VMEM)
LIMIT = 32 * 1024 * 1024


def greet(peers):
    for peer in peers:
        pl.semaphore_signal(pltpu.get_barrier_semaphore(), inc=1, device_id=peer, device_id_type=MESH)


def greeted(peers):
    pl.semaphore_wait(pltpu.get_barrier_semaphore(), len(peers))


def remote(src, dst, send_sem, recv_sem, peer):
    return pltpu.make_async_remote_copy(
        src_ref=src, dst_ref=dst, send_sem=send_sem, recv_sem=recv_sem, device_id=peer, device_id_type=MESH
    )


def send(src, dst, send_sem, recv_sem, peer):
    copy = remote(src, dst, send_sem, recv_sem, peer)
    copy.start()
    return copy


def wait_all(copies):
    for copy in copies:
        copy.wait()


def slab_peers(slabs):
    me = lax.axis_index("slab")
    return [lax.rem(me + d, slabs) for d in range(1, slabs)]


def place():
    band, slab = lax.axis_index("band"), lax.axis_index("slab")
    return band // 4, slab // 2, lax.rem(band, 4), lax.rem(slab, 2)


def device(y_hi, y_lo, z, core):
    return {"band": y_hi * 4 + z, "slab": y_lo * 2 + core}


def pairs_of(perts):
    return [(p, q) for p in range(perts) for q in range(p + 1)]


def total_of(one, two):
    total = sum(a * b for a, b in zip(one, two))
    total = total[0:8] + total[8:16] + total[16:24]
    return jnp.sum(total, axis=0, keepdims=True)


def start_kernel(
    coef_ref, map_ref, pot_ref, data_ref, starts_ref, narrow_ref, share_ref,
    own_coef, own_map, coefs_ref, maps_ref, send_sem, recv_sem,
):
    slabs, two, npw = coefs_ref.shape
    ny = N2 // slabs
    me = lax.axis_index("slab")
    peers = slab_peers(slabs)
    chunk = 1536
    y_hi, y_lo, z, core = place()

    def around(step, other):
        to = lax.rem(y_hi * 2 + y_lo + step + 4, 4)
        return device(to // 2, lax.rem(to, 2), z, other)

    chips = [around(step, other) for step in (-1, 1) for other in (0, 1)]
    everyone = [device(y_hi, y_lo, z, 1 - core)] + chips
    greet(everyone)
    for r in range(npw // LANES):
        own_map[0:1, r * LANES : (r + 1) * LANES] = map_ref[r : r + 1, :]
    for i in range(npw // chunk):
        at = pl.ds(i * chunk, chunk)
        block = coef_ref[:, at].astype(F32)
        for t in range(slabs):
            own_coef[t, :, at] = block[two * t : two * (t + 1)].astype(BF16)
    greeted(everyone)
    coef_copies = []
    for i, peer in enumerate(peers):
        to = {"slab": peer}
        coef_copies.append(send(own_coef.at[peer], coefs_ref.at[me], send_sem.at[0, i], recv_sem.at[0, i], to))
    coefs_ref[me] = own_coef[me]
    edges = iota((56, LANES), 0) * (TILE * ny * N3)
    below = jnp.zeros((56, LANES), jnp.int32)
    for r in range(npw // LANES):
        below = below + (own_map[0:1, r * LANES : (r + 1) * LANES] < edges).astype(jnp.int32)
    count = jnp.sum(below.astype(F32), axis=1, keepdims=True)
    spread = jnp.where(iota((56, LANES), 0) == iota((56, LANES), 1), count, 0.0)
    starts = jnp.sum(spread, axis=0, keepdims=True).astype(jnp.int32)
    after = pltpu.roll(starts, LANES - 1, 1)
    lane = iota((1, LANES), 1)
    over = (after > starts + NEAR) & (lane < TILES)
    flag = jnp.max(over.astype(F32), axis=1, keepdims=True).astype(jnp.int32)
    own_map[0:1, npw : npw + LANES] = jnp.where(lane == TILES + 1, flag, starts)
    near = send(own_map, maps_ref.at[me], send_sem.at[1, 2], recv_sem.at[1, 2], everyone[0])
    copies = []
    for other in (0, 1):
        to = around(2 * core - 1, other)
        copies.append(send(own_map, maps_ref.at[me], send_sem.at[1, other], recv_sem.at[1, core], to))
    maps_ref[me] = own_map[...]
    data_ref[...] = jnp.full(data_ref.shape, -1.0, F32)
    narrow_ref[...] = pot_ref[...].astype(BF16)
    width = share_ref.shape[1]
    share_ref[...] = pot_ref[:, pl.ds(pl.multiple_of(lax.axis_index("band") * width, LANES), width)]
    near.wait()
    for other in (0, 1):
        copies[other].wait_send()
        slot = maps_ref.at[(1 - y_lo) * 2 + other]
        remote(own_map, slot, send_sem.at[1, other], recv_sem.at[1, other], everyone[0]).wait_recv()
    for s in range(slabs):
        starts_ref[s] = maps_ref[s, :, npw : npw + LANES]
    y_first = (iota((slabs, 1), 0) * ny).astype(F32)
    for i in range(npw // chunk):
        at = pl.ds(i * chunk, chunk)
        cell = jnp.concatenate([maps_ref[s, :, at] for s in range(slabs)], axis=0).astype(F32)
        row = jnp.floor((cell + 0.5) * (1.0 / N3))
        zpos = cell - row * N3
        xpos = jnp.floor((row + 0.5) * (1.0 / ny))
        ypos = row - xpos * ny + y_first
        kin = 2.0 * (xpos * xpos / (N1 * N1) + ypos * ypos / (N2 * N2) + zpos * zpos / (N3 * N3))
        for s in range(slabs):
            lines = [part[s : s + 1] for part in (row, zpos, kin)]
            data_ref[s, 2:5, at] = jnp.concatenate(lines, axis=0)
    wait_all(coef_copies)
    for s in range(slabs):
        for i in range(npw // chunk):
            at = pl.ds(i * chunk, chunk)
            data_ref[s, 0:2, at] = coefs_ref[s, :, at].astype(F32)


def dense_kernel(
    turned_ref, pot_ref, far_ref, share_ref, coef_ref, tab_ref,
    psi_ref, back_ref, bands_ref, shares_ref, gram_ref,
    pots_ref, send_sem, recv_sem, coef_send, coef_recv, share_send, share_recv,
):
    slabs = pots_ref.shape[0]
    y_hi, y_lo, z, core = place()
    me = lax.axis_index("slab")
    distant = (1 - y_lo) * 2 + core
    sibling = device(y_hi, y_lo, z, 1 - core)
    steps = [(a, b) for a in range(2) for b in range(4) if a + b > 0]
    others = [(lax.rem(y_hi + a, 2), lax.rem(z + b, 4)) for a, b in steps]
    members = [device(a, y_lo, b, core) for a, b in others]
    perts = shares_ref.shape[0]
    pert = lax.axis_index("pert")
    p_peers = [{"pert": lax.rem(pert + d, perts)} for d in range(1, perts)]
    everyone = [sibling] + members + p_peers
    greet(everyone)
    part = bands_ref.shape[3]
    quarter = pl.ds(pl.multiple_of(lax.axis_index("pert") * part, LANES), part)
    bands_ref[y_hi, z] = coef_ref[:, quarter]
    pots_ref[me] = pot_ref[...]
    pots_ref[distant] = far_ref[...]
    shares_ref[pert] = share_ref[...]
    greeted(everyone)
    copies = []
    for i, member in enumerate(members):
        src = coef_ref.at[:, quarter]
        copies.append(send(src, bands_ref.at[y_hi, z], coef_send.at[i], coef_recv.at[i], member))
    near = [
        send(pot_ref, pots_ref.at[me], send_sem.at[0], recv_sem.at[0], sibling),
        send(far_ref, pots_ref.at[distant], send_sem.at[1], recv_sem.at[1], sibling),
    ]
    for i, peer in enumerate(p_peers):
        copies.append(send(share_ref, shares_ref.at[pert], share_send.at[i], share_recv.at[i], peer))

    inv_x = transposed(tab_ref[...])
    unroll = 16

    @pl.loop(0, N2 // unroll)
    def _(group):
        rows = [group * unroll + u for u in range(unroll)]
        done = [dot(inv_x, turned_ref[row]).astype(BF16) for row in rows]
        for row, value in zip(rows, done):
            psi_ref[row] = value

    wait_all(near)

    width = 16
    lane = iota((N1 // slabs, LANES), 1)

    @pl.loop(0, N2 // width)
    def _(group):
        first = pl.multiple_of(group * width, width)
        done = []
        for v in range(width // 4):
            quads = [[], [], [], []]
            for s in range(slabs):
                parts = []
                for j in range(3):
                    off = pl.multiple_of(group * (width * N3) + (3 * v + j) * LANES, LANES)
                    parts.append(pots_ref[s, :, pl.ds(off, LANES)].astype(F32))
                a, b, c = parts
                quads[0].append(a)
                quads[1].append(jnp.where(lane < 32, pltpu.roll(a, 32, 1), pltpu.roll(b, 32, 1)))
                quads[2].append(jnp.where(lane < 64, pltpu.roll(b, 64, 1), pltpu.roll(c, 64, 1)))
                quads[3].append(pltpu.roll(c, 96, 1))
            for u in range(4):
                pot = jnp.concatenate(quads[u], axis=0)
                psi = psi_ref[first + 4 * v + u].astype(F32)
                product = jnp.concatenate([pot * psi[:, :LANES], pot * psi[:, LANES:]], axis=1)
                done.append(dot(tab_ref[...], product.astype(BF16)).astype(BF16))
        back_ref[:, pl.ds(first, width), :] = jnp.swapaxes(jnp.stack(done, axis=0), 0, 1)

    wait_all(copies)
    parts = [[shares_ref[p, :, j * LANES : (j + 1) * LANES] for j in range(PARTS)] for p in range(perts)]
    sums = [total_of(parts[p], parts[q]) for p, q in pairs_of(perts)]
    sums.append(jnp.zeros((16 - len(sums), LANES), F32))
    gram_ref[...] = jnp.concatenate(sums, axis=0)


def middle_kernel(
    waves_ref, bands_ref, index_ref, energy_ref, data_ref, step_ref,
    got_ref, corr_ref, rhs_ref, back_ref, total_ref, send_sem, recv_sem,
):
    slabs, quarters, two, part = waves_ref.shape
    half, zs, bands, _ = bands_ref.shape
    chunk = 1152
    pert, slab = lax.axis_index("pert"), lax.axis_index("slab")
    steps = [(a, b) for a in (2, 1, 3, 0) for b in (2, 3, 1, 0) if a + b > 0]
    others = [(lax.rem(pert + a, quarters), lax.rem(slab + b, slabs)) for a, b in steps]
    peers = [{"pert": c, "slab": t} for c, t in others]
    greet(peers)
    greeted(peers)
    copies = []
    for i, (c, t) in enumerate(others):
        src, dst = waves_ref.at[t, c], got_ref.at[pert, slab]
        copies.append(send(src, dst, send_sem.at[0, i], recv_sem.at[0, i], peers[i]))
    got_ref[pert, slab] = waves_ref[slab, pert]
    data_ref[...] = index_ref[...]
    wait_all(copies)

    def waves_at(at):
        parts = [got_ref[c, t, :, at].astype(F32) for c in range(quarters) for t in range(slabs)]
        return jnp.concatenate(parts, axis=0)

    def bands_at(at):
        parts = [bands_ref[a, c, :, at].astype(F32) for a in range(half) for c in range(zs)]
        return jnp.concatenate(parts, axis=0).astype(BF16)

    rows, count = quarters * slabs * two, half * zs * bands
    total = jnp.zeros((rows, count), F32)
    for i in range(part // chunk):
        at = pl.ds(i * chunk, chunk)
        total = total + dot_nt(waves_at(at).astype(BF16), bands_at(at))
    total_ref[...] = jnp.concatenate([total[: rows // 2], total[rows // 2 :]], axis=1).astype(BF16)

    copies = []
    for i, peer in enumerate(peers):
        copies.append(send(total_ref, corr_ref.at[i], send_sem.at[1, i], recv_sem.at[1, i], peer))
    wait_all(copies)
    total = total_ref[...].astype(F32)
    for i in range(len(peers)):
        total = total + corr_ref[i].astype(F32)
    correlation = jnp.concatenate([total[:, :count], total[:, count:]], axis=0).astype(BF16)

    overlap = jnp.zeros((rows, rows), F32)
    for i in range(part // chunk):
        at = pl.ds(i * chunk, chunk)
        waves = waves_at(at)
        rhs = (waves - dot(correlation, bands_at(at))).astype(BF16)
        overlap = overlap + dot_nt(rhs, waves.astype(BF16))
        rhs = rhs.astype(F32)
        for c in range(quarters):
            for t in range(slabs):
                first = two * (c * slabs + t)
                rhs_ref[c, t, :, at] = rhs[first : first + two].astype(BF16)
    own = rows // quarters
    same = lax.rem(iota((rows, rows), 0), own) == lax.rem(iota((rows, rows), 1), own)
    kept = jnp.where(same, overlap, 0.0)
    lane = iota((rows, LANES), 1)
    tail = jnp.zeros((rows, LANES), F32)
    for p in range(quarters):
        mine = jnp.sum(kept[:, p * own : (p + 1) * own], axis=1, keepdims=True)
        high = mine.astype(BF16).astype(F32)
        tail = jnp.where(lane == p, high, tail)
        tail = jnp.where(lane == quarters + p, mine - high, tail)
    for c in range(quarters):
        for t in range(slabs):
            first = two * (c * slabs + t)
            rhs_ref[c, t, :, part:] = tail[first : first + two].astype(BF16)

    copies = []
    for i, (c, t) in enumerate(others):
        src, dst = rhs_ref.at[c, t], back_ref.at[slab, pert]
        copies.append(send(src, dst, send_sem.at[2, i], recv_sem.at[2, i], peers[i]))
    back_ref[slab, pert] = rhs_ref[pert, slab]
    wait_all(copies)

    numer = jnp.zeros((two, chunk), F32)
    denom = jnp.zeros((two, chunk), F32)
    tail = jnp.zeros((two, LANES), F32)
    energy = [jnp.full((1, chunk), energy_ref[slab * two + b], F32) for b in range(two)]
    energy = jnp.concatenate(energy, axis=0)
    for s in range(slabs):
        for q in range(quarters):
            tail = tail + back_ref[s, q, :, part:].astype(F32)
            for i in range(part // chunk):
                at = pl.ds(q * part + i * chunk, chunk)
                mine = back_ref[s, q, :, i * chunk : (i + 1) * chunk].astype(F32)
                data_ref[s, 0:2, at] = mine
                squares = mine * mine
                numer = numer + squares
                denom = denom + (index_ref[s, 4:5, at] - energy) * squares
    step = -jnp.sum(numer, axis=1, keepdims=True) / jnp.sum(denom, axis=1, keepdims=True)
    step = step * (4.0 * N1 * N2 * N3 / count)
    tail = step * (tail + pltpu.roll(tail, LANES - quarters, 1))
    tail = jnp.sum(tail, axis=0, keepdims=True)
    wide = jnp.broadcast_to(step, (two, LANES))
    step_ref[...] = jnp.concatenate([wide, tail, jnp.zeros((8 - two - 1, LANES), F32)], axis=0)


def end_kernel(
    turned_ref, psi_ref, step_ref, pots_ref, gram_ref, tab_ref, out_ref, projected_ref,
    dens_ref, from_core, a_ref, b_ref, a_from_y, b_from_z, a_sum, b_sum, a_from_z, b_from_y,
    sums_ref, from_sums, core_send, core_recv, a_send, a_recv, b_send, b_recv,
    a2_send, a2_recv, b2_send, b2_recv, sum_send, sum_recv,
):
    perts, planes, _ = pots_ref.shape
    slabs = dens_ref.shape[0]
    y_hi, y_lo, z, core = place()
    sibling = device(y_hi, y_lo, z, 1 - core)
    y_coords = [(1 - y_hi, y_lo), (1 - y_hi, 1 - y_lo), (y_hi, 1 - y_lo)]
    y_peers = [device(a, b, z, core) for a, b in y_coords]
    y_others = [device(a, b, z, 1 - core) for a, b in y_coords]
    z_coords = [lax.rem(z + d, 4) for d in range(1, 4)]
    z_peers = [device(y_hi, y_lo, c, core) for c in z_coords]
    everyone = [sibling] + y_peers + y_others + z_peers
    greet(everyone)
    pairs = pairs_of(perts)
    line = iota((1, LANES), 1)
    sums = [gram_ref[0 : len(pairs)]]
    sums += [jnp.where(line == p, step_ref[2:3], 0.0) for p in range(perts)]
    sums.append(jnp.zeros((16 - len(pairs) - perts, LANES), F32))
    sums_ref[0] = jnp.concatenate(sums, axis=0)

    inv_x = transposed(tab_ref[...])
    lane = iota((N1, LANES), 1)
    half = 4 * PARTS

    def density_part(h, first, last):
        @pl.loop(first, last)
        def _(group):
            done = []
            for v in range(4):
                quad = h * 12 + group * 4 + v
                parts = []
                for u in range(4):
                    row = quad * 4 + u
                    field = dot(inv_x, turned_ref[row]).astype(BF16).astype(F32)
                    terms = psi_ref[row].astype(F32) * field
                    parts.append(step_ref[0:1] * terms[:, :LANES] + step_ref[1:2] * terms[:, LANES:])
                one, two, three = [pltpu.roll(parts[u], LANES - 32 * u, 1) for u in (1, 2, 3)]
                tiles = [
                    jnp.where(lane < 96, parts[0], one),
                    jnp.where(lane < 64, one, two),
                    jnp.where(lane < 32, two, three),
                ]
                done += [(quad * 3 + j, tile) for j, tile in enumerate(tiles)]
            for at, tile in done:
                for s in range(slabs):
                    dens_ref[s, at] = tile[s * planes : (s + 1) * planes].astype(BF16)

    halves = [1 - y_hi, y_hi]
    core_copies, a_copies, b_copies = [], [], []

    def to_sibling(k):
        h = halves[k]
        for l in range(2):
            src = dens_ref.at[l * 2 + 1 - core, pl.ds(h * half, half)]
            core_copies.append(
                send(src, from_core.at[k, l], core_send.at[k, l], core_recv.at[k, l], sibling)
            )

    def to_others(k):
        h = halves[k]
        wait_all(core_copies[2 * k : 2 * k + 2])
        for l in range(2):
            @pl.loop(0, 4)
            def _(c):
                done = []
                for j in range(PARTS):
                    at = c * PARTS + j
                    total = dens_ref[l * 2 + core, h * half + at].astype(F32) + from_core[k, l, at].astype(F32)
                    done.append(total.astype(BF16))
                for j in range(PARTS):
                    if j < PART_A:
                        a_ref[k, l, c, j] = done[j]
                    else:
                        b_ref[k, c, l, j - PART_A] = done[j]
        targets = [(0, y_lo), (1, 1 - y_lo)] if k == 0 else [(2, 1 - y_lo)]
        for i, l in targets:
            a_copies.append(send(a_ref.at[k, l], a_from_y.at[i], a_send.at[i], a_recv.at[i], y_peers[i]))
        for i, c in enumerate(z_coords):
            b_copies.append(
                send(b_ref.at[k, c], b_from_z.at[k, i], b_send.at[k, i], b_recv.at[k, i], z_peers[i])
            )

    def sum_sends(level, first, group):
        copies = []
        for i, peer in enumerate(group):
            k = first + i
            copies.append(send(sums_ref.at[level], from_sums.at[k], sum_send.at[k], sum_recv.at[k], peer))
        return copies

    def sum_up(level, first, copies):
        wait_all(copies)
        total = sums_ref[level]
        for i in range(len(copies)):
            total = total + from_sums[first + i]
        sums_ref[level + 1] = total

    density_part(halves[0], 0, 3)
    greeted(everyone)
    to_sibling(0)
    near = [sibling] + y_peers + y_others
    near_copies = sum_sends(0, 0, near)
    density_part(halves[1], 0, 1)
    to_others(0)
    density_part(halves[1], 1, 3)
    to_sibling(1)

    def pot(p, j):
        return pots_ref[p, :, j * LANES : (j + 1) * LANES]

    to_others(1)

    sum_up(0, 0, near_copies)
    far_copies = sum_sends(1, len(near), z_peers)
    wait_all(a_copies)

    @pl.loop(0, 4)
    def _(c):
        done = []
        for j in range(PART_A):
            total = a_ref[1, y_lo, c, j].astype(F32)
            for i in range(3):
                total = total + a_from_y[i, c, j].astype(F32)
            done.append(total.astype(BF16))
        for j in range(PART_A):
            a_sum[c, j] = done[j]

    copies = []
    for i, c in enumerate(z_coords):
        copies.append(send(a_sum.at[c], a_from_z.at[i], a2_send.at[i], a2_recv.at[i], z_peers[i]))
    wait_all(b_copies)
    spots = [(k, l, j) for k in range(2) for l in range(2) for j in range(PART_B)]
    done = []
    for k, l, j in spots:
        total = b_ref[k, z, l, j].astype(F32)
        for i in range(3):
            total = total + b_from_z[k, i, l, j].astype(F32)
        done.append(total.astype(BF16))
    for (k, l, j), value in zip(spots, done):
        b_sum[k, l, j] = value
    for i, (k, l) in enumerate([(0, y_lo), (0, 1 - y_lo), (1, 1 - y_lo)]):
        copies.append(send(b_sum.at[k, l], b_from_y.at[i], b2_send.at[i], b2_recv.at[i], y_peers[i]))
    wait_all(copies)
    density = []
    for j in range(PARTS):
        if j < PART_A:
            total = a_sum[z, j].astype(F32)
            for i in range(3):
                total = total + a_from_z[i, j].astype(F32)
        else:
            total = b_sum[1, y_lo, j - PART_A].astype(F32)
            for i in range(3):
                total = total + b_from_y[i, j - PART_A].astype(F32)
        density.append(total)
    sum_up(1, len(near), far_copies)

    cells = 1.0 / (N1 * N2 * N3)
    totals = jnp.broadcast_to(jnp.sum(sums_ref[2], axis=1, keepdims=True) * cells, (16, LANES))
    gram = {pair: totals[k : k + 1] for k, pair in enumerate(pairs)}
    rhs = [totals[len(pairs) + p : len(pairs) + p + 1] for p in range(perts)]
    factor = {}
    for p in range(perts):
        for q in range(p + 1):
            value = gram[p, q]
            for k in range(q):
                value = value - factor[p, k] * factor[q, k]
            factor[p, q] = jnp.sqrt(value) if p == q else value / factor[q, q]
    coeffs = []
    for p in range(perts):
        value = rhs[p]
        for k in range(p):
            value = value - factor[p, k] * coeffs[k]
        coeffs.append(value / factor[p, p])
    for p in reversed(range(perts)):
        value = coeffs[p]
        for k in range(p + 1, perts):
            value = value - factor[k, p] * coeffs[k]
        coeffs[p] = value / factor[p, p]
    for j in range(PARTS):
        value = density[j]
        for p in range(perts):
            value = value - coeffs[p] * pot(p, j)
        out_ref[:, j * LANES : (j + 1) * LANES] = value
    projected_ref[...] = jnp.concatenate(rhs + rhs, axis=0)


def cost(flops, moved):
    return pl.CostEstimate(flops=int(flops), bytes_accessed=int(moved), transcendentals=0)


def params(collective=None):
    if collective is None:
        return pltpu.CompilerParams(vmem_limit_bytes=LIMIT)
    return pltpu.CompilerParams(vmem_limit_bytes=LIMIT, collective_id=collective, has_side_effects=True)


def shape(dims, kind):
    return jax.ShapeDtypeStruct(dims, kind)


def sems(*dims):
    return [pltpu.SemaphoreType.DMA(dims)] * 2


def start_of(coefs, wave_map, pot, slabs):
    bands, npw = coefs.shape
    block = (slabs, bands // slabs, npw)
    return pl.pallas_call(
        start_kernel,
        out_shape=(
            shape((slabs, 8, npw + 2 * WIN), F32),
            shape((slabs, 1, LANES), jnp.int32),
            shape(pot.shape, BF16),
            shape((pot.shape[0], pot.shape[1] // 8), F32),
        ),
        in_specs=[VMEM] * 3,
        out_specs=(VMEM,) * 4,
        scratch_shapes=[
            pltpu.VMEM(block, BF16),
            pltpu.VMEM((1, npw + LANES), jnp.int32),
            pltpu.VMEM(block, BF16),
            pltpu.VMEM((slabs, 1, npw + LANES), jnp.int32),
        ]
        + sems(2, slabs - 1),
        compiler_params=params(1),
        name="start",
    )(coefs, wave_map.reshape(npw // LANES, LANES), pot)


def zy_of(starts, data, tab):
    return pl.pallas_call(
        zy_kernel,
        out_shape=shape((N2, N1, 2 * LANES), BF16),
        in_specs=[SMEM] + [VMEM] * 2,
        out_specs=VMEM,
        scratch_shapes=[pltpu.VMEM((N1, 2 * N2, N3), BF16)],
        compiler_params=params(),
        cost_estimate=cost(2e10, 8e6),
        name="scatter_zy",
    )(starts, data, tab)


def dense_of(turned, pot, far, share, coefs, tab, slabs, perts):
    bands, npw = coefs.shape
    return pl.pallas_call(
        dense_kernel,
        out_shape=(
            shape((N2, N1, 2 * LANES), BF16),
            shape((N1, N2, 2 * LANES), BF16),
            shape((2, 4, bands, npw // QUARTERS), BF16),
            shape((perts,) + share.shape, F32),
            shape((16, LANES), F32),
        ),
        in_specs=[VMEM] * 6,
        out_specs=(VMEM,) * 5,
        scratch_shapes=[
            pltpu.VMEM((slabs,) + pot.shape, BF16),
        ]
        + sems(2)
        + sems(7)
        + sems(perts - 1),
        compiler_params=params(4),
        cost_estimate=cost(2e10, 8e6),
        name="dense",
    )(turned, pot, far, share, coefs, tab)


def gather_of(starts, data, back, tab, npw):
    slabs = data.shape[0]
    return pl.pallas_call(
        gather_kernel,
        out_shape=shape((slabs, QUARTERS, 2, npw // QUARTERS), BF16),
        in_specs=[SMEM] + [VMEM] * 3,
        out_specs=VMEM,
        scratch_shapes=[pltpu.VMEM((slabs, 2, data.shape[2]), F32)],
        compiler_params=params(),
        cost_estimate=cost(2e10, 8e6),
        name="gather",
    )(starts, data, back, tab)


def middle_of(waves, bands, index, energies):
    slabs, quarters, two, part = waves.shape
    peers = slabs * quarters - 1
    small = (slabs * quarters * two // 2, LANES)
    longer = pltpu.VMEM((slabs, quarters, two, part + LANES), BF16)
    return pl.pallas_call(
        middle_kernel,
        out_shape=(shape(index.shape, F32), shape((8, LANES), F32)),
        in_specs=[VMEM] * 3 + [SMEM],
        out_specs=(VMEM, VMEM),
        scratch_shapes=[
            pltpu.VMEM(waves.shape, BF16),
            pltpu.VMEM((peers,) + small, BF16),
            longer,
            longer,
            pltpu.VMEM(small, BF16),
        ]
        + sems(3, peers),
        compiler_params=params(2),
        name="middle",
    )(waves, bands, index, energies)


def end_of(turned, psi, step, pots, gram, tab, slabs):
    _, planes, width = pots.shape
    tile = (planes, LANES)
    return pl.pallas_call(
        end_kernel,
        out_shape=(shape((planes, width), F32), shape((8, LANES), F32)),
        in_specs=[VMEM] * 6,
        out_specs=(VMEM, VMEM),
        scratch_shapes=[
            pltpu.VMEM((slabs, 8 * PARTS) + tile, BF16),
            pltpu.VMEM((2, 2, 4 * PARTS) + tile, BF16),
            pltpu.VMEM((2, 2, 4, PART_A) + tile, BF16),
            pltpu.VMEM((2, 4, 2, PART_B) + tile, BF16),
            pltpu.VMEM((3, 4, PART_A) + tile, BF16),
            pltpu.VMEM((2, 3, 2, PART_B) + tile, BF16),
            pltpu.VMEM((4, PART_A) + tile, BF16),
            pltpu.VMEM((2, 2, PART_B) + tile, BF16),
            pltpu.VMEM((3, PART_A) + tile, BF16),
            pltpu.VMEM((3, PART_B) + tile, BF16),
            pltpu.VMEM((3, 16, LANES), F32),
            pltpu.VMEM((10, 16, LANES), F32),
        ]
        + sems(2, 2)
        + sems(3)
        + sems(2, 3)
        + sems(3)
        + sems(3)
        + sems(10),
        compiler_params=params(3),
        name="density",
    )(turned, psi, step, pots, gram, tab)


def next_chip():
    pairs = []
    for band in range(8):
        for slab in range(4):
            core = slab % 2
            to = (band // 4 * 2 + slab // 2 + 2 * core - 1) % 4
            pairs.append((band * 4 + slab, (to // 2 * 4 + band % 4) * 4 + to % 2 * 2 + core))
    return pairs


def per_device(wave_coeffs, band_energies, trial_potentials, wave_map):
    slabs = lax.axis_size("slab")
    npw = wave_coeffs.shape[1]
    planes, cross = trial_potentials.shape[1:]
    tab = cosines(N1)
    pot = trial_potentials.reshape(planes, cross)
    data, starts, narrow, share = start_of(wave_coeffs, wave_map, pot, slabs)
    far = lax.ppermute(narrow, ("band", "slab"), next_chip())
    turned = zy_of(starts, data, tab)
    perts = lax.axis_size("pert")
    psi, back, all_bands, pots, gram = dense_of(turned, narrow, far, share, wave_coeffs, tab, slabs, perts)
    waves = gather_of(starts, data, back, tab, npw)
    data, step = middle_of(waves, all_bands, data, band_energies)
    turned = zy_of(starts, data, tab)
    residual, projected = end_of(turned, psi, step, pots, gram, tab, slabs)
    return (residual.reshape(1, planes, -1), projected[:perts, :1])


def solution(mesh):
    return jax.shard_map(
        per_device,
        mesh=mesh,
        in_specs=(P("band", "slab"), P("band"), P("pert", "slab", None), P("slab")),
        out_specs=(P("pert", "slab", "band"), P(None, "pert")),
        check_vma=False,
    )
```
